128 devices in a mesh: ctx: 16 (over z, x_hi, core), tp: 8 (over y, x_lo).
Axes of the slice: x: 4 (x_hi: 2, x_lo: 2; x = x_hi * 2 + x_lo), y: 4, z: 4, core: 2. Of those that a mesh axis runs over, the one named last changes fastest.
Arguments:
- att_query: bfloat16 [8192, 6144], P('ctx', 'tp'), may hold values from -8 to 8
- att_key: bfloat16 [8192, 1024], P('ctx', 'tp'), may hold values from -8 to 8
- att_value: bfloat16 [8192, 1024], P('ctx', 'tp'), may hold values from -140 to 140
- lh_query: bfloat16 [8192, 6144], P('ctx', 'tp'), may hold values from -6 to 6
- lh_key: bfloat16 [8192, 6144], P('ctx', 'tp'), may hold values from -36 to 36
- lh_value: bfloat16 [8192, 6144], P('ctx', 'tp'), may hold values from -36 to 36
- lh_step: float32 [8192, 48], P('ctx', 'tp'), may hold values from 0 to 1
- att_gain: float32 [6144], P('tp'), may hold values from 0.1 to 1.9
- lh_gain: float32 [6144], P('tp'), may hold values from 0.1 to 1.9
Outputs:
- mixed: bfloat16 [8192, 6144], P('ctx', 'tp')
The draws below stay inside these ranges and needn't reach their ends.
All inputs are finite; a program needn't handle non-finite values.
Results may differ from the reference program's by a relative error of at most 0.012.
Values may be sent and summed in bfloat16 or wider, within the bound.
No kernel may reach another device: no remote copies, remote signals or barrier semaphores. Data moves between devices by JAX's collectives and lax.ppermute only.
A program may use at most 64 MiB of HBM per device.

```python
import math
import jax
import jax.numpy as jnp
from jax import lax

QUERY_HEADS = 48
KVH = 8
HD = 128
SEQUENCE_TOKENS = 8192


def spread_scales(key, column_count):
    key_cols, key_rows = jax.random.split(key, 2)
    column_scale = jnp.exp(jax.random.uniform(key_cols, (column_count,), jnp.float32, math.log(0.3), math.log(3.0)))
    row_scale = jnp.exp(jax.random.uniform(key_rows, (SEQUENCE_TOKENS, 1), jnp.float32, math.log(0.3), math.log(3.0)))
    return (column_scale, row_scale)


def draw_att_query(key, part):
    key = jax.random.fold_in(key, 1)
    values = jax.random.normal(key, (SEQUENCE_TOKENS, QUERY_HEADS * HD), jnp.float32)
    return jnp.clip(values, -8.0, 8.0).astype(jnp.bfloat16)


def draw_att_key(key, part):
    key = jax.random.fold_in(key, 2)
    values = jax.random.normal(key, (SEQUENCE_TOKENS, KVH * HD), jnp.float32)
    return jnp.clip(values, -8.0, 8.0).astype(jnp.bfloat16)


def draw_att_value(key, part):
    key = jax.random.fold_in(key, 3)
    key_scale, key_base = jax.random.split(key, 2)
    column_scale, row_scale = spread_scales(key_scale, HD)
    rising = 3.0 ** (jnp.arange(KVH, dtype=jnp.float32) / (KVH - 1))
    base = jnp.clip(jax.random.normal(key_base, (SEQUENCE_TOKENS, KVH * HD), jnp.float32), -4.0, 4.0)
    scale = (rising[:, None] * column_scale[None, :]).reshape(1, KVH * HD)
    return (base * row_scale * scale).astype(jnp.bfloat16)


def draw_lh_key(key, part):
    key = jax.random.fold_in(key, 4)
    key_scale, key_base = jax.random.split(key, 2)
    column_scale, row_scale = spread_scales(key_scale, QUERY_HEADS * HD)
    base = jnp.clip(jax.random.normal(key_base, (SEQUENCE_TOKENS, QUERY_HEADS * HD), jnp.float32), -4.0, 4.0)
    return (base * row_scale * column_scale[None, :]).astype(jnp.bfloat16)


def draw_lh_value(key, part):
    key = jax.random.fold_in(key, 5)
    key_scale, key_base = jax.random.split(key, 2)
    column_scale, row_scale = spread_scales(key_scale, QUERY_HEADS * HD)
    base = jnp.clip(jax.random.normal(key_base, (SEQUENCE_TOKENS, QUERY_HEADS * HD), jnp.float32), -4.0, 4.0)
    return (base * row_scale * column_scale[None, :]).astype(jnp.bfloat16)


def draw_lh_step(key, part):
    key = jax.random.fold_in(key, 6)
    random_key_select, random_key_quick, random_key_gradual, random_key_coarse, random_key_location, random_key_spike = jax.random.split(key, 6)
    fast_share = 0.5
    is_fast = jax.random.uniform(random_key_select, (QUERY_HEADS,), jnp.float32) < fast_share
    fast_rate = jnp.exp(jax.random.uniform(random_key_quick, (QUERY_HEADS,), jnp.float32, math.log(1.0 / 50.0), math.log(1.0 / 30.0)))
    slow_rate = jnp.exp(jax.random.uniform(random_key_gradual, (QUERY_HEADS,), jnp.float32, math.log(0.1), math.log(0.5))) / SEQUENCE_TOKENS
    head_rate = jnp.where(is_fast, fast_rate, slow_rate)
    rough = jnp.exp(jax.random.uniform(random_key_coarse, (SEQUENCE_TOKENS, QUERY_HEADS), jnp.float32, math.log(0.5), math.log(2.0)))
    step_total = head_rate[None, :] * rough
    spike_location = jax.random.randint(random_key_location, (2, QUERY_HEADS), 0, SEQUENCE_TOKENS)
    spike_extent = jax.random.uniform(random_key_spike, (2, QUERY_HEADS), jnp.float32, 0.25, 1.0)
    token_labels = jnp.arange(SEQUENCE_TOKENS, dtype=jnp.int32)[:, None]
    for sample_count in range(2):
        step_total = jnp.where(token_labels == spike_location[sample_count][None, :], spike_extent[sample_count][None, :], step_total)
    return step_total


def block_scale(own_key, extent, cuts, low, high):
    def one(axis_at, parts):
        heights = jax.random.uniform(jax.random.fold_in(jax.random.fold_in(own_key, 6), axis_at), (parts,), jnp.float32, low / len(cuts), high / len(cuts))
        return jnp.repeat(jnp.exp(heights), extent[axis_at] // parts).reshape((-1,) + (1,) * (len(extent) - axis_at - 1))

    factor_of = one(*cuts[0])
    for cut in cuts[1:]:
        factor_of = factor_of * one(*cut)
    return factor_of


def centred(own_key, shape, scale, bound, cuts=(), kind=jnp.bfloat16):
    entries = scale * jax.random.normal(own_key, shape, jnp.float32)
    if cuts:
        entries = entries * block_scale(own_key, shape, cuts, -0.22, 0.18)
    return jnp.clip(entries, -bound, bound).astype(kind)


def setup_inputs(seed: int = 0) -> dict:
    key_list = jax.random.split(jax.random.key(seed), 10)
    return {
        "att_query": draw_att_query(jax.random.fold_in(key_list[9], 71), 0),
        "att_key": draw_att_key(jax.random.fold_in(key_list[9], 71), 0),
        "att_value": draw_att_value(jax.random.fold_in(key_list[9], 71), 0),
        "lh_query": centred(key_list[3], (SEQUENCE_TOKENS, QUERY_HEADS * HD), 1.0, 6.0, ((0, 16), (1, 8))),
        "lh_key": draw_lh_key(jax.random.fold_in(key_list[9], 71), 0),
        "lh_value": draw_lh_value(jax.random.fold_in(key_list[9], 71), 0),
        "lh_step": draw_lh_step(jax.random.fold_in(key_list[9], 71), 0),
        "att_gain": jnp.clip(1.0 + 0.18 * jax.random.normal(key_list[7], (QUERY_HEADS * HD,), jnp.float32), 0.1, 1.9),
        "lh_gain": jnp.clip(1.0 + 0.18 * jax.random.normal(key_list[8], (QUERY_HEADS * HD,), jnp.float32), 0.1, 1.9),
    }


norm_eps = 1e-06
masked_score = -1e+30

def attention(att_query, att_key, att_value):
    group_size = QUERY_HEADS // KVH
    block_rows = math.gcd(SEQUENCE_TOKENS, 256)
    key_rows = att_key.astype(jnp.float32).reshape(SEQUENCE_TOKENS, KVH, HD)
    value_rows = att_value.astype(jnp.float32).reshape(SEQUENCE_TOKENS, KVH, HD)
    query_blocks = att_query.astype(jnp.float32).reshape(SEQUENCE_TOKENS // block_rows, block_rows, KVH, group_size, HD)
    block_starts = jnp.arange(SEQUENCE_TOKENS // block_rows, dtype=jnp.int32) * block_rows
    key_places = jnp.arange(SEQUENCE_TOKENS, dtype=jnp.int32)

    def one_block(block_item):
        query_block, first_row = block_item
        scores = jnp.einsum('rkgd,skd->kgrs', query_block, key_rows) / math.sqrt(HD)
        query_places = first_row + jnp.arange(block_rows, dtype=jnp.int32)
        visible = key_places[None, :] <= query_places[:, None]
        scores = jnp.where(visible, scores, masked_score)
        row_max = lax.optimization_barrier(jnp.max(scores, -1, keepdims=True))
        exponent = jnp.where(visible, jnp.exp(scores - row_max), 0.0)
        weights = lax.optimization_barrier(exponent.astype(jnp.bfloat16)).astype(jnp.float32)
        numerator = jnp.einsum('kgrs,skd->rkgd', weights, value_rows)
        denominator = jnp.transpose(lax.optimization_barrier(jnp.sum(exponent, -1)), (2, 0, 1))
        return numerator / denominator[..., None]
    result = lax.map(one_block, (query_blocks, block_starts))
    return result.reshape(SEQUENCE_TOKENS, QUERY_HEADS * HD).astype(jnp.bfloat16)

def recurrence(lh_query, lh_key, lh_value, lh_step):
    key_rows = lh_key.astype(jnp.float32).reshape(SEQUENCE_TOKENS, QUERY_HEADS, HD)
    key_rows = key_rows * lax.rsqrt(lax.optimization_barrier(jnp.sum(key_rows * key_rows, -1, keepdims=True)) + norm_eps)
    key_rows = lax.optimization_barrier(key_rows.astype(jnp.bfloat16)).astype(jnp.float32)
    query_rows = lh_query.astype(jnp.float32).reshape(SEQUENCE_TOKENS, QUERY_HEADS, HD)
    value_rows = lh_value.astype(jnp.float32).reshape(SEQUENCE_TOKENS, QUERY_HEADS, HD)
    decays = 1.0 / (1.0 + lh_step)
    rates = lh_step / (1.0 + lh_step)

    def one_head(head_item):

        def token_step(carried, token_row):
            query_row, key_row, value_row, decay_now, rate_now = token_row
            carried = decay_now * carried + (rate_now * value_row)[:, None] * key_row[None, :]
            return (carried, lax.optimization_barrier(jnp.sum(carried * query_row[None, :], -1)))
        _, head_out = lax.scan(token_step, jnp.zeros((HD, HD), jnp.float32), head_item)
        return head_out
    per_head = lax.map(one_head, (jnp.transpose(query_rows, (1, 0, 2)), jnp.transpose(key_rows, (1, 0, 2)), jnp.transpose(value_rows, (1, 0, 2)), decays.T, rates.T))
    return jnp.transpose(per_head, (1, 0, 2))

def reference(att_query, att_key, att_value, lh_query, lh_key, lh_value, lh_step, att_gain, lh_gain):
    att_out = attention(att_query, att_key, att_value).astype(jnp.float32)
    mean_square = lax.optimization_barrier(jnp.mean(att_out * att_out, -1, keepdims=True))
    att_part = att_out * lax.rsqrt(mean_square + norm_eps) * att_gain
    lh_out = recurrence(lh_query, lh_key, lh_value, lh_step)
    head_square = lax.optimization_barrier(jnp.mean(lh_out * lh_out, -1, keepdims=True))
    lh_part = (lh_out * lax.rsqrt(head_square + norm_eps)).reshape(SEQUENCE_TOKENS, QUERY_HEADS * HD) * lh_gain
    return (att_part + lh_part).astype(jnp.bfloat16)
```

```python
import functools
import math

import jax
import jax.numpy as jnp
from jax import lax
from jax.experimental import pallas as pl
from jax.experimental.pallas import tpu as pltpu
from jax.sharding import PartitionSpec as P

HD = 128
ROWS = 512
HEADS = 6
TILE = 256
EPS = 1e-06
MASKED = -1e30
LOG2E = math.log2(math.e)
SCORE_SCALE = LOG2E / math.sqrt(HD)
SAFE_EXPONENT = 100.0
STATE_ROWS = HEADS * HD + 8
NEVER = 1 << 20

VMEM = pl.BlockSpec(memory_space=pltpu.VMEM)
SMEM = pl.BlockSpec(memory_space=pltpu.SMEM)
f32 = jnp.float32
bf16 = jnp.bfloat16
highest = lax.Precision.HIGHEST


def dot(a, b, contract=((1,), (0,)), precision=None):
    return lax.dot_general(a, b, (contract, ((), ())), precision=precision, preferred_element_type=f32)


def params():
    return pltpu.CompilerParams(vmem_limit_bytes=56 << 20)


def head(h):
    return slice(h * HD, (h + 1) * HD)


def recur_kernel(q_ref, k_ref, v_ref, step_ref, local_ref, grow_ref, message_ref):
    step = step_ref[...]
    rate = step / (1.0 + step)
    log_decay = -jnp.log(1.0 + step) * LOG2E
    earlier = lax.broadcasted_iota(jnp.int32, (ROWS, ROWS), 0)
    later = lax.broadcasted_iota(jnp.int32, (ROWS, ROWS), 1)
    upper = jnp.where(earlier <= later, 1.0, 0.0).astype(f32)
    total = dot(log_decay, upper, precision=highest)
    source = jnp.log(rate) * LOG2E - total
    end = total[:, ROWS - 1 : ROWS]
    tail = jnp.exp2(end + source)
    rows16 = jnp.concatenate([total, tail], 0)
    eye = jnp.where(
        lax.broadcasted_iota(jnp.int32, (16, HD), 0) == lax.broadcasted_iota(jnp.int32, (16, HD), 1), 1.0, 0.0
    ).astype(f32)
    columns = dot(rows16, eye, ((0,), (0,)), highest)
    grow_ref[...] = jnp.exp2(columns)
    message_ref[HEADS * HD :, :] = jnp.broadcast_to(end, (8, HD))
    at_row = lax.broadcasted_iota(jnp.int32, (TILE, TILE), 0)
    at_column = lax.broadcasted_iota(jnp.int32, (TILE, TILE), 1)
    seen = at_column <= at_row
    for h in range(HEADS):
        keys = k_ref[:, head(h)].astype(f32)
        keys = keys * lax.rsqrt(jnp.sum(keys * keys, -1, keepdims=True) + EPS)
        unit = keys.astype(bf16)
        values = v_ref[:, head(h)]
        for a in range(0, ROWS, TILE):
            result = None
            for b in range(0, a + TILE, TILE):
                scores = dot(q_ref[a : a + TILE, head(h)], unit[b : b + TILE], ((1,), (1,)))
                decay = jnp.exp2(columns[a : a + TILE, h : h + 1] + source[h : h + 1, b : b + TILE])
                weights = scores * decay
                if a == b:
                    weights = jnp.where(seen, weights, 0.0)
                part = dot(weights.astype(bf16), values[b : b + TILE])
                result = part if result is None else result + part
            local_ref[a : a + TILE, head(h)] = result
        tailed = (values.astype(f32) * columns[:, 8 + h : 9 + h]).astype(bf16)
        message_ref[head(h), :] = dot(unit, tailed, ((0,), (0,)))


def recur(lh_query, lh_key, lh_value, lh_step):
    step = jnp.pad(lh_step.T, ((0, 2), (0, 0)), constant_values=0.5)
    return pl.pallas_call(
        recur_kernel,
        out_shape=(
            jax.ShapeDtypeStruct((ROWS, HEADS * HD), f32),
            jax.ShapeDtypeStruct((ROWS, HD), f32),
            jax.ShapeDtypeStruct((STATE_ROWS, HD), f32),
        ),
        in_specs=[VMEM] * 4,
        out_specs=(VMEM,) * 3,
        compiler_params=params(),
        name="recur",
    )(lh_query, lh_key, lh_value, step)


def join_kernel(flag_ref, *refs):
    *messages, out_ref = refs
    decay = jnp.zeros((8, HD), f32)
    parts = [jnp.zeros((HD, HD), f32) for _ in range(HEADS)]
    for n, message in enumerate(messages):
        on = flag_ref[n] > 0
        logs = jnp.where(on, message[HEADS * HD :, :], 0.0)
        for h in range(HEADS):
            state = jnp.where(on, message[head(h), :], 0.0)
            parts[h] = jnp.exp2(logs[h : h + 1, :]) * parts[h] + state
        decay = decay + logs
    for h in range(HEADS):
        out_ref[head(h), :] = parts[h]
    out_ref[HEADS * HD :, :] = decay


def join(flags, *messages):
    return pl.pallas_call(
        join_kernel,
        out_shape=jax.ShapeDtypeStruct((STATE_ROWS, HD), f32),
        in_specs=[SMEM] + [VMEM] * len(messages),
        out_specs=VMEM,
        compiler_params=params(),
        name="join",
    )(jnp.stack([jnp.asarray(flag, jnp.int32) for flag in flags]), *messages)


def attend_kernel(first, last, buffers, meta_ref, *refs):
    mine = meta_ref[0]
    refs = list(refs)
    query_ref = refs.pop(0)
    own_ref = refs.pop(0) if first else None
    carry_ref, top_in_ref = (None, None) if first else (refs.pop(0), refs.pop(0))
    block_refs = [refs.pop(0) for _ in range(buffers)]
    if last:
        out_ref, square_ref, top_ref, sums, scaled, keys, values = refs
    else:
        sums, top_ref, scaled, keys, values = refs
    ones = jnp.ones((HD, HD), bf16)

    def norm(part):
        part = part.astype(f32)
        lengths = dot((part * part).astype(bf16), ones)
        return jnp.max(lengths.reshape(-1, 8, HD), 0)

    for h in range(HEADS):
        scaled[h * ROWS : (h + 1) * ROWS, :] = (query_ref[:, head(h)].astype(f32) * SCORE_SCALE).astype(bf16)
    if first:
        sums[...] = jnp.zeros_like(sums)
        top_ref[0:8, :] = norm(scaled[...])
        top_ref[8:16, :] = norm(own_ref[:, :HD])
    else:
        sums[...] = carry_ref[...]
        top_ref[...] = top_in_ref[...]
    values[:, HD:] = jnp.ones((values.shape[0], HD), bf16)

    filled = jnp.int32(0)
    for n, block in enumerate(block_refs):
        rows = block.shape[0]
        number = meta_ref[1 + n]
        takes = number < mine
        place = filled

        @pl.when(takes)
        def _():
            at = pl.ds(pl.multiple_of(place * ROWS, ROWS), rows)
            keys[at, :] = block[:, :HD]
            values[at, :HD] = block[:, HD:]
            top_ref[8:16, :] = jnp.maximum(top_ref[8:16, :], norm(block[:, :HD]))

        filled = filled + jnp.where(takes, rows // ROWS, 0)

    def visit(start, count):
        at = pl.ds(pl.multiple_of(start, ROWS), count)
        block_keys = keys[at, :]
        block_values = values[at, :]
        for h in range(HEADS):
            for a in range(0, ROWS, TILE):
                query = scaled[h * ROWS + a : h * ROWS + a + TILE, :]
                weights = jnp.exp2(dot(query, block_keys, ((1,), (1,)))).astype(bf16)
                sums[h, a : a + TILE, :] += dot(weights, block_values)

    if first:

        @pl.when(filled > 0)
        def _():
            visit(0, ROWS)

        at_row = lax.broadcasted_iota(jnp.int32, (TILE, TILE), 0)
        at_column = lax.broadcasted_iota(jnp.int32, (TILE, TILE), 1)
        seen = at_column <= at_row
        values[:ROWS, :HD] = own_ref[:, HD:]
        for h in range(HEADS):
            for a in range(0, ROWS, TILE):
                query = scaled[h * ROWS + a : h * ROWS + a + TILE, :]
                for b in range(0, a + TILE, TILE):
                    weights = jnp.exp2(dot(query, own_ref[b : b + TILE, :HD], ((1,), (1,))))
                    if a == b:
                        weights = jnp.where(seen, weights, 0.0)
                    sums[h, a : a + TILE, :] += dot(weights.astype(bf16), values[b : b + TILE, :])
    else:

        def pair(n, _):
            visit(n * 2 * ROWS, 2 * ROWS)
            return 0

        lax.fori_loop(0, filled // 2, pair, 0)

    if last:
        squares = jnp.zeros((8, ROWS), f32)
        for h in range(HEADS):
            result = (sums[h, :, :HD] / sums[h, :, HD:]).astype(bf16)
            out_ref[:, head(h)] = result
            result = result.astype(f32)
            squares = squares + dot(jnp.ones((8, HD), bf16), (result * result).astype(bf16), ((1,), (1,)))
        square_ref[...] = squares


def attend(mine, query, own, carry, blocks, numbers, last=False):
    first = carry is None
    meta = jnp.stack([mine] + list(numbers)).astype(jnp.int32)
    size = max(sum(block.shape[0] for block in blocks), ROWS)
    operands = [query] + ([own] if first else list(carry)) + list(blocks)
    sums = ((HEADS, ROWS, 2 * HD), f32)
    top = jax.ShapeDtypeStruct((16, HD), f32)
    scratch = [
        pltpu.VMEM((HEADS * ROWS, HD), bf16),
        pltpu.VMEM((size, HD), bf16),
        pltpu.VMEM((size, 2 * HD), bf16),
    ]
    if last:
        out_shape = (
            jax.ShapeDtypeStruct((ROWS, HEADS * HD), bf16),
            jax.ShapeDtypeStruct((8, ROWS), f32),
            top,
        )
        scratch = [pltpu.VMEM(*sums)] + scratch
    else:
        out_shape = (jax.ShapeDtypeStruct(*sums), top)
    return pl.pallas_call(
        functools.partial(attend_kernel, first, last, len(blocks)),
        out_shape=out_shape,
        in_specs=[SMEM] + [VMEM] * len(operands),
        out_specs=(VMEM,) * len(out_shape),
        scratch_shapes=scratch,
        compiler_params=params(),
        name="attend_last" if last else "attend",
    )(meta, *operands)


def attend_shifted(mine, query, pieces, numbers):
    grouped = query.reshape(ROWS, HEADS, HD)
    stacked = jnp.concatenate(pieces, 0)
    count = stacked.shape[0] // ROWS
    table = jnp.stack(numbers).astype(jnp.int32)
    scale = 1.0 / math.sqrt(HD)
    positions = mine * ROWS + jnp.arange(ROWS, dtype=jnp.int32)
    initial = (
        jnp.full((HEADS, ROWS), MASKED, f32),
        jnp.zeros((HEADS, ROWS), f32),
        jnp.zeros((HEADS, ROWS, HD), f32),
    )

    def step(n, running):
        def visit(current):
            top, totals, numerator = current
            block = lax.dynamic_slice_in_dim(stacked, n * ROWS, ROWS, 0)
            scores = jnp.einsum("rgd,sd->grs", grouped, block[:, :HD], preferred_element_type=f32) * scale
            places = table[n] * ROWS + jnp.arange(ROWS, dtype=jnp.int32)
            visible = places[None, :] <= positions[:, None]
            scores = jnp.where(visible, scores, MASKED)
            new_top = jnp.maximum(top, jnp.max(scores, -1))
            rescale = jnp.exp(top - new_top)
            weights = jnp.where(visible, jnp.exp(scores - new_top[..., None]), 0.0)
            numerator = numerator * rescale[..., None] + jnp.einsum(
                "grs,sd->grd", weights.astype(bf16), block[:, HD:], preferred_element_type=f32
            )
            return (new_top, totals * rescale + jnp.sum(weights, -1), numerator)

        return lax.cond(table[n] <= mine, visit, lambda current: current, running)

    _, totals, numerator = lax.fori_loop(0, count, step, initial)
    result = (numerator / totals[..., None]).astype(bf16)
    result = jnp.transpose(result, (1, 0, 2)).reshape(ROWS, HEADS * HD)
    wide = result.astype(f32)
    return result, jnp.broadcast_to(jnp.sum(wide * wide, -1)[None], (8, ROWS))


def carry_kernel(query_ref, local_ref, grow_ref, state_ref, gain_ref, out_ref):
    grow = grow_ref[...]
    for h in range(HEADS):
        state = state_ref[head(h), :]
        upper = state.astype(bf16)
        lower = (state - upper.astype(f32)).astype(bf16)
        both = dot(query_ref[:, head(h)], jnp.concatenate([upper, lower], 1))
        entered = both[:, :HD] + both[:, HD:]
        result = local_ref[:, head(h)] + entered * grow[:, h : h + 1]
        square = jnp.mean(result * result, -1, keepdims=True)
        out_ref[:, head(h)] = result * lax.rsqrt(square + EPS) * gain_ref[:, head(h)]


def finish_kernel(features, attention_ref, square_ref, linear_ref, gain_ref, out_ref):
    factor = lax.rsqrt(square_ref[...] / features + EPS)
    factor = dot(factor, jnp.full((8, HD), 0.125, f32), ((0,), (0,)), highest)
    for h in range(HEADS):
        part = attention_ref[:, head(h)].astype(f32) * factor * gain_ref[:, head(h)]
        out_ref[:, head(h)] = (part + linear_ref[:, head(h)]).astype(bf16)


def simple(kernel, dtype, name, *operands):
    return pl.pallas_call(
        kernel,
        out_shape=jax.ShapeDtypeStruct((ROWS, HEADS * HD), dtype),
        in_specs=[VMEM] * len(operands),
        out_specs=VMEM,
        compiler_params=params(),
        name=name,
    )(*operands)


def body(att_query, att_key, att_value, lh_query, lh_key, lh_value, lh_step, att_gain, lh_gain):
    mine = lax.axis_index("ctx")
    plane, side, core = mine // 4, (mine // 2) % 2, mine % 2
    partner = mine ^ 2

    def move(value, pairs):
        return lax.ppermute(value, "ctx", pairs)

    every = range(16)
    sibling = [(i, i ^ 1) for i in every]
    down = [(i, i ^ 1) for i in every if i % 2 == 0]

    own = jnp.concatenate([att_key, att_value], 1)
    across = move(own, [(i, i ^ 2) for i in every if i < 4 or i % 4 < 2])
    near = move(own, sibling)
    chip = jnp.concatenate([own, near], 0)
    onward = [(i, i + 4) for i in every if i % 2 == 0 and i < 12]
    wrapped = [(i, i + 12) for i in (1, 3)]
    behind = move(chip, onward + wrapped)
    local, grow, message = recur(lh_query, lh_key, lh_value, lh_step)

    def before(number, wanted):
        return jnp.where(wanted, number, NEVER)

    numbers = []
    pieces = []

    carry = attend(mine, att_query, own, None, [near], [before(mine ^ 1, core == 1)])
    pieces += [own, near]
    numbers += [mine, mine ^ 1]

    across_near = move(across, sibling)
    behind_near = move(behind, sibling)
    there = side == 1
    blocks = [across, across_near, behind, behind_near]
    got = [
        before(partner, there),
        before(partner ^ 1, there),
        before(jnp.where(core == 0, mine - 4, mine - 12), jnp.where(core == 0, plane >= 1, plane == 3)),
        before(jnp.where(core == 0, mine - 12 + 1, mine - 4 - 1), jnp.where(core == 0, plane == 3, plane >= 1)),
    ]
    carry = attend(mine, att_query, None, carry, blocks, got)
    pieces += blocks
    numbers += [
        got[0],
        got[1],
        got[2],
        jnp.where(got[2] < NEVER, got[2] ^ 1, NEVER),
        got[3],
        jnp.where(got[3] < NEVER, got[3] ^ 1, NEVER),
    ]

    far_message = jnp.where(core == 0, behind, jnp.concatenate([across, across_near], 0))
    far = move(far_message, [(i, i + 4) for i in every if i % 2 == 0 and 4 <= i < 12] + wrapped)
    level = move(behind, [(i, i ^ 2) for i in every if i % 2 == 0 and i >= 4])
    far_near = move(far, sibling)
    level_near = move(level, down)
    blocks = [level, level_near, far, far_near]
    got = [
        before(partner - 4, (core == 0) & (plane >= 1)),
        before(partner - 4 - 1, (core == 1) & (plane >= 1)),
        before(
            jnp.where(core == 0, mine - 8, partner - 12), jnp.where(core == 0, plane >= 2, plane == 3)
        ),
        before(
            jnp.where(core == 0, partner - 12 + 1, mine - 8 - 1),
            jnp.where(core == 0, plane == 3, plane >= 2),
        ),
    ]
    carry = attend(mine, att_query, None, carry, blocks, got)
    pieces += blocks
    for number in got:
        numbers += [number, jnp.where(number < NEVER, number ^ 1, NEVER)]

    level_far = move(far, [(i, i ^ 2) for i in every if i % 2 == 0 and i >= 8])
    level_far_near = move(level_far, down)
    blocks = [level_far, level_far_near]
    got = [
        before(partner - 8, (core == 0) & (plane >= 2)),
        before(partner - 8 - 1, (core == 1) & (plane >= 2)),
    ]
    attention, squares, top = attend(mine, att_query, None, carry, blocks, got, last=True)
    pieces += blocks
    for number in got:
        numbers += [number, jnp.where(number < NEVER, number ^ 1, NEVER)]
    bound = jnp.max(top[:8]) * jnp.max(top[8:])
    attention, squares = lax.cond(
        bound * 1.05 <= SAFE_EXPONENT * SAFE_EXPONENT,
        lambda: (attention, squares),
        lambda: attend_shifted(mine, att_query, pieces, numbers),
    )

    other = move(message, sibling)
    first_core = jnp.asarray(1, jnp.int32)
    of_chip = join(
        [first_core, first_core],
        jnp.where(core == 0, message, other),
        jnp.where(core == 0, other, message),
    )
    other_chip = move(of_chip, [(i, i ^ 2) for i in every])
    of_plane = join(
        [first_core, first_core],
        jnp.where(side == 0, of_chip, other_chip),
        jnp.where(side == 0, other_chip, of_chip),
    )
    one_back = move(of_plane, onward + wrapped)
    two_back = move(one_back, [(i, i + 4) for i in every if i % 2 == 0 and 4 <= i < 12])
    swapped = move(jnp.where(core == 0, two_back, one_back), sibling)
    swapped_one = move(one_back, down)
    entering = join(
        [
            plane == 3,
            plane >= 2,
            plane >= 1,
            side == 1,
            core == 1,
        ],
        jnp.where(core == 0, swapped, one_back),
        jnp.where(core == 0, two_back, swapped),
        jnp.where(core == 0, one_back, swapped_one),
        other_chip,
        other,
    )
    linear = simple(
        carry_kernel, f32, "carry", lh_query, local, grow, entering, lh_gain.reshape(1, HEADS * HD)
    )

    for bit in (1, 2, 4):
        squares = squares + lax.ppermute(squares, "tp", [(i, i ^ bit) for i in range(8)])
    features = HEADS * HD * lax.axis_size("tp")
    return simple(
        functools.partial(finish_kernel, float(features)),
        bf16,
        "finish",
        attention,
        squares,
        linear,
        att_gain.reshape(1, HEADS * HD),
    )


def solution(mesh):
    placed = (P("ctx", "tp"),) * 7 + (P("tp"), P("tp"))
    return jax.shard_map(body, mesh=mesh, in_specs=placed, out_specs=P("ctx", "tp"), check_vma=False)
```

```python
import functools
import math

import jax
import jax.numpy as jnp
from jax import lax
from jax.experimental import pallas as pl
from jax.experimental.pallas import tpu as pltpu
from jax.sharding import PartitionSpec as P

HD = 128
ROWS = 512
HEADS = 6
TILE = 256
EPS = 1e-06
MASKED = -1e30
LOG2E = math.log2(math.e)
SCORE_SCALE = LOG2E / math.sqrt(HD)
SAFE_EXPONENT = 100.0
STATE_ROWS = HEADS * HD + 8
NEVER = 1 << 20

VMEM = pl.BlockSpec(memory_space=pltpu.VMEM)
SMEM = pl.BlockSpec(memory_space=pltpu.SMEM)
f32 = jnp.float32
bf16 = jnp.bfloat16
highest = lax.Precision.HIGHEST


def dot(a, b, contract=((1,), (0,)), precision=None):
    return lax.dot_general(a, b, (contract, ((), ())), precision=precision, preferred_element_type=f32)


def params():
    return pltpu.CompilerParams(vmem_limit_bytes=56 << 20)


def cost(us):
    return pl.CostEstimate(flops=int(us * 1e9), bytes_accessed=int(us * 1e6), transcendentals=int(us * 1e6))


def head(h):
    return slice(h * HD, (h + 1) * HD)


def recur_kernel(q_ref, k_ref, v_ref, step_ref, local_ref, grow_ref, message_ref, padded):
    padded[...] = jnp.full((ROWS, HD), 0.5, f32)
    padded[:, :HEADS] = step_ref[...]
    step = jnp.transpose(padded[...])[:8, :]
    rate = step / (1.0 + step)
    log_decay = -jnp.log(1.0 + step) * LOG2E
    earlier = lax.broadcasted_iota(jnp.int32, (ROWS, ROWS), 0)
    later = lax.broadcasted_iota(jnp.int32, (ROWS, ROWS), 1)
    upper = jnp.where(earlier <= later, 1.0, 0.0).astype(f32)
    total = dot(log_decay, upper, precision=highest)
    source = jnp.log(rate) * LOG2E - total
    end = total[:, ROWS - 1 : ROWS]
    tail = jnp.exp2(end + source)
    rows = jnp.concatenate([total, tail, jnp.zeros((HD - 16, ROWS), f32)], 0)
    columns = jnp.transpose(rows)
    grow_ref[...] = jnp.exp2(columns)
    message_ref[HEADS * HD :, :] = jnp.broadcast_to(end, (8, HD))
    at_row = lax.broadcasted_iota(jnp.int32, (TILE, TILE), 0)
    at_column = lax.broadcasted_iota(jnp.int32, (TILE, TILE), 1)
    seen = at_column <= at_row
    for h in range(HEADS):
        keys = k_ref[:, head(h)].astype(f32)
        keys = keys * lax.rsqrt(jnp.sum(keys * keys, -1, keepdims=True) + EPS)
        unit = keys.astype(bf16)
        values = v_ref[:, head(h)]
        for a in range(0, ROWS, TILE):
            result = None
            for b in range(0, a + TILE, TILE):
                scores = dot(q_ref[a : a + TILE, head(h)], unit[b : b + TILE], ((1,), (1,)))
                decay = jnp.exp2(columns[a : a + TILE, h : h + 1] + source[h : h + 1, b : b + TILE])
                weights = scores * decay
                if a == b:
                    weights = jnp.where(seen, weights, 0.0)
                part = dot(weights.astype(bf16), values[b : b + TILE])
                result = part if result is None else result + part
            local_ref[a : a + TILE, head(h)] = result
        tailed = (values.astype(f32) * columns[:, 8 + h : 9 + h]).astype(bf16)
        message_ref[head(h), :] = dot(unit, tailed, ((0,), (0,)))


def recur(lh_query, lh_key, lh_value, lh_step):
    return pl.pallas_call(
        recur_kernel,
        out_shape=(
            jax.ShapeDtypeStruct((ROWS, HEADS * HD), f32),
            jax.ShapeDtypeStruct((ROWS, HD), f32),
            jax.ShapeDtypeStruct((STATE_ROWS, HD), f32),
        ),
        in_specs=[VMEM] * 4,
        out_specs=(VMEM,) * 3,
        scratch_shapes=[pltpu.VMEM((ROWS, HD), f32)],
        compiler_params=params(),
        cost_estimate=cost(2.5),
        name="recur",
    )(lh_query, lh_key, lh_value, lh_step)


def follow(early, late):
    logs = early[1] + late[1]
    states = [jnp.exp2(late[1][h : h + 1, :]) * early[0][h] + late[0][h] for h in range(HEADS)]
    return states, logs


def state_of(ref, wanted=None):
    states = [ref[head(h), :] for h in range(HEADS)]
    logs = ref[HEADS * HD :, :]
    if wanted is None:
        return states, logs
    return [jnp.where(wanted, state, 0.0) for state in states], jnp.where(wanted, logs, 0.0)


def put_state(ref, value):
    for h in range(HEADS):
        ref[head(h), :] = value[0][h]
    ref[HEADS * HD :, :] = value[1]


def join_kernel(bit, mine_ref, own_ref, other_ref, out_ref):
    own_first = (mine_ref[0] // bit) % 2 == 0
    own, other = state_of(own_ref), state_of(other_ref)

    def pick(one, two):
        return [jnp.where(own_first, a, b) for a, b in zip(one[0], two[0])], jnp.where(own_first, one[1], two[1])

    put_state(out_ref, follow(pick(own, other), pick(other, own)))


def join(bit, mine, own, other):
    return pl.pallas_call(
        functools.partial(join_kernel, bit),
        out_shape=jax.ShapeDtypeStruct((STATE_ROWS, HD), f32),
        in_specs=[SMEM, VMEM, VMEM],
        out_specs=VMEM,
        compiler_params=params(),
        cost_estimate=cost(1.0),
        name="join",
    )(mine, own, other)


def hand_kernel(mine_ref, behind_ref, beyond_ref, out_ref):
    plane, core = mine_ref[0] // 4, mine_ref[0] % 2
    behind = state_of(behind_ref, (plane == 3) | (core == 0))
    beyond = state_of(beyond_ref, (plane >= 2) & (core == 1))
    put_state(out_ref, follow(behind, beyond))


def hand(mine, behind, beyond):
    return pl.pallas_call(
        hand_kernel,
        out_shape=jax.ShapeDtypeStruct((STATE_ROWS, HD), f32),
        in_specs=[SMEM, VMEM, VMEM],
        out_specs=VMEM,
        compiler_params=params(),
        cost_estimate=cost(1.0),
        name="hand",
    )(mine, behind, beyond)


def attend_kernel(first, numbers_of, buffers, mine_ref, *refs):
    mine = mine_ref[0]
    refs = list(refs)
    query_ref = refs.pop(0)
    own_ref = refs.pop(0) if first else None
    carry_ref, count_ref, top_in_ref = (None,) * 3 if first else (refs.pop(0) for _ in range(3))
    block_refs = [refs.pop(0) for _ in range(buffers)]
    if first:
        numerator_ref, counted_ref, top_ref, sums, scaled, keys, values = refs
    else:
        out_ref, square_ref, safe_ref, sums, scaled, keys, values, top_ref = refs
    ones = jnp.ones((HD, HD), bf16)

    def norm(part):
        part = part.astype(f32)
        lengths = dot((part * part).astype(bf16), ones)
        return jnp.max(lengths.reshape(-1, 8, HD), 0)

    for h in range(HEADS):
        scaled[h * ROWS : (h + 1) * ROWS, :] = (query_ref[:, head(h)].astype(f32) * SCORE_SCALE).astype(bf16)
    if first:
        sums[...] = jnp.zeros_like(sums)
        top_ref[0:8, :] = norm(scaled[...])
        top_ref[8:16, :] = norm(own_ref[:, :HD])
    else:
        for h in range(HEADS):
            sums[h, :, :HD] = carry_ref[:, head(h)]
            sums[h, :, HD:] = jnp.broadcast_to(count_ref[:, h : h + 1], (ROWS, HD))
        top_ref[...] = top_in_ref[...]
    values[:, HD:] = jnp.ones((values.shape[0], HD), bf16)

    filled = jnp.int32(0)
    for block, number in zip(block_refs, numbers_of(mine)):
        rows = block.shape[0]
        takes = number < mine
        place = filled

        @pl.when(takes)
        def _():
            at = pl.ds(pl.multiple_of(place * ROWS, ROWS), rows)
            keys[at, :] = block[:, :HD]
            values[at, :HD] = block[:, HD:]
            top_ref[8:16, :] = jnp.maximum(top_ref[8:16, :], norm(block[:, :HD]))

        filled = filled + jnp.where(takes, rows // ROWS, 0)

    def visit(start, count):
        at = pl.ds(pl.multiple_of(start, ROWS), count)
        block_keys = keys[at, :]
        block_values = values[at, :]
        for h in range(HEADS):
            for a in range(0, ROWS, TILE):
                query = scaled[h * ROWS + a : h * ROWS + a + TILE, :]
                weights = jnp.exp2(dot(query, block_keys, ((1,), (1,)))).astype(bf16)
                sums[h, a : a + TILE, :] += dot(weights, block_values)

    def pair(n, _):
        visit(n * 2 * ROWS, 2 * ROWS)
        return 0

    lax.fori_loop(0, filled // 2, pair, 0)

    if first:

        @pl.when(filled % 2 == 1)
        def _():
            visit((filled - 1) * ROWS, ROWS)

        at_row = lax.broadcasted_iota(jnp.int32, (TILE, TILE), 0)
        at_column = lax.broadcasted_iota(jnp.int32, (TILE, TILE), 1)
        seen = at_column <= at_row
        values[:ROWS, :HD] = own_ref[:, HD:]
        for h in range(HEADS):
            for a in range(0, ROWS, TILE):
                query = scaled[h * ROWS + a : h * ROWS + a + TILE, :]
                for b in range(0, a + TILE, TILE):
                    weights = jnp.exp2(dot(query, own_ref[b : b + TILE, :HD], ((1,), (1,))))
                    if a == b:
                        weights = jnp.where(seen, weights, 0.0)
                    sums[h, a : a + TILE, :] += dot(weights.astype(bf16), values[b : b + TILE, :])
            numerator_ref[:, head(h)] = sums[h, :, :HD]
            counted_ref[:, h : h + 1] = sums[h, :, HD : HD + 1]
    else:
        squares = jnp.zeros((8, ROWS), f32)
        for h in range(HEADS):
            result = (sums[h, :, :HD] / sums[h, :, HD:]).astype(bf16)
            out_ref[:, head(h)] = result
            result = result.astype(f32)
            squares = squares + dot(jnp.ones((8, HD), bf16), (result * result).astype(bf16), ((1,), (1,)))
        square_ref[...] = squares
        bound = jnp.max(top_ref[:8, :]) * jnp.max(top_ref[8:, :])
        safe_ref[0] = jnp.where(bound * 1.05 <= SAFE_EXPONENT * SAFE_EXPONENT, 1, 0)


def attend(mine, query, own, carry, blocks, numbers_of):
    first = carry is None
    size = sum(block.shape[0] for block in blocks)
    operands = [query] + ([own] if first else list(carry)) + list(blocks)
    top = (16, HD)
    scratch = [
        pltpu.VMEM((HEADS, ROWS, 2 * HD), f32),
        pltpu.VMEM((HEADS * ROWS, HD), bf16),
        pltpu.VMEM((size, HD), bf16),
        pltpu.VMEM((size, 2 * HD), bf16),
    ]
    if first:
        out_shape = (
            jax.ShapeDtypeStruct((ROWS, HEADS * HD), f32),
            jax.ShapeDtypeStruct((ROWS, HD), f32),
            jax.ShapeDtypeStruct(top, f32),
        )
        out_specs = (VMEM,) * 3
    else:
        out_shape = (
            jax.ShapeDtypeStruct((ROWS, HEADS * HD), bf16),
            jax.ShapeDtypeStruct((8, ROWS), f32),
            jax.ShapeDtypeStruct((1,), jnp.int32),
        )
        out_specs = (VMEM, VMEM, SMEM)
        scratch.append(pltpu.VMEM(top, f32))
    return pl.pallas_call(
        functools.partial(attend_kernel, first, numbers_of, len(blocks)),
        out_shape=out_shape,
        in_specs=[SMEM] + [VMEM] * len(operands),
        out_specs=out_specs,
        scratch_shapes=scratch,
        compiler_params=params(),
        cost_estimate=cost(14.0),
        name="attend_near" if first else "attend_far",
    )(mine, *operands)


def attend_shifted(mine, query, pieces, numbers):
    grouped = query.reshape(ROWS, HEADS, HD)
    stacked = jnp.concatenate(pieces, 0)
    count = stacked.shape[0] // ROWS
    table = jnp.stack(numbers).astype(jnp.int32)
    scale = 1.0 / math.sqrt(HD)
    positions = mine * ROWS + jnp.arange(ROWS, dtype=jnp.int32)
    initial = (
        jnp.full((HEADS, ROWS), MASKED, f32),
        jnp.zeros((HEADS, ROWS), f32),
        jnp.zeros((HEADS, ROWS, HD), f32),
    )

    def step(n, running):
        def visit(current):
            top, totals, numerator = current
            block = lax.dynamic_slice_in_dim(stacked, n * ROWS, ROWS, 0)
            scores = jnp.einsum("rgd,sd->grs", grouped, block[:, :HD], preferred_element_type=f32) * scale
            places = table[n] * ROWS + jnp.arange(ROWS, dtype=jnp.int32)
            visible = places[None, :] <= positions[:, None]
            scores = jnp.where(visible, scores, MASKED)
            new_top = jnp.maximum(top, jnp.max(scores, -1))
            rescale = jnp.exp(top - new_top)
            weights = jnp.where(visible, jnp.exp(scores - new_top[..., None]), 0.0)
            numerator = numerator * rescale[..., None] + jnp.einsum(
                "grs,sd->grd", weights.astype(bf16), block[:, HD:], preferred_element_type=f32
            )
            return (new_top, totals * rescale + jnp.sum(weights, -1), numerator)

        return lax.cond(table[n] <= mine, visit, lambda current: current, running)

    _, totals, numerator = lax.fori_loop(0, count, step, initial)
    result = (numerator / totals[..., None]).astype(bf16)
    result = jnp.transpose(result, (1, 0, 2)).reshape(ROWS, HEADS * HD)
    wide = result.astype(f32)
    return result, jnp.broadcast_to(jnp.sum(wide * wide, -1)[None], (8, ROWS))


def carry_kernel(
    mine_ref, query_ref, local_ref, grow_ref, kept_ref, handed_ref, chip_ref, core_ref, gain_ref, out_ref
):
    mine = mine_ref[0]
    plane, side, core = mine // 4, (mine // 2) % 2, mine % 2
    kept, handed = state_of(kept_ref), state_of(handed_ref)

    def pick(one, two, wanted):
        states = [jnp.where(wanted, jnp.where(core == 0, a, b), 0.0) for a, b in zip(one[0], two[0])]
        return states, jnp.where(wanted, jnp.where(core == 0, one[1], two[1]), 0.0)

    entering = pick(handed, kept, plane >= 2)
    entering = follow(entering, pick(kept, handed, plane >= 1))
    entering = follow(entering, state_of(chip_ref, side == 1))
    entering = follow(entering, state_of(core_ref, core == 1))
    grow = grow_ref[...]
    for h in range(HEADS):
        state = entering[0][h]
        upper = state.astype(bf16)
        lower = (state - upper.astype(f32)).astype(bf16)
        both = dot(query_ref[:, head(h)], jnp.concatenate([upper, lower], 1))
        entered = both[:, :HD] + both[:, HD:]
        result = local_ref[:, head(h)] + entered * grow[:, h : h + 1]
        square = jnp.mean(result * result, -1, keepdims=True)
        out_ref[:, head(h)] = result * lax.rsqrt(square + EPS) * gain_ref[head(h)][None, :]


def finish_kernel(features, attention_ref, square_ref, other_ref, linear_ref, gain_ref, out_ref):
    factor = lax.rsqrt((square_ref[...] + other_ref[...]) / features + EPS)
    factor = dot(factor, jnp.full((8, HD), 0.125, f32), ((0,), (0,)), highest)
    for h in range(HEADS):
        part = attention_ref[:, head(h)].astype(f32) * factor * gain_ref[head(h)][None, :]
        out_ref[:, head(h)] = (part + linear_ref[:, head(h)]).astype(bf16)


def simple(kernel, dtype, name, scalar, *operands):
    return pl.pallas_call(
        kernel,
        out_shape=jax.ShapeDtypeStruct((ROWS, HEADS * HD), dtype),
        in_specs=[SMEM] * len(scalar) + [VMEM] * len(operands),
        out_specs=VMEM,
        compiler_params=params(),
        cost_estimate=cost(2.0),
        name=name,
    )(*scalar, *operands)


def body(att_query, att_key, att_value, lh_query, lh_key, lh_value, lh_step, att_gain, lh_gain):
    mine = lax.axis_index("ctx")
    place = mine.reshape(1).astype(jnp.int32)

    def move(value, pairs):
        return lax.ppermute(value, "ctx", pairs)

    every = range(16)
    sibling = [(i, i ^ 1) for i in every]
    sideways = [(i, i ^ 2) for i in every]
    last_plane = [(i, i + 4) for i in every if i % 2 == 0 and i < 12] + [(i, i + 12) for i in (1, 3)]
    plane_before = [(i, i + 8) for i in every if i % 2 == 1 and i < 8]

    own = jnp.concatenate([att_key, att_value], 1)
    across = move(own, [(i, i ^ 2) for i in every if i < 4 or i % 4 < 2])
    near = move(own, sibling)
    chip = jnp.concatenate([own, near], 0)
    behind = move(chip, last_plane)
    beyond = move(chip, plane_before)

    local, grow, message = recur(lh_query, lh_key, lh_value, lh_step)
    other = move(message, sibling)
    of_chip = join(1, place, message, other)
    other_chip = move(of_chip, sideways)

    across_near = move(across, sibling)
    behind_near = move(behind, sibling)
    level = move(behind, [(i, j) for i, j in sideways if (i % 2 == 0 and i >= 4) or i >= 12])
    level_beyond = move(beyond, [(i, j) for i, j in sideways if i % 2 == 1 and i >= 8])

    def where(number, wanted):
        return jnp.where(wanted, number, NEVER)

    def parts(mine):
        return mine // 4, (mine // 2) % 2, mine % 2, mine - mine % 2

    def columns(number):
        return number + 2 - 4 * ((number // 2) % 2)

    def brought(mine, core):
        plane, _, _, even = parts(mine)
        if core == 0:
            return where(even - 4, plane >= 1)
        return where(even - 12, plane == 3)

    def near_numbers(mine):
        plane, side, core, even = parts(mine)
        siding = side == 1
        own_bring = jnp.where(core == 0, brought(mine, 0), brought(mine, 1))
        other_bring = jnp.where(core == 0, brought(mine, 1), brought(mine, 0))
        return [where(mine - 1, core == 1), where(even - 2, siding), where(even - 2, siding), own_bring, other_bring]

    def far_numbers(mine):
        plane, side, core, even = parts(mine)
        beyond_at = where(even - 8, plane >= 2)
        own_bring = jnp.where(core == 0, brought(mine, 0), brought(mine, 1))
        other_bring = jnp.where(core == 0, brought(mine, 1), brought(mine, 0))
        return [
            where(beyond_at, core == 1),
            where(beyond_at, core == 0),
            own_bring,
            other_bring,
            where(beyond_at, core == 1),
            where(beyond_at, core == 0),
        ]

    near_blocks = [near, across, across_near, behind, behind_near]
    carry = attend(place, att_query, own, None, near_blocks, near_numbers)

    of_plane = join(2, place, of_chip, other_chip)
    state_behind = move(of_plane, last_plane)
    state_beyond = move(of_plane, plane_before)

    beyond_near = move(beyond, sibling)
    level_near = move(level, sibling)
    level_beyond_near = move(level_beyond, sibling)
    far_blocks = [beyond, beyond_near, level, level_near, level_beyond, level_beyond_near]
    attention, squares, safe = attend(place, att_query, None, carry, far_blocks, far_numbers)

    def shifted():
        _, side, core, even = parts(mine)
        pieces = [own] + near_blocks + far_blocks
        firsts = [mine] + near_numbers(mine) + far_numbers(mine)
        flip = [False, False] + [False] * 2 + [True] * 2 + [True] * 6
        numbers = []
        for n, (piece, number) in enumerate(zip(pieces, firsts)):
            numbers += [number] if piece.shape[0] == ROWS else [number, number + 1]
        return attend_shifted(mine, att_query, pieces, numbers)

    attention, squares = lax.cond(safe[0] > 0, lambda: (attention, squares), shifted)

    kept = hand(place, state_behind, state_beyond)
    handed = move(kept, sibling)
    linear = simple(
        carry_kernel, f32, "carry", [place], lh_query, local, grow, kept, handed, other_chip, other, lh_gain
    )

    def over(value, bit):
        return lax.ppermute(value, "tp", [(i, i ^ bit) for i in range(8)])

    squares = squares + over(squares, 1)
    squares = squares + over(squares, 2)
    features = HEADS * HD * lax.axis_size("tp")
    return simple(
        functools.partial(finish_kernel, float(features)),
        bf16,
        "finish",
        [],
        attention,
        squares,
        over(squares, 4),
        linear,
        att_gain,
    )


def solution(mesh):
    placed = (P("ctx", "tp"),) * 7 + (P("tp"), P("tp"))
    return jax.shard_map(body, mesh=mesh, in_specs=placed, out_specs=P("ctx", "tp"), check_vma=False)
```

```python
import functools
import math

import jax
import jax.numpy as jnp
from jax import lax
from jax.experimental import pallas as pl
from jax.experimental.pallas import tpu as pltpu
from jax.sharding import PartitionSpec as P

HD = 128
ROWS = 512
HEADS = 6
TILE = 256
EPS = 1e-06
MASKED = -1e30
LOG2E = math.log2(math.e)
SCORE_SCALE = LOG2E / math.sqrt(HD)
SAFE_EXPONENT = 100.0
STATE_ROWS = HEADS * HD + 8
NEVER = 1 << 20

VMEM = pl.BlockSpec(memory_space=pltpu.VMEM)
SMEM = pl.BlockSpec(memory_space=pltpu.SMEM)
f32 = jnp.float32
bf16 = jnp.bfloat16
highest = lax.Precision.HIGHEST


def dot(a, b, contract=((1,), (0,)), precision=None):
    return lax.dot_general(a, b, (contract, ((), ())), precision=precision, preferred_element_type=f32)


def params(megabytes):
    return pltpu.CompilerParams(vmem_limit_bytes=megabytes << 20)


def cost(us):
    return pl.CostEstimate(flops=int(us * 1e9), bytes_accessed=int(us * 1e6), transcendentals=int(us * 1e6))


def head(h):
    return slice(h * HD, (h + 1) * HD)


def recur_kernel(q_ref, k_ref, v_ref, step_ref, local_ref, grow_ref, message_ref, padded):
    padded[...] = jnp.full((8, ROWS), 0.5, f32)
    padded[:HEADS, :] = step_ref[...]
    step = padded[...]
    rate = step / (1.0 + step)
    total = -jnp.log(1.0 + step) * LOG2E
    place = lax.broadcasted_iota(jnp.int32, (8, ROWS), 1)
    reach = 1
    while reach < ROWS:
        total = total + jnp.where(place >= reach, pltpu.roll(total, reach, 1), 0.0)
        reach *= 2
    source = jnp.log(rate) * LOG2E - total
    end = total[:, ROWS - 1 : ROWS]
    tail = jnp.exp2(end + source)
    rows = jnp.concatenate([total, tail, jnp.zeros((HD - 16, ROWS), f32)], 0)
    columns = jnp.transpose(rows)
    grow_ref[...] = jnp.exp2(columns)
    message_ref[HEADS * HD :, :] = jnp.broadcast_to(end, (8, HD))
    at_row = lax.broadcasted_iota(jnp.int32, (TILE, TILE), 0)
    at_column = lax.broadcasted_iota(jnp.int32, (TILE, TILE), 1)
    seen = at_column <= at_row
    for h in range(HEADS):
        keys = k_ref[:, head(h)].astype(f32)
        keys = keys * lax.rsqrt(jnp.sum(keys * keys, -1, keepdims=True) + EPS)
        unit = keys.astype(bf16)
        values = v_ref[:, head(h)]
        for a in range(0, ROWS, TILE):
            result = None
            for b in range(0, a + TILE, TILE):
                scores = dot(q_ref[a : a + TILE, head(h)], unit[b : b + TILE], ((1,), (1,)))
                decay = jnp.exp2(columns[a : a + TILE, h : h + 1] + source[h : h + 1, b : b + TILE])
                weights = scores * decay
                if a == b:
                    weights = jnp.where(seen, weights, 0.0)
                part = dot(weights.astype(bf16), values[b : b + TILE])
                result = part if result is None else result + part
            local_ref[a : a + TILE, head(h)] = result
        tailed = (values.astype(f32) * columns[:, 8 + h : 9 + h]).astype(bf16)
        message_ref[head(h), :] = dot(unit, tailed, ((0,), (0,)))


def recur(lh_query, lh_key, lh_value, lh_step):
    return pl.pallas_call(
        recur_kernel,
        out_shape=(
            jax.ShapeDtypeStruct((ROWS, HEADS * HD), f32),
            jax.ShapeDtypeStruct((ROWS, HD), f32),
            jax.ShapeDtypeStruct((STATE_ROWS, HD), f32),
        ),
        in_specs=[VMEM] * 4,
        out_specs=(VMEM,) * 3,
        scratch_shapes=[pltpu.VMEM((8, ROWS), f32)],
        compiler_params=params(16),
        cost_estimate=cost(2.5),
        name="recur",
    )(lh_query, lh_key, lh_value, lh_step.T)


def follow(early, late):
    logs = early[1] + late[1]
    states = [jnp.exp2(late[1][h : h + 1, :]) * early[0][h] + late[0][h] for h in range(HEADS)]
    return states, logs


def state_of(ref, wanted=None):
    states = [ref[head(h), :] for h in range(HEADS)]
    logs = ref[HEADS * HD :, :]
    if wanted is None:
        return states, logs
    return [jnp.where(wanted, state, 0.0) for state in states], jnp.where(wanted, logs, 0.0)


def put_state(ref, value):
    for h in range(HEADS):
        ref[head(h), :] = value[0][h]
    ref[HEADS * HD :, :] = value[1]


def join_kernel(bit, mine_ref, own_ref, other_ref, out_ref):
    own_first = (mine_ref[0] // bit) % 2 == 0
    own, other = state_of(own_ref), state_of(other_ref)

    def pick(one, two):
        return [jnp.where(own_first, a, b) for a, b in zip(one[0], two[0])], jnp.where(own_first, one[1], two[1])

    put_state(out_ref, follow(pick(own, other), pick(other, own)))


def join(bit, mine, own, other):
    return pl.pallas_call(
        functools.partial(join_kernel, bit),
        out_shape=jax.ShapeDtypeStruct((STATE_ROWS, HD), f32),
        in_specs=[SMEM, VMEM, VMEM],
        out_specs=VMEM,
        compiler_params=params(14),
        cost_estimate=cost(1.0),
        name="join",
    )(mine, own, other)


def hand_kernel(mine_ref, behind_ref, beyond_ref, out_ref):
    plane, core = mine_ref[0] // 4, mine_ref[0] % 2
    behind = state_of(behind_ref, (plane == 3) | (core == 0))
    beyond = state_of(beyond_ref, (plane >= 2) & (core == 1))
    put_state(out_ref, follow(behind, beyond))


def hand(mine, behind, beyond):
    return pl.pallas_call(
        hand_kernel,
        out_shape=jax.ShapeDtypeStruct((STATE_ROWS, HD), f32),
        in_specs=[SMEM, VMEM, VMEM],
        out_specs=VMEM,
        compiler_params=params(14),
        cost_estimate=cost(1.0),
        name="hand",
    )(mine, behind, beyond)


def attend_kernel(first, numbers_of, buffers, mine_ref, *refs):
    mine = mine_ref[0]
    refs = list(refs)
    query_ref = refs.pop(0)
    own_ref = refs.pop(0) if first else None
    carry_ref, count_ref, top_in_ref = (None,) * 3 if first else (refs.pop(0) for _ in range(3))
    block_refs = [refs.pop(0) for _ in range(buffers)]
    if first:
        numerator_ref, counted_ref, top_ref, sums, scaled, keys, values = refs
    else:
        out_ref, square_ref, safe_ref, sums, scaled, keys, values, top_ref = refs
    ones = jnp.ones((HD, HD), bf16)

    def norm(part):
        part = part.astype(f32)
        lengths = dot((part * part).astype(bf16), ones)
        return jnp.max(lengths.reshape(-1, 8, HD), 0)

    for h in range(HEADS):
        scaled[h * ROWS : (h + 1) * ROWS, :] = (query_ref[:, head(h)].astype(f32) * SCORE_SCALE).astype(bf16)
    sums[...] = jnp.zeros_like(sums)
    if first:
        top_ref[0:8, :] = norm(scaled[...])
        top_ref[8:16, :] = norm(own_ref[:, :HD])
    else:
        top_ref[...] = top_in_ref[...]
    values[:, HD:] = jnp.ones((values.shape[0], HD), bf16)

    filled = jnp.int32(0)
    for block, number in zip(block_refs, numbers_of(mine)):
        rows = block.shape[0]
        takes = number < mine
        place = filled

        @pl.when(takes)
        def _():
            at = pl.ds(pl.multiple_of(place * ROWS, ROWS), rows)
            keys[at, :] = block[:, :HD]
            values[at, :HD] = block[:, HD:]
            top_ref[8:16, :] = jnp.maximum(top_ref[8:16, :], norm(block[:, :HD]))

        filled = filled + jnp.where(takes, rows // ROWS, 0)

    def visit(start, count):
        at = pl.ds(pl.multiple_of(start, ROWS), count)
        block_keys = keys[at, :]
        block_values = values[at, :]
        for h in range(HEADS):
            for a in range(0, ROWS, TILE):
                query = scaled[h * ROWS + a : h * ROWS + a + TILE, :]
                weights = jnp.exp2(dot(query, block_keys, ((1,), (1,)))).astype(bf16)
                sums[h, a : a + TILE, :] += dot(weights, block_values)

    def pair(n, _):
        visit(n * 2 * ROWS, 2 * ROWS)
        return 0

    lax.fori_loop(0, filled // 2, pair, 0)

    if first:

        @pl.when(filled % 2 == 1)
        def _():
            visit((filled - 1) * ROWS, ROWS)

        at_row = lax.broadcasted_iota(jnp.int32, (TILE, TILE), 0)
        at_column = lax.broadcasted_iota(jnp.int32, (TILE, TILE), 1)
        seen = at_column <= at_row
        values[:ROWS, :HD] = own_ref[:, HD:]
        for h in range(HEADS):
            for a in range(0, ROWS, TILE):
                query = scaled[h * ROWS + a : h * ROWS + a + TILE, :]
                for b in range(0, a + TILE, TILE):
                    weights = jnp.exp2(dot(query, own_ref[b : b + TILE, :HD], ((1,), (1,))))
                    if a == b:
                        weights = jnp.where(seen, weights, 0.0)
                    sums[h, a : a + TILE, :] += dot(weights.astype(bf16), values[b : b + TILE, :])
            numerator_ref[:, head(h)] = sums[h, :, :HD]
            counted_ref[:, h : h + 1] = sums[h, :, HD : HD + 1]
    else:
        squares = jnp.zeros((ROWS, HD), f32)
        for h in range(HEADS):
            count = sums[h, :, HD:] + count_ref[:, h : h + 1]
            result = ((sums[h, :, :HD] + carry_ref[:, head(h)]) / count).astype(bf16)
            out_ref[:, head(h)] = result
            result = result.astype(f32)
            squares = squares + result * result
        square_ref[...] = dot(jnp.ones((8, HD), f32), squares, ((1,), (1,)), highest)
        bound = jnp.max(top_ref[:8, :]) * jnp.max(top_ref[8:, :])
        safe_ref[0] = jnp.where(bound * 1.05 <= SAFE_EXPONENT * SAFE_EXPONENT, 1, 0)


def attend(mine, query, own, carry, blocks, numbers_of):
    first = carry is None
    size = sum(block.shape[0] for block in blocks)
    operands = [query] + ([own] if first else list(carry)) + list(blocks)
    top = (16, HD)
    scratch = [
        pltpu.VMEM((HEADS, ROWS, 2 * HD), f32),
        pltpu.VMEM((HEADS * ROWS, HD), bf16),
        pltpu.VMEM((size, HD), bf16),
        pltpu.VMEM((size, 2 * HD), bf16),
    ]
    if first:
        out_shape = (
            jax.ShapeDtypeStruct((ROWS, HEADS * HD), f32),
            jax.ShapeDtypeStruct((ROWS, HD), f32),
            jax.ShapeDtypeStruct(top, f32),
        )
        out_specs = (VMEM,) * 3
    else:
        out_shape = (
            jax.ShapeDtypeStruct((ROWS, HEADS * HD), bf16),
            jax.ShapeDtypeStruct((8, ROWS), f32),
            jax.ShapeDtypeStruct((1,), jnp.int32),
        )
        out_specs = (VMEM, VMEM, SMEM)
        scratch.append(pltpu.VMEM(top, f32))
    return pl.pallas_call(
        functools.partial(attend_kernel, first, numbers_of, len(blocks)),
        out_shape=out_shape,
        in_specs=[SMEM] + [VMEM] * len(operands),
        out_specs=out_specs,
        scratch_shapes=scratch,
        compiler_params=params(26),
        cost_estimate=cost(14.0),
        name="attend_near" if first else "attend_far",
    )(mine, *operands)


def attend_shifted(mine, query, pieces, numbers):
    grouped = query.reshape(ROWS, HEADS, HD)
    stacked = jnp.concatenate(pieces, 0)
    count = stacked.shape[0] // ROWS
    table = jnp.stack(numbers).astype(jnp.int32)
    scale = 1.0 / math.sqrt(HD)
    positions = mine * ROWS + jnp.arange(ROWS, dtype=jnp.int32)
    initial = (
        jnp.full((HEADS, ROWS), MASKED, f32),
        jnp.zeros((HEADS, ROWS), f32),
        jnp.zeros((HEADS, ROWS, HD), f32),
    )

    def step(n, running):
        def visit(current):
            top, totals, numerator = current
            block = lax.dynamic_slice_in_dim(stacked, n * ROWS, ROWS, 0)
            scores = jnp.einsum("rgd,sd->grs", grouped, block[:, :HD], preferred_element_type=f32) * scale
            places = table[n] * ROWS + jnp.arange(ROWS, dtype=jnp.int32)
            visible = places[None, :] <= positions[:, None]
            scores = jnp.where(visible, scores, MASKED)
            new_top = jnp.maximum(top, jnp.max(scores, -1))
            rescale = jnp.exp(top - new_top)
            weights = jnp.where(visible, jnp.exp(scores - new_top[..., None]), 0.0)
            numerator = numerator * rescale[..., None] + jnp.einsum(
                "grs,sd->grd", weights.astype(bf16), block[:, HD:], preferred_element_type=f32
            )
            return (new_top, totals * rescale + jnp.sum(weights, -1), numerator)

        return lax.cond(table[n] <= mine, visit, lambda current: current, running)

    _, totals, numerator = lax.fori_loop(0, count, step, initial)
    result = (numerator / totals[..., None]).astype(bf16)
    result = jnp.transpose(result, (1, 0, 2)).reshape(ROWS, HEADS * HD)
    wide = result.astype(f32)
    return result, jnp.broadcast_to(jnp.sum(wide * wide, -1)[None], (8, ROWS))


def carry_kernel(
    mine_ref, query_ref, local_ref, grow_ref, kept_ref, handed_ref, chip_ref, core_ref, gain_ref, out_ref
):
    mine = mine_ref[0]
    plane, side, core = mine // 4, (mine // 2) % 2, mine % 2
    kept, handed = state_of(kept_ref), state_of(handed_ref)

    def pick(one, two, wanted):
        states = [jnp.where(wanted, jnp.where(core == 0, a, b), 0.0) for a, b in zip(one[0], two[0])]
        return states, jnp.where(wanted, jnp.where(core == 0, one[1], two[1]), 0.0)

    entering = pick(handed, kept, plane >= 2)
    entering = follow(entering, pick(kept, handed, plane >= 1))
    entering = follow(entering, state_of(chip_ref, side == 1))
    entering = follow(entering, state_of(core_ref, core == 1))
    grow = grow_ref[...]
    for h in range(HEADS):
        state = entering[0][h]
        upper = state.astype(bf16)
        lower = (state - upper.astype(f32)).astype(bf16)
        both = dot(query_ref[:, head(h)], jnp.concatenate([upper, lower], 1))
        entered = both[:, :HD] + both[:, HD:]
        result = local_ref[:, head(h)] + entered * grow[:, h : h + 1]
        square = jnp.mean(result * result, -1, keepdims=True)
        out_ref[:, head(h)] = result * lax.rsqrt(square + EPS) * gain_ref[head(h)][None, :]


def finish_kernel(features, attention_ref, square_ref, other_ref, linear_ref, gain_ref, out_ref):
    factor = lax.rsqrt((square_ref[...] + other_ref[...]) / features + EPS)
    factor = dot(factor, jnp.full((8, HD), 0.125, f32), ((0,), (0,)), highest)
    for h in range(HEADS):
        part = attention_ref[:, head(h)].astype(f32) * factor * gain_ref[head(h)][None, :]
        out_ref[:, head(h)] = (part + linear_ref[:, head(h)]).astype(bf16)


def simple(kernel, dtype, name, scalar, *operands):
    return pl.pallas_call(
        kernel,
        out_shape=jax.ShapeDtypeStruct((ROWS, HEADS * HD), dtype),
        in_specs=[SMEM] * len(scalar) + [VMEM] * len(operands),
        out_specs=VMEM,
        compiler_params=params(14),
        cost_estimate=cost(2.0),
        name=name,
    )(*scalar, *operands)


def body(att_query, att_key, att_value, lh_query, lh_key, lh_value, lh_step, att_gain, lh_gain):
    mine = lax.axis_index("ctx")
    place = mine.reshape(1).astype(jnp.int32)

    def move(value, pairs):
        return lax.ppermute(value, "ctx", pairs)

    every = range(16)
    sibling = [(i, i ^ 1) for i in every]
    sideways = [(i, i ^ 2) for i in every]
    last_plane = [(i, i + 4) for i in every if i % 2 == 0 and i < 12] + [(i, i + 12) for i in (1, 3)]
    plane_before = [(i, i + 8) for i in every if i % 2 == 1 and i < 8]

    own = jnp.concatenate([att_key, att_value], 1)
    across = move(own, [(i, i ^ 2) for i in every if i < 4 or i % 4 < 2])
    near = move(own, sibling)
    chip = jnp.concatenate([own, near], 0)
    chip, lh_step = lax.optimization_barrier((chip, lh_step))
    behind = move(chip, last_plane)
    beyond = move(chip, plane_before)

    local, grow, message = recur(lh_query, lh_key, lh_value, lh_step)
    other = move(message, sibling)
    of_chip = join(1, place, message, other)
    other_chip = move(of_chip, sideways)

    across_near = move(across, sibling)
    behind_near = move(behind, sibling)
    level = move(behind, [(i, j) for i, j in sideways if (i % 2 == 0 and i >= 4) or i >= 12])
    level_beyond = move(beyond, [(i, j) for i, j in sideways if i % 2 == 1 and i >= 8])

    def where(number, wanted):
        return jnp.where(wanted, number, NEVER)

    def parts(mine):
        return mine // 4, (mine // 2) % 2, mine % 2, mine - mine % 2

    def columns(number):
        return number + 2 - 4 * ((number // 2) % 2)

    def brought(mine, core):
        plane, _, _, even = parts(mine)
        if core == 0:
            return where(even - 4, plane >= 1)
        return where(even - 12, plane == 3)

    def near_numbers(mine):
        plane, side, core, even = parts(mine)
        siding = side == 1
        own_bring = jnp.where(core == 0, brought(mine, 0), brought(mine, 1))
        other_bring = jnp.where(core == 0, brought(mine, 1), brought(mine, 0))
        return [where(mine - 1, core == 1), where(even - 2, siding), where(even - 2, siding), own_bring, other_bring]

    def far_numbers(mine):
        plane, side, core, even = parts(mine)
        beyond_at = where(even - 8, plane >= 2)
        own_bring = jnp.where(core == 0, brought(mine, 0), brought(mine, 1))
        other_bring = jnp.where(core == 0, brought(mine, 1), brought(mine, 0))
        return [
            where(beyond_at, core == 1),
            where(beyond_at, core == 0),
            own_bring,
            other_bring,
            where(beyond_at, core == 1),
            where(beyond_at, core == 0),
        ]

    near_blocks = [near, across, across_near, behind, behind_near]
    near_blocks, of_chip = lax.optimization_barrier((near_blocks, of_chip))
    carry = attend(place, att_query, own, None, near_blocks, near_numbers)
    carry, other_chip, beyond, level, level_beyond = lax.optimization_barrier(
        (carry, other_chip, beyond, level, level_beyond)
    )

    of_plane = join(2, place, of_chip, other_chip)
    state_behind = move(of_plane, last_plane)
    state_beyond = move(of_plane, plane_before)

    beyond_near = move(beyond, sibling)
    level_near = move(level, sibling)
    level_beyond_near = move(level_beyond, sibling)
    far_blocks = [beyond, beyond_near, level, level_near, level_beyond, level_beyond_near]
    far_blocks, of_plane = lax.optimization_barrier((far_blocks, of_plane))
    attention, squares, safe = attend(place, att_query, None, carry, far_blocks, far_numbers)
    safe, state_behind, state_beyond = lax.optimization_barrier((safe, state_behind, state_beyond))

    def shifted():
        _, side, core, even = parts(mine)
        pieces = [own] + near_blocks + far_blocks
        firsts = [mine] + near_numbers(mine) + far_numbers(mine)
        flip = [False, False] + [False] * 2 + [True] * 2 + [True] * 6
        numbers = []
        for n, (piece, number) in enumerate(zip(pieces, firsts)):
            numbers += [number] if piece.shape[0] == ROWS else [number, number + 1]
        return attend_shifted(mine, att_query, pieces, numbers)

    attention, squares = lax.cond(safe[0] > 0, lambda: (attention, squares), shifted)

    kept = hand(place, state_behind, state_beyond)
    handed = move(kept, sibling)
    linear = simple(
        carry_kernel, f32, "carry", [place], lh_query, local, grow, kept, handed, other_chip, other, lh_gain
    )

    def over(value, bit):
        return lax.ppermute(value, "tp", [(i, i ^ bit) for i in range(8)])

    squares = squares + over(squares, 1)
    squares = squares + over(squares, 2)
    features = HEADS * HD * lax.axis_size("tp")
    return simple(
        functools.partial(finish_kernel, float(features)),
        bf16,
        "finish",
        [],
        attention,
        squares,
        over(squares, 4),
        linear,
        att_gain,
    )


def solution(mesh):
    placed = (P("ctx", "tp"),) * 7 + (P("tp"), P("tp"))
    return jax.shard_map(body, mesh=mesh, in_specs=placed, out_specs=P("ctx", "tp"), check_vma=False)
```

```python
import functools
import math

import jax
import jax.numpy as jnp
from jax import lax
from jax.experimental import pallas as pl
from jax.experimental.pallas import tpu as pltpu
from jax.sharding import PartitionSpec as P

HD = 128
ROWS = 512
HEADS = 6
TILE = 256
EPS = 1e-06
MASKED = -1e30
LOG2E = math.log2(math.e)
SCORE_SCALE = LOG2E / math.sqrt(HD)
SAFE_EXPONENT = 100.0
STATE_ROWS = HEADS * HD + 8
NEVER = 1 << 20

VMEM = pl.BlockSpec(memory_space=pltpu.VMEM)
SMEM = pl.BlockSpec(memory_space=pltpu.SMEM)
HBM = pl.BlockSpec(memory_space=pltpu.HBM)
f32 = jnp.float32
bf16 = jnp.bfloat16
highest = lax.Precision.HIGHEST


def dot(a, b, contract=((1,), (0,)), precision=None):
    return lax.dot_general(a, b, (contract, ((), ())), precision=precision, preferred_element_type=f32)


def params(megabytes):
    return pltpu.CompilerParams(vmem_limit_bytes=megabytes << 20)


def cost(us):
    return pl.CostEstimate(flops=int(us * 1e9), bytes_accessed=int(us * 1e6), transcendentals=int(us * 1e6))


def head(h):
    return slice(h * HD, (h + 1) * HD)


def fetch(source, target, done):
    copies = [
        pltpu.make_async_copy(source.at[:, head(h)], target.at[:, head(h)], done.at[h]) for h in range(HEADS)
    ]
    for copy in copies:
        copy.start()
    return copies


def recur_kernel(
    q_hbm, k_hbm, v_hbm, step_ref, local_ref, grow_ref, message_ref, padded, q_ref, k_ref, v_ref, k_in, q_in, v_in
):
    key_copies = fetch(k_hbm, k_ref, k_in)
    query_copies = fetch(q_hbm, q_ref, q_in)
    value_copies = fetch(v_hbm, v_ref, v_in)
    padded[...] = jnp.full((8, ROWS), 0.5, f32)
    padded[:HEADS, :] = step_ref[...]
    step = padded[...]
    rate = step / (1.0 + step)
    total = -jnp.log(1.0 + step) * LOG2E
    place = lax.broadcasted_iota(jnp.int32, (8, ROWS), 1)
    reach = 1
    while reach < ROWS:
        total = total + jnp.where(place >= reach, pltpu.roll(total, reach, 1), 0.0)
        reach *= 2
    source = jnp.log(rate) * LOG2E - total
    end = total[:, ROWS - 1 : ROWS]
    tail = jnp.exp2(end + source)
    rows = jnp.concatenate([total, tail, jnp.zeros((HD - 16, ROWS), f32)], 0)
    columns = jnp.transpose(rows)
    grow_ref[...] = jnp.exp2(columns)
    message_ref[HEADS * HD :, :] = jnp.broadcast_to(end, (8, HD))
    at_row = lax.broadcasted_iota(jnp.int32, (TILE, TILE), 0)
    at_column = lax.broadcasted_iota(jnp.int32, (TILE, TILE), 1)
    seen = at_column <= at_row
    for h in range(HEADS):
        key_copies[h].wait()
        query_copies[h].wait()
        value_copies[h].wait()
        keys = k_ref[:, head(h)].astype(f32)
        keys = keys * lax.rsqrt(jnp.sum(keys * keys, -1, keepdims=True) + EPS)
        unit = keys.astype(bf16)
        values = v_ref[:, head(h)]
        for a in range(0, ROWS, TILE):
            result = None
            for b in range(0, a + TILE, TILE):
                scores = dot(q_ref[a : a + TILE, head(h)], unit[b : b + TILE], ((1,), (1,)))
                decay = jnp.exp2(columns[a : a + TILE, h : h + 1] + source[h : h + 1, b : b + TILE])
                weights = scores * decay
                if a == b:
                    weights = jnp.where(seen, weights, 0.0)
                part = dot(weights.astype(bf16), values[b : b + TILE])
                result = part if result is None else result + part
            local_ref[a : a + TILE, head(h)] = result
        tailed = (values.astype(f32) * columns[:, 8 + h : 9 + h]).astype(bf16)
        message_ref[head(h), :] = dot(unit, tailed, ((0,), (0,)))


def recur(lh_query, lh_key, lh_value, lh_step):
    return pl.pallas_call(
        recur_kernel,
        out_shape=(
            jax.ShapeDtypeStruct((ROWS, HEADS * HD), f32),
            jax.ShapeDtypeStruct((ROWS, HD), f32),
            jax.ShapeDtypeStruct((STATE_ROWS, HD), f32),
        ),
        in_specs=[HBM] * 3 + [VMEM],
        out_specs=(VMEM,) * 3,
        scratch_shapes=[pltpu.VMEM((8, ROWS), f32)]
        + [pltpu.VMEM((ROWS, HEADS * HD), bf16)] * 3
        + [pltpu.SemaphoreType.DMA((HEADS,))] * 3,
        compiler_params=params(16),
        cost_estimate=cost(0.2),
        name="recur",
    )(lh_query, lh_key, lh_value, lh_step.T)


def beside_kernel(key_hbm, value_hbm, out_ref, done):
    copies = [
        pltpu.make_async_copy(key_hbm, out_ref.at[:, :HD], done.at[0]),
        pltpu.make_async_copy(value_hbm, out_ref.at[:, HD:], done.at[1]),
    ]
    for copy in copies:
        copy.start()
    for copy in copies:
        copy.wait()


def beside(key, value):
    return pl.pallas_call(
        beside_kernel,
        out_shape=jax.ShapeDtypeStruct((ROWS, 2 * HD), bf16),
        in_specs=[HBM, HBM],
        out_specs=VMEM,
        scratch_shapes=[pltpu.SemaphoreType.DMA((2,))],
        compiler_params=params(14),
        name="beside",
    )(key, value)


def stack_kernel(one_ref, two_ref, out_ref):
    out_ref[:ROWS, :] = one_ref[...]
    out_ref[ROWS:, :] = two_ref[...]


def stack(one, two):
    return pl.pallas_call(
        stack_kernel,
        out_shape=jax.ShapeDtypeStruct((2 * ROWS, 2 * HD), bf16),
        in_specs=[VMEM, VMEM],
        out_specs=VMEM,
        compiler_params=params(14),
        name="stack",
    )(one, two)


def follow(early, late):
    logs = early[1] + late[1]
    states = [jnp.exp2(late[1][h : h + 1, :]) * early[0][h] + late[0][h] for h in range(HEADS)]
    return states, logs


def state_of(ref, wanted=None):
    states = [ref[head(h), :] for h in range(HEADS)]
    logs = ref[HEADS * HD :, :]
    if wanted is None:
        return states, logs
    return [jnp.where(wanted, state, 0.0) for state in states], jnp.where(wanted, logs, 0.0)


def put_state(ref, value):
    for h in range(HEADS):
        ref[head(h), :] = value[0][h]
    ref[HEADS * HD :, :] = value[1]


def join_kernel(bit, mine_ref, own_ref, other_ref, out_ref):
    own_first = (mine_ref[0] // bit) % 2 == 0
    own, other = state_of(own_ref), state_of(other_ref)

    def pick(one, two):
        return [jnp.where(own_first, a, b) for a, b in zip(one[0], two[0])], jnp.where(own_first, one[1], two[1])

    put_state(out_ref, follow(pick(own, other), pick(other, own)))


def join_pair_kernel(first_ref, second_ref, out_ref):
    put_state(out_ref, follow(state_of(first_ref), state_of(second_ref)))


def join_pair(first, second):
    return pl.pallas_call(
        join_pair_kernel,
        out_shape=jax.ShapeDtypeStruct((STATE_ROWS, HD), f32),
        in_specs=[VMEM, VMEM],
        out_specs=VMEM,
        compiler_params=params(14),
        cost_estimate=cost(0.2),
        name="join",
    )(first, second)


def join(bit, mine, own, other):
    return pl.pallas_call(
        functools.partial(join_kernel, bit),
        out_shape=jax.ShapeDtypeStruct((STATE_ROWS, HD), f32),
        in_specs=[SMEM, VMEM, VMEM],
        out_specs=VMEM,
        compiler_params=params(14),
        cost_estimate=cost(0.2),
        name="join",
    )(mine, own, other)


def hand_kernel(mine_ref, behind_ref, beyond_ref, out_ref):
    plane, core = mine_ref[0] // 4, mine_ref[0] % 2
    behind = state_of(behind_ref, (plane == 3) | (core == 0))
    beyond = state_of(beyond_ref, (plane >= 2) & (core == 1))
    put_state(out_ref, follow(behind, beyond))


def hand(mine, behind, beyond):
    return pl.pallas_call(
        hand_kernel,
        out_shape=jax.ShapeDtypeStruct((STATE_ROWS, HD), f32),
        in_specs=[SMEM, VMEM, VMEM],
        out_specs=VMEM,
        compiler_params=params(14),
        cost_estimate=cost(0.2),
        name="hand",
    )(mine, behind, beyond)


def attend_kernel(first, last, numbers_of, buffers, mine_ref, *refs):
    mine = mine_ref[0]
    refs = list(refs)

    def take(count):
        return [refs.pop(0) for _ in range(count)]

    if first:
        query_hbm, own_ref = take(2)
    else:
        scaled, carry_ref, count_ref, top_in_ref = take(4)
    block_refs = take(buffers)
    if first:
        scaled, numerator_ref, counted_ref, top_ref, sums, keys, values, query_ref, query_in = refs
        copies = fetch(query_hbm, query_ref, query_in)
    elif last:
        out_ref, square_ref, safe_ref, sums, keys, values, top_ref = refs
    else:
        numerator_ref, counted_ref, top_ref, sums, keys, values = refs

    def highest_of(part):
        return jnp.max(jnp.abs(part).reshape(-1, 16, HD), 0)

    if first:
        top_ref[16:32, :] = highest_of(own_ref[:, :HD])
    else:
        top_ref[...] = top_in_ref[...]
    values[:, HD:] = jnp.ones((values.shape[0], HD), bf16)

    filled = jnp.int32(0)
    for block, number in zip(block_refs, numbers_of(mine)):
        rows = block.shape[0]
        takes = number < mine
        place = filled

        @pl.when(takes)
        def _():
            at = pl.ds(pl.multiple_of(place * ROWS, ROWS), rows)
            keys[at, :] = block[:, :HD]
            values[at, :HD] = block[:, HD:]
            top_ref[16:32, :] = jnp.maximum(top_ref[16:32, :], highest_of(block[:, :HD]))

        filled = filled + jnp.where(takes, rows // ROWS, 0)

    if first:
        longest = jnp.zeros((ROWS, HD), f32)
        ones = jnp.ones((HD, HD), bf16)
        for h in range(HEADS):
            copies[h].wait()
            query = query_ref[:, head(h)].astype(f32) * SCORE_SCALE
            scaled[h * ROWS : (h + 1) * ROWS, :] = query.astype(bf16)
            longest = jnp.maximum(longest, dot((query * query).astype(bf16), ones))
        top_ref[0:16, :] = jnp.max(longest.reshape(-1, 16, HD), 0).astype(bf16)
    sums[...] = jnp.zeros_like(sums)

    def visit(start, count):
        at = pl.ds(pl.multiple_of(start, ROWS), count)
        block_keys = keys[at, :]
        block_values = values[at, :]
        for h in range(HEADS):
            for a in range(0, ROWS, TILE):
                query = scaled[h * ROWS + a : h * ROWS + a + TILE, :]
                weights = jnp.exp2(dot(query, block_keys, ((1,), (1,)))).astype(bf16)
                sums[h, a : a + TILE, :] += dot(weights, block_values)

    def pair(n, _):
        visit(n * 2 * ROWS, 2 * ROWS)
        return 0

    lax.fori_loop(0, filled // 2, pair, 0)

    if first:

        @pl.when(filled % 2 == 1)
        def _():
            visit((filled - 1) * ROWS, ROWS)

        at_row = lax.broadcasted_iota(jnp.int32, (TILE, TILE), 0)
        at_column = lax.broadcasted_iota(jnp.int32, (TILE, TILE), 1)
        seen = at_column <= at_row
        values[:ROWS, :HD] = own_ref[:, HD:]
        for h in range(HEADS):
            for a in range(0, ROWS, TILE):
                query = scaled[h * ROWS + a : h * ROWS + a + TILE, :]
                for b in range(0, a + TILE, TILE):
                    weights = jnp.exp2(dot(query, own_ref[b : b + TILE, :HD], ((1,), (1,))))
                    if a == b:
                        weights = jnp.where(seen, weights, 0.0)
                    sums[h, a : a + TILE, :] += dot(weights.astype(bf16), values[b : b + TILE, :])
            numerator_ref[:, head(h)] = sums[h, :, :HD]
            counted_ref[:, h : h + 1] = sums[h, :, HD : HD + 1]
    elif not last:
        for h in range(HEADS):
            numerator_ref[:, head(h)] = sums[h, :, :HD] + carry_ref[:, head(h)]
            counted_ref[:, h : h + 1] = sums[h, :, HD : HD + 1] + count_ref[:, h : h + 1]
    else:
        squares = jnp.zeros((ROWS, HD), f32)
        for h in range(HEADS):
            count = sums[h, :, HD:] + count_ref[:, h : h + 1]
            result = ((sums[h, :, :HD] + carry_ref[:, head(h)]) / count).astype(bf16)
            out_ref[:, head(h)] = result
            result = result.astype(f32)
            squares = squares + result * result
        square_ref[...] = dot(jnp.ones((8, HD), f32), squares, ((1,), (1,)), highest)
        key_top = jnp.max(top_ref[16:32, :].astype(f32), 0, keepdims=True)
        bound = jnp.max(top_ref[0:16, :].astype(f32)) * jnp.sum(key_top * key_top)
        safe_ref[0] = jnp.where(bound * 1.05 <= SAFE_EXPONENT * SAFE_EXPONENT, 1, 0)


def attend(mine, query, own, carry, blocks, numbers_of, last=False):
    first = carry is None
    size = sum(block.shape[0] for block in blocks)
    operands = [query, own] if first else list(carry)
    top = (32, HD)
    in_specs = [SMEM] + ([HBM] if first else [VMEM]) + [VMEM] * (len(operands) - 1 + len(blocks))
    scratch = [
        pltpu.VMEM((HEADS, ROWS, 2 * HD), f32),
        pltpu.VMEM((size, HD), bf16),
        pltpu.VMEM((size, 2 * HD), bf16),
    ]
    if last:
        out_shape = (
            jax.ShapeDtypeStruct((ROWS, HEADS * HD), bf16),
            jax.ShapeDtypeStruct((8, ROWS), f32),
            jax.ShapeDtypeStruct((1,), jnp.int32),
        )
        out_specs = (VMEM, VMEM, SMEM)
        scratch.append(pltpu.VMEM(top, bf16))
    else:
        out_shape = (
            jax.ShapeDtypeStruct((ROWS, HEADS * HD), f32),
            jax.ShapeDtypeStruct((ROWS, HD), f32),
            jax.ShapeDtypeStruct(top, bf16),
        )
        if first:
            out_shape = (jax.ShapeDtypeStruct((HEADS * ROWS, HD), bf16),) + out_shape
            scratch += [pltpu.VMEM((ROWS, HEADS * HD), bf16), pltpu.SemaphoreType.DMA((HEADS,))]
        out_specs = (VMEM,) * len(out_shape)
    result = pl.pallas_call(
        functools.partial(attend_kernel, first, last, numbers_of, len(blocks)),
        out_shape=out_shape,
        in_specs=in_specs,
        out_specs=out_specs,
        scratch_shapes=scratch,
        compiler_params=params(20),
        cost_estimate=cost(0.2),
        name="attend_first" if first else "attend_last" if last else "attend_middle",
    )(mine, *operands, *blocks)
    if first or last:
        return result
    return (carry[0],) + tuple(result)


def attend_shifted(mine, query, pieces, numbers):
    grouped = query.reshape(ROWS, HEADS, HD)
    stacked = jnp.concatenate(pieces, 0)
    count = stacked.shape[0] // ROWS
    table = jnp.stack(numbers).astype(jnp.int32)
    scale = 1.0 / math.sqrt(HD)
    positions = mine * ROWS + jnp.arange(ROWS, dtype=jnp.int32)
    initial = (
        jnp.full((HEADS, ROWS), MASKED, f32),
        jnp.zeros((HEADS, ROWS), f32),
        jnp.zeros((HEADS, ROWS, HD), f32),
    )

    def step(n, running):
        def visit(current):
            top, totals, numerator = current
            block = lax.dynamic_slice_in_dim(stacked, n * ROWS, ROWS, 0)
            scores = jnp.einsum("rgd,sd->grs", grouped, block[:, :HD], preferred_element_type=f32) * scale
            places = table[n] * ROWS + jnp.arange(ROWS, dtype=jnp.int32)
            visible = places[None, :] <= positions[:, None]
            scores = jnp.where(visible, scores, MASKED)
            new_top = jnp.maximum(top, jnp.max(scores, -1))
            rescale = jnp.exp(top - new_top)
            weights = jnp.where(visible, jnp.exp(scores - new_top[..., None]), 0.0)
            numerator = numerator * rescale[..., None] + jnp.einsum(
                "grs,sd->grd", weights.astype(bf16), block[:, HD:], preferred_element_type=f32
            )
            return (new_top, totals * rescale + jnp.sum(weights, -1), numerator)

        return lax.cond(table[n] <= mine, visit, lambda current: current, running)

    _, totals, numerator = lax.fori_loop(0, count, step, initial)
    result = (numerator / totals[..., None]).astype(bf16)
    result = jnp.transpose(result, (1, 0, 2)).reshape(ROWS, HEADS * HD)
    wide = result.astype(f32)
    return result, jnp.broadcast_to(jnp.sum(wide * wide, -1)[None], (8, ROWS))


def carry_kernel(
    mine_ref,
    query_hbm,
    local_ref,
    grow_ref,
    kept_ref,
    handed_ref,
    chip_ref,
    core_ref,
    gain_ref,
    out_ref,
    query_ref,
    query_in,
):
    mine = mine_ref[0]
    copies = fetch(query_hbm, query_ref, query_in)
    plane, side, core = mine // 4, (mine // 2) % 2, mine % 2
    kept, handed = state_of(kept_ref), state_of(handed_ref)

    def pick(one, two, wanted):
        states = [jnp.where(wanted, jnp.where(core == 0, a, b), 0.0) for a, b in zip(one[0], two[0])]
        return states, jnp.where(wanted, jnp.where(core == 0, one[1], two[1]), 0.0)

    entering = pick(handed, kept, plane >= 2)
    entering = follow(entering, pick(kept, handed, plane >= 1))
    entering = follow(entering, state_of(chip_ref, side == 1))
    entering = follow(entering, state_of(core_ref, core == 1))
    grow = grow_ref[...]
    for h in range(HEADS):
        state = entering[0][h]
        upper = state.astype(bf16)
        lower = (state - upper.astype(f32)).astype(bf16)
        copies[h].wait()
        both = dot(query_ref[:, head(h)], jnp.concatenate([upper, lower], 1))
        entered = both[:, :HD] + both[:, HD:]
        result = local_ref[:, head(h)] + entered * grow[:, h : h + 1]
        square = jnp.mean(result * result, -1, keepdims=True)
        out_ref[:, head(h)] = result * lax.rsqrt(square + EPS) * gain_ref[head(h)][None, :]


def finish_kernel(features, attention_ref, square_ref, other_ref, linear_ref, gain_ref, out_ref):
    factor = lax.rsqrt((square_ref[...] + other_ref[...]) / features + EPS)
    factor = dot(factor, jnp.full((8, HD), 0.125, f32), ((0,), (0,)), highest)
    for h in range(HEADS):
        part = attention_ref[:, head(h)].astype(f32) * factor * gain_ref[head(h)][None, :]
        out_ref[:, head(h)] = (part + linear_ref[:, head(h)]).astype(bf16)


def carry_in(place, lh_query, *operands):
    return pl.pallas_call(
        carry_kernel,
        out_shape=jax.ShapeDtypeStruct((ROWS, HEADS * HD), f32),
        in_specs=[SMEM, HBM] + [VMEM] * len(operands),
        out_specs=VMEM,
        scratch_shapes=[pltpu.VMEM((ROWS, HEADS * HD), bf16), pltpu.SemaphoreType.DMA((HEADS,))],
        compiler_params=params(14),
        cost_estimate=cost(0.2),
        name="carry",
    )(place, lh_query, *operands)


def finish(features, *operands):
    return pl.pallas_call(
        functools.partial(finish_kernel, features),
        out_shape=jax.ShapeDtypeStruct((ROWS, HEADS * HD), bf16),
        in_specs=[VMEM] * len(operands),
        out_specs=VMEM,
        compiler_params=params(14),
        cost_estimate=cost(0.2),
        name="finish",
    )(*operands)


def body(att_query, att_key, att_value, lh_query, lh_key, lh_value, lh_step, att_gain, lh_gain):
    mine = lax.axis_index("ctx")
    place = mine.reshape(1).astype(jnp.int32)

    def move(value, pairs):
        return lax.ppermute(value, "ctx", pairs)

    every = range(16)
    sibling = [(i, i ^ 1) for i in every]
    sideways = [(i, i ^ 2) for i in every]
    last_plane = [(i, i + 4) for i in every if i % 2 == 0 and i < 12] + [(i, i + 12) for i in (1, 3)]
    plane_before = [(i, i + 8) for i in every if i % 2 == 1 and i < 8]

    def tied(*values):
        return lax.optimization_barrier(values)

    lh_query, lh_key, lh_value, far_query, att_key, att_value = [
        pltpu.with_memory_space_constraint(array, pltpu.HBM)
        for array in (lh_query, lh_key, lh_value, att_query, att_key, att_value)
    ]
    own = beside(att_key, att_value)
    across = move(own, [(i, i ^ 2) for i in every if i < 4 or i % 4 < 2])
    near = move(own, sibling)
    chip = stack(own, near)
    chip, lh_step = tied(chip, lh_step)
    behind = move(chip, last_plane)
    beyond = move(chip, plane_before)

    local, grow, message = recur(lh_query, lh_key, lh_value, lh_step)
    across, message = tied(across, message)
    both = lax.all_gather(message, "ctx", axis_index_groups=[[i, i + 1] for i in every if i % 2 == 0])
    first, second = both[0], both[1]
    of_chip = join_pair(first, second)
    other_chip = move(of_chip, sideways)
    across_near = move(across, sibling)

    def where(number, wanted):
        return jnp.where(wanted, number, NEVER)

    def parts(mine):
        return mine // 4, (mine // 2) % 2, mine % 2, mine - mine % 2

    def brought(mine, core):
        plane, _, _, even = parts(mine)
        if core == 0:
            return where(even - 4, plane >= 1)
        return where(even - 12, plane == 3)

    def first_numbers(mine):
        _, side, core, even = parts(mine)
        return [where(mine - 1, core == 1)] + [where(even - 2, side == 1)] * 2

    def behind_numbers(mine):
        _, _, core, _ = parts(mine)
        zero, one = brought(mine, 0), brought(mine, 1)
        return [jnp.where(core == 0, zero, one), jnp.where(core == 0, one, zero)]

    def beyond_numbers(mine):
        plane, _, core, even = parts(mine)
        number = where(even - 8, plane >= 2)
        return [where(number, core == 1), where(number, core == 0)]

    def both_numbers(mine):
        return behind_numbers(mine) + beyond_numbers(mine)

    first_blocks = [near, across, across_near]
    carry = attend(place, far_query, own, None, first_blocks, first_numbers)

    carry, behind, beyond = tied(carry, behind, beyond)
    level = move(behind, [(i, j) for i, j in sideways if (i % 2 == 0 and i >= 4) or i >= 12])
    behind_near = move(behind, sibling)
    level_beyond = move(beyond, [(i, j) for i, j in sideways if i % 2 == 1 and i >= 8])
    beyond_near = move(beyond, sibling)
    middle_blocks = [behind, behind_near, beyond, beyond_near]
    carry = attend(place, None, None, carry, middle_blocks, both_numbers)

    carry, other_chip, level, level_beyond = tied(carry, other_chip, level, level_beyond)
    of_plane = join(2, place, of_chip, other_chip)
    state_behind = move(of_plane, last_plane)
    state_beyond = move(of_plane, plane_before)
    level_near = move(level, sibling)
    level_beyond_near = move(level_beyond, sibling)
    last_blocks = [level, level_near, level_beyond, level_beyond_near]
    last_blocks, of_plane = tied(last_blocks, of_plane)
    attention, squares, safe = attend(place, None, None, carry, last_blocks, both_numbers, last=True)
    safe, squares, state_behind, state_beyond = tied(safe, squares, state_behind, state_beyond)

    def shifted():
        pieces = [own] + first_blocks + middle_blocks + last_blocks
        firsts = [mine] + first_numbers(mine) + both_numbers(mine) + both_numbers(mine)
        numbers = []
        for piece, number in zip(pieces, firsts):
            numbers += [number] if piece.shape[0] == ROWS else [number, number + 1]
        return attend_shifted(mine, att_query, pieces, numbers)

    attention, squares = lax.cond(safe[0] > 0, lambda: (attention, squares), shifted)

    kept = hand(place, state_behind, state_beyond)
    handed = move(kept, sibling)
    linear = carry_in(place, lh_query, local, grow, kept, handed, other_chip, first, lh_gain)

    def over(value, bit):
        return lax.ppermute(value, "tp", [(i, i ^ bit) for i in range(8)])

    first_round = over(squares, 1)
    first_round, linear = tied(first_round, linear)
    squares = squares + first_round
    squares = squares + over(squares, 2)
    features = HEADS * HD * lax.axis_size("tp")
    return finish(float(features), attention, squares, over(squares, 4), linear, att_gain)


def solution(mesh):
    placed = (P("ctx", "tp"),) * 7 + (P("tp"), P("tp"))
    return jax.shard_map(body, mesh=mesh, in_specs=placed, out_specs=P("ctx", "tp"), check_vma=False)
```

```python
import functools
import math

import jax
import jax.numpy as jnp
from jax import lax
from jax.experimental import pallas as pl
from jax.experimental.pallas import tpu as pltpu
from jax.sharding import PartitionSpec as P

HD = 128
ROWS = 512
HEADS = 6
TILE = 256
EPS = 1e-06
MASKED = -1e30
LOG2E = math.log2(math.e)
SCORE_SCALE = LOG2E / math.sqrt(HD)
SAFE_EXPONENT = 100.0
STATE_ROWS = HEADS * HD + 8
NEVER = 1 << 20

VMEM = pl.BlockSpec(memory_space=pltpu.VMEM)
SMEM = pl.BlockSpec(memory_space=pltpu.SMEM)
f32 = jnp.float32
bf16 = jnp.bfloat16
highest = lax.Precision.HIGHEST


def dot(a, b, contract=((1,), (0,)), precision=None):
    return lax.dot_general(a, b, (contract, ((), ())), precision=precision, preferred_element_type=f32)


def params(megabytes):
    return pltpu.CompilerParams(vmem_limit_bytes=megabytes << 20)


def cost(us):
    return pl.CostEstimate(flops=int(us * 1e9), bytes_accessed=int(us * 1e6), transcendentals=int(us * 1e6))


def head(h):
    return slice(h * HD, (h + 1) * HD)


def recur_kernel(
    q_hbm, k_hbm, v_hbm, step_ref, local_ref, grow_ref, message_ref, padded
):
    k_ref, q_ref, v_ref = k_hbm, q_hbm, v_hbm
    padded[...] = jnp.full((8, ROWS), 0.5, f32)
    padded[:HEADS, :] = step_ref[...]
    step = padded[...]
    rate = step / (1.0 + step)
    total = -jnp.log(1.0 + step) * LOG2E
    place = lax.broadcasted_iota(jnp.int32, (8, ROWS), 1)
    reach = 1
    while reach < ROWS:
        total = total + jnp.where(place >= reach, pltpu.roll(total, reach, 1), 0.0)
        reach *= 2
    source = jnp.log(rate) * LOG2E - total
    end = total[:, ROWS - 1 : ROWS]
    tail = jnp.exp2(end + source)
    rows = jnp.concatenate([total, tail, jnp.zeros((HD - 16, ROWS), f32)], 0)
    columns = jnp.transpose(rows)
    grow_ref[...] = jnp.exp2(columns)
    message_ref[HEADS * HD :, :] = jnp.broadcast_to(end, (8, HD))
    at_row = lax.broadcasted_iota(jnp.int32, (TILE, TILE), 0)
    at_column = lax.broadcasted_iota(jnp.int32, (TILE, TILE), 1)
    seen = at_column <= at_row
    for h in range(HEADS):
        keys = k_ref[:, head(h)].astype(f32)
        keys = keys * lax.rsqrt(jnp.sum(keys * keys, -1, keepdims=True) + EPS)
        unit = keys.astype(bf16)
        values = v_ref[:, head(h)]
        for a in range(0, ROWS, TILE):
            result = None
            for b in range(0, a + TILE, TILE):
                scores = dot(q_ref[a : a + TILE, head(h)], unit[b : b + TILE], ((1,), (1,)))
                decay = jnp.exp2(columns[a : a + TILE, h : h + 1] + source[h : h + 1, b : b + TILE])
                weights = scores * decay
                if a == b:
                    weights = jnp.where(seen, weights, 0.0)
                part = dot(weights.astype(bf16), values[b : b + TILE])
                result = part if result is None else result + part
            local_ref[a : a + TILE, head(h)] = result
        tailed = (values.astype(f32) * columns[:, 8 + h : 9 + h]).astype(bf16)
        message_ref[head(h), :] = dot(unit, tailed, ((0,), (0,)))


def recur(lh_query, lh_key, lh_value, lh_step):
    return pl.pallas_call(
        recur_kernel,
        out_shape=(
            jax.ShapeDtypeStruct((ROWS, HEADS * HD), f32),
            jax.ShapeDtypeStruct((ROWS, HD), f32),
            jax.ShapeDtypeStruct((STATE_ROWS, HD), f32),
        ),
        in_specs=[VMEM] * 4,
        out_specs=(VMEM,) * 3,
        scratch_shapes=[pltpu.VMEM((8, ROWS), f32)]
,
        compiler_params=params(16),
        cost_estimate=cost(0.2),
        name="recur",
    )(lh_query, lh_key, lh_value, lh_step.T)


def beside_kernel(key_ref, value_ref, out_ref):
    out_ref[:, :HD] = key_ref[...]
    out_ref[:, HD:] = value_ref[...]


def beside(key, value):
    return pl.pallas_call(
        beside_kernel,
        out_shape=jax.ShapeDtypeStruct((ROWS, 2 * HD), bf16),
        in_specs=[VMEM, VMEM],
        out_specs=VMEM,
        compiler_params=params(14),
        name="beside",
    )(key, value)


def stack_kernel(one_ref, two_ref, out_ref):
    out_ref[:ROWS, :] = one_ref[...]
    out_ref[ROWS:, :] = two_ref[...]


def stack(one, two):
    return pl.pallas_call(
        stack_kernel,
        out_shape=jax.ShapeDtypeStruct((2 * ROWS, 2 * HD), bf16),
        in_specs=[VMEM, VMEM],
        out_specs=VMEM,
        compiler_params=params(14),
        name="stack",
    )(one, two)


def follow(early, late):
    logs = early[1] + late[1]
    states = [jnp.exp2(late[1][h : h + 1, :]) * early[0][h] + late[0][h] for h in range(HEADS)]
    return states, logs


def state_of(ref, wanted=None):
    states = [ref[head(h), :] for h in range(HEADS)]
    logs = ref[HEADS * HD :, :]
    if wanted is None:
        return states, logs
    return [jnp.where(wanted, state, 0.0) for state in states], jnp.where(wanted, logs, 0.0)


def put_state(ref, value):
    for h in range(HEADS):
        ref[head(h), :] = value[0][h]
    ref[HEADS * HD :, :] = value[1]


def join_kernel(bit, mine_ref, own_ref, other_ref, out_ref):
    own_first = (mine_ref[0] // bit) % 2 == 0
    own, other = state_of(own_ref), state_of(other_ref)

    def pick(one, two):
        return [jnp.where(own_first, a, b) for a, b in zip(one[0], two[0])], jnp.where(own_first, one[1], two[1])

    put_state(out_ref, follow(pick(own, other), pick(other, own)))


def join(bit, mine, own, other):
    return pl.pallas_call(
        functools.partial(join_kernel, bit),
        out_shape=jax.ShapeDtypeStruct((STATE_ROWS, HD), f32),
        in_specs=[SMEM, VMEM, VMEM],
        out_specs=VMEM,
        compiler_params=params(14),
        cost_estimate=cost(0.2),
        name="join",
    )(mine, own, other)


def hand_kernel(mine_ref, behind_ref, beyond_ref, out_ref):
    plane, core = mine_ref[0] // 4, mine_ref[0] % 2
    behind = state_of(behind_ref, (plane == 3) | (core == 0))
    beyond = state_of(beyond_ref, (plane >= 2) & (core == 1))
    put_state(out_ref, follow(behind, beyond))


def hand(mine, behind, beyond):
    return pl.pallas_call(
        hand_kernel,
        out_shape=jax.ShapeDtypeStruct((STATE_ROWS, HD), f32),
        in_specs=[SMEM, VMEM, VMEM],
        out_specs=VMEM,
        compiler_params=params(14),
        cost_estimate=cost(0.2),
        name="hand",
    )(mine, behind, beyond)


def attend_kernel(first, last, numbers_of, buffers, kept_numbers_of, kept, mine_ref, query_ref, own_ref, *refs):
    mine = mine_ref[0]
    refs = list(refs)

    def take(count):
        return [refs.pop(0) for _ in range(count)]

    if not first:
        carry_ref, count_ref, top_in_ref = take(3)
    block_refs = take(buffers)
    kept_refs = take(kept)
    if last:
        out_ref, square_ref, sums, keys, values, top_ref, tops = refs
    else:
        numerator_ref, counted_ref, top_ref, sums, keys, values = refs

    def highest_of(part):
        return jnp.max(jnp.abs(part).reshape(-1, 16, HD), 0)

    def fill(blocks, numbers):
        filled = jnp.int32(0)
        for block, number in zip(blocks, numbers):
            rows = block.shape[0]
            takes = number < mine
            place = filled

            @pl.when(takes)
            def _():
                at = pl.ds(pl.multiple_of(place * ROWS, ROWS), rows)
                keys[at, :] = block[:, :HD]
                values[at, :HD] = block[:, HD:]
                top_ref[16:32, :] = jnp.maximum(top_ref[16:32, :], highest_of(block[:, :HD]))

            filled = filled + jnp.where(takes, rows // ROWS, 0)
        return filled

    if first:
        top_ref[16:32, :] = highest_of(own_ref[:, :HD])
        longest = jnp.zeros((ROWS, HD), f32)
        ones = jnp.ones((HD, HD), bf16)
        for h in range(HEADS):
            query = query_ref[:, head(h)].astype(f32)
            longest = jnp.maximum(longest, dot((query * query).astype(bf16), ones))
        top_ref[0:16, :] = jnp.max(longest.reshape(-1, 16, HD), 0).astype(bf16)
    else:
        top_ref[...] = top_in_ref[...]
    values[:, HD:] = jnp.ones((values.shape[0], HD), bf16)
    filled = fill(block_refs, numbers_of(mine))
    sums[...] = jnp.zeros_like(sums)

    def visit(start, count):
        at = pl.ds(pl.multiple_of(start, ROWS), count)
        block_keys = keys[at, :]
        block_values = values[at, :]
        for h in range(HEADS):
            for a in range(0, ROWS, TILE):
                scores = dot(query_ref[a : a + TILE, head(h)], block_keys, ((1,), (1,)))
                weights = jnp.exp2(scores * SCORE_SCALE).astype(bf16)
                sums[h, a : a + TILE, :] += dot(weights, block_values)

    def pair(n, _):
        visit(n * 2 * ROWS, 2 * ROWS)
        return 0

    lax.fori_loop(0, filled // 2, pair, 0)

    if first:

        @pl.when(filled % 2 == 1)
        def _():
            visit((filled - 1) * ROWS, ROWS)

        at_row = lax.broadcasted_iota(jnp.int32, (TILE, TILE), 0)
        at_column = lax.broadcasted_iota(jnp.int32, (TILE, TILE), 1)
        seen = at_column <= at_row
        values[:ROWS, :HD] = own_ref[:, HD:]
        for h in range(HEADS):
            for a in range(0, ROWS, TILE):
                for b in range(0, a + TILE, TILE):
                    scores = dot(query_ref[a : a + TILE, head(h)], own_ref[b : b + TILE, :HD], ((1,), (1,)))
                    weights = jnp.exp2(scores * SCORE_SCALE)
                    if a == b:
                        weights = jnp.where(seen, weights, 0.0)
                    sums[h, a : a + TILE, :] += dot(weights.astype(bf16), values[b : b + TILE, :])
            numerator_ref[:, head(h)] = sums[h, :, :HD]
            counted_ref[:, h : h + 1] = sums[h, :, HD : HD + 1]
    elif not last:
        for h in range(HEADS):
            numerator_ref[:, head(h)] = sums[h, :, :HD] + carry_ref[:, head(h)]
            counted_ref[:, h : h + 1] = sums[h, :, HD : HD + 1] + count_ref[:, h : h + 1]
    else:
        key_top = jnp.max(top_ref[16:32, :].astype(f32), 0, keepdims=True)
        bound = jnp.max(top_ref[0:16, :].astype(f32)) * jnp.sum(key_top * key_top) * SCORE_SCALE**2
        large = bound * 1.05 > SAFE_EXPONENT * SAFE_EXPONENT

        @pl.when(large)
        def _():
            before = fill(kept_refs + block_refs, kept_numbers_of(mine) + numbers_of(mine))
            at = pl.ds(pl.multiple_of(before * ROWS, ROWS), ROWS)
            keys[at, :] = own_ref[:, :HD]
            values[at, :HD] = own_ref[:, HD:]
            sums[...] = jnp.zeros_like(sums)
            tops[...] = jnp.full_like(tops, MASKED)

            def step(n, _):
                at = pl.ds(pl.multiple_of((n // (2 * HEADS)) * ROWS, ROWS), ROWS)
                h = (n % (2 * HEADS)) // 2
                a = (n % 2) * TILE
                rows = pl.ds(pl.multiple_of(a, TILE), TILE)
                query = query_ref[rows, pl.ds(pl.multiple_of(h * HD, HD), HD)]
                scores = dot(query, keys[at, :], ((1,), (1,))) * SCORE_SCALE
                row = lax.broadcasted_iota(jnp.int32, (TILE, ROWS), 0) + a
                column = lax.broadcasted_iota(jnp.int32, (TILE, ROWS), 1)
                column = column - jnp.where(n // (2 * HEADS) < before, ROWS, 0)
                visible = column <= row
                scores = jnp.where(visible, scores, MASKED)
                old = tops[h, rows, :]
                new = jnp.maximum(old[:, :1], jnp.max(scores, 1, keepdims=True))
                weights = jnp.where(visible, jnp.exp2(scores - new), 0.0).astype(bf16)
                sums[h, rows, :] = sums[h, rows, :] * jnp.exp2(old[:, :1] - new) + dot(weights, values[at, :])
                tops[h, rows, :] = jnp.broadcast_to(new, (TILE, HD))
                return 0

            lax.fori_loop(0, (before + 1) * 2 * HEADS, step, 0)

        squares = jnp.zeros((ROWS, HD), f32)
        for h in range(HEADS):
            count = sums[h, :, HD:] + jnp.where(large, 0.0, count_ref[:, h : h + 1])
            result = (sums[h, :, :HD] + jnp.where(large, 0.0, carry_ref[:, head(h)])) / count
            result = result.astype(bf16)
            out_ref[:, head(h)] = result
            result = result.astype(f32)
            squares = squares + result * result
        square_ref[...] = dot(jnp.ones((8, HD), f32), squares, ((1,), (1,)), highest)


def attend(mine, query, own, carry, blocks, numbers_of, kept=None, kept_numbers_of=None):
    first, last = carry is None, kept is not None
    kept = kept or []
    size = sum(block.shape[0] for block in blocks)
    size = 16 * ROWS if last else size
    operands = [query, own] + list(carry or []) + list(blocks) + kept
    top = (32, HD)
    scratch = [
        pltpu.VMEM((HEADS, ROWS, 2 * HD), f32),
        pltpu.VMEM((size, HD), bf16),
        pltpu.VMEM((size, 2 * HD), bf16),
    ]
    if last:
        out_shape = (
            jax.ShapeDtypeStruct((ROWS, HEADS * HD), bf16),
            jax.ShapeDtypeStruct((8, ROWS), f32),
        )
        scratch += [pltpu.VMEM(top, bf16), pltpu.VMEM((HEADS, ROWS, HD), f32)]
    else:
        out_shape = (
            jax.ShapeDtypeStruct((ROWS, HEADS * HD), f32),
            jax.ShapeDtypeStruct((ROWS, HD), f32),
            jax.ShapeDtypeStruct(top, bf16),
        )
    return pl.pallas_call(
        functools.partial(attend_kernel, first, last, numbers_of, len(blocks), kept_numbers_of, len(kept)),
        out_shape=out_shape,
        in_specs=[SMEM] + [VMEM] * len(operands),
        out_specs=(VMEM,) * len(out_shape),
        scratch_shapes=scratch,
        compiler_params=params(20),
        cost_estimate=cost(0.2),
        name="attend_first" if first else "attend_last" if last else "attend_middle",
    )(mine, *operands)


def carry_kernel(
    mine_ref,
    query_hbm,
    local_ref,
    grow_ref,
    kept_ref,
    handed_ref,
    chip_ref,
    core_ref,
    gain_ref,
    out_ref,
):
    mine = mine_ref[0]
    query_ref = query_hbm
    plane, side, core = mine // 4, (mine // 2) % 2, mine % 2
    kept, handed = state_of(kept_ref), state_of(handed_ref)

    def pick(one, two, wanted):
        states = [jnp.where(wanted, jnp.where(core == 0, a, b), 0.0) for a, b in zip(one[0], two[0])]
        return states, jnp.where(wanted, jnp.where(core == 0, one[1], two[1]), 0.0)

    entering = pick(handed, kept, plane >= 2)
    entering = follow(entering, pick(kept, handed, plane >= 1))
    entering = follow(entering, state_of(chip_ref, side == 1))
    entering = follow(entering, state_of(core_ref, core == 1))
    grow = grow_ref[...]
    for h in range(HEADS):
        state = entering[0][h]
        upper = state.astype(bf16)
        lower = (state - upper.astype(f32)).astype(bf16)
        both = dot(query_ref[:, head(h)], jnp.concatenate([upper, lower], 1))
        entered = both[:, :HD] + both[:, HD:]
        result = local_ref[:, head(h)] + entered * grow[:, h : h + 1]
        square = jnp.mean(result * result, -1, keepdims=True)
        out_ref[:, head(h)] = result * lax.rsqrt(square + EPS) * gain_ref[head(h)][None, :]


def finish_kernel(features, attention_ref, square_ref, other_ref, linear_ref, gain_ref, out_ref):
    factor = lax.rsqrt((square_ref[...] + other_ref[...]) / features + EPS)
    factor = dot(factor, jnp.full((8, HD), 0.125, f32), ((0,), (0,)), highest)
    for h in range(HEADS):
        part = attention_ref[:, head(h)].astype(f32) * factor * gain_ref[head(h)][None, :]
        out_ref[:, head(h)] = (part + linear_ref[:, head(h)]).astype(bf16)


def carry_in(place, lh_query, *operands):
    return pl.pallas_call(
        carry_kernel,
        out_shape=jax.ShapeDtypeStruct((ROWS, HEADS * HD), f32),
        in_specs=[SMEM, VMEM] + [VMEM] * len(operands),
        out_specs=VMEM,
        compiler_params=params(14),
        cost_estimate=cost(0.2),
        name="carry",
    )(place, lh_query, *operands)


def finish(features, *operands):
    return pl.pallas_call(
        functools.partial(finish_kernel, features),
        out_shape=jax.ShapeDtypeStruct((ROWS, HEADS * HD), bf16),
        in_specs=[VMEM] * len(operands),
        out_specs=VMEM,
        compiler_params=params(14),
        cost_estimate=cost(0.2),
        name="finish",
    )(*operands)


def body(att_query, att_key, att_value, lh_query, lh_key, lh_value, lh_step, att_gain, lh_gain):
    mine = lax.axis_index("ctx")
    place = mine.reshape(1).astype(jnp.int32)

    def move(value, pairs):
        return lax.ppermute(value, "ctx", pairs)

    every = range(16)
    sibling = [(i, i ^ 1) for i in every]
    sideways = [(i, i ^ 2) for i in every]
    last_plane = [(i, i + 4) for i in every if i % 2 == 0 and i < 12] + [(i, i + 12) for i in (1, 3)]
    plane_before = [(i, i + 8) for i in every if i % 2 == 1 and i < 8]

    def tied(*values):
        return lax.optimization_barrier(values)

    lh_query, lh_key, lh_value, far_query, att_key, att_value = [
        array
        for array in (lh_query, lh_key, lh_value, att_query, att_key, att_value)
    ]
    near_query = att_query
    lh_query, lh_key, lh_value = [
        pltpu.with_memory_space_constraint(array, pltpu.HBM) for array in (lh_query, lh_key, lh_value)
    ]
    own = beside(att_key, att_value)
    across = move(own, [(i, i ^ 2) for i in every if i < 4 or i % 4 < 2])
    near = move(own, sibling)
    chip = stack(own, near)
    chip, lh_step = tied(chip, lh_step)
    behind = move(chip, last_plane)

    local, grow, message = recur(lh_query, lh_key, lh_value, lh_step)
    chip, across, message = tied(chip, across, message)
    beyond = move(chip, plane_before)
    across_near = move(across, sibling)
    first = move(message, sibling)
    of_chip = join(1, place, message, first)
    other_chip = move(of_chip, sideways)
    behind, of_chip = tied(behind, of_chip)
    behind_near = move(behind, sibling)
    level = move(behind, [(i, j) for i, j in sideways if (i % 2 == 0 and i >= 4) or i >= 12])

    def where(number, wanted):
        return jnp.where(wanted, number, NEVER)

    def parts(mine):
        return mine // 4, (mine // 2) % 2, mine % 2, mine - mine % 2

    def brought(mine, core):
        plane, _, _, even = parts(mine)
        if core == 0:
            return where(even - 4, plane >= 1)
        return where(even - 12, plane == 3)

    def behind_numbers(mine):
        _, _, core, _ = parts(mine)
        zero, one = brought(mine, 0), brought(mine, 1)
        return [jnp.where(core == 0, zero, one), jnp.where(core == 0, one, zero)]

    def beyond_numbers(mine):
        plane, _, core, even = parts(mine)
        number = where(even - 8, plane >= 2)
        return [where(number, core == 1), where(number, core == 0)]

    def first_numbers(mine):
        _, side, core, even = parts(mine)
        near_numbers = [where(mine - 1, core == 1)] + [where(even - 2, side == 1)] * 2
        return near_numbers + behind_numbers(mine)

    def middle_numbers(mine):
        return behind_numbers(mine) + beyond_numbers(mine)

    first_blocks = [near, across, across_near, behind, behind_near]
    carry = attend(place, near_query, own, None, first_blocks, first_numbers)
    carry, other_chip, beyond, level = tied(carry, other_chip, beyond, level)
    level_beyond = move(beyond, [(i, j) for i, j in sideways if i % 2 == 1 and i >= 8])
    beyond_near = move(beyond, sibling)
    level_near = move(level, sibling)
    of_plane = join(2, place, of_chip, other_chip)
    state_behind = move(of_plane, last_plane)
    state_beyond = move(of_plane, plane_before)
    middle_blocks = [level, level_near, beyond, beyond_near]
    middle_blocks, of_plane = tied(middle_blocks, of_plane)
    carry = attend(place, near_query, own, carry, middle_blocks, middle_numbers)
    carry, level_beyond, state_behind, state_beyond = tied(carry, level_beyond, state_behind, state_beyond)
    level_beyond_near = move(level_beyond, sibling)
    kept = hand(place, state_behind, state_beyond)
    handed = move(kept, sibling)
    last_blocks = [level_beyond, level_beyond_near]
    last_blocks, kept = tied(last_blocks, kept)
    attention, squares = attend(
        place,
        near_query,
        own,
        carry,
        last_blocks,
        beyond_numbers,
        first_blocks + middle_blocks,
        lambda mine: first_numbers(mine) + middle_numbers(mine),
    )
    squares, handed = tied(squares, handed)
    linear = carry_in(place, lh_query, local, grow, kept, handed, other_chip, first, lh_gain)

    def over(value, bit):
        return lax.ppermute(value, "tp", [(i, i ^ bit) for i in range(8)])

    first_round = over(squares, 1)
    first_round, linear = tied(first_round, linear)
    squares = squares + first_round
    squares = squares + over(squares, 2)
    features = HEADS * HD * lax.axis_size("tp")
    return finish(float(features), attention, squares, over(squares, 4), linear, att_gain)


def solution(mesh):
    placed = (P("ctx", "tp"),) * 7 + (P("tp"), P("tp"))
    return jax.shard_map(body, mesh=mesh, in_specs=placed, out_specs=P("ctx", "tp"), check_vma=False)
```

```python
import functools
import math

import jax
import jax.numpy as jnp
from jax import lax
from jax.experimental import pallas as pl
from jax.experimental.pallas import tpu as pltpu
from jax.sharding import PartitionSpec as P

HD = 128
ROWS = 512
HEADS = 6
TILE = 256
EPS = 1e-06
MASKED = -1e30
LOG2E = math.log2(math.e)
SCORE_SCALE = LOG2E / math.sqrt(HD)
SAFE_EXPONENT = 100.0
STATE_ROWS = HEADS * HD + 8
NEVER = 1 << 20

VMEM = pl.BlockSpec(memory_space=pltpu.VMEM)
SMEM = pl.BlockSpec(memory_space=pltpu.SMEM)
f32 = jnp.float32
bf16 = jnp.bfloat16
highest = lax.Precision.HIGHEST


def dot(a, b, contract=((1,), (0,)), precision=None):
    return lax.dot_general(a, b, (contract, ((), ())), precision=precision, preferred_element_type=f32)


def params(megabytes):
    return pltpu.CompilerParams(vmem_limit_bytes=megabytes << 20)


def cost(us):
    return pl.CostEstimate(flops=int(us * 1e9), bytes_accessed=int(us * 1e6), transcendentals=int(us * 1e6))


def head(h):
    return slice(h * HD, (h + 1) * HD)


def recur_kernel(
    q_hbm, k_hbm, v_hbm, step_ref, local_ref, grow_ref, message_ref, padded
):
    k_ref, q_ref, v_ref = k_hbm, q_hbm, v_hbm
    padded[...] = jnp.full((8, ROWS), 0.5, f32)
    padded[:HEADS, :] = step_ref[...]
    step = padded[...]
    rate = step / (1.0 + step)
    total = -jnp.log(1.0 + step) * LOG2E
    place = lax.broadcasted_iota(jnp.int32, (8, ROWS), 1)
    reach = 1
    while reach < ROWS:
        total = total + jnp.where(place >= reach, pltpu.roll(total, reach, 1), 0.0)
        reach *= 2
    source = jnp.log(rate) * LOG2E - total
    end = total[:, ROWS - 1 : ROWS]
    tail = jnp.exp2(end + source)
    rows = jnp.concatenate([total, tail, jnp.zeros((HD - 16, ROWS), f32)], 0)
    columns = jnp.transpose(rows)
    grow_ref[...] = jnp.exp2(columns)
    message_ref[HEADS * HD :, :] = jnp.broadcast_to(end, (8, HD))
    at_row = lax.broadcasted_iota(jnp.int32, (TILE, TILE), 0)
    at_column = lax.broadcasted_iota(jnp.int32, (TILE, TILE), 1)
    seen = at_column <= at_row
    for h in range(HEADS):
        keys = k_ref[:, head(h)].astype(f32)
        keys = keys * lax.rsqrt(jnp.sum(keys * keys, -1, keepdims=True) + EPS)
        unit = keys.astype(bf16)
        values = v_ref[:, head(h)]
        for a in range(0, ROWS, TILE):
            result = None
            for b in range(0, a + TILE, TILE):
                scores = dot(q_ref[a : a + TILE, head(h)], unit[b : b + TILE], ((1,), (1,)))
                decay = jnp.exp2(columns[a : a + TILE, h : h + 1] + source[h : h + 1, b : b + TILE])
                weights = scores * decay
                if a == b:
                    weights = jnp.where(seen, weights, 0.0)
                part = dot(weights.astype(bf16), values[b : b + TILE])
                result = part if result is None else result + part
            local_ref[a : a + TILE, head(h)] = result
        tailed = (values.astype(f32) * columns[:, 8 + h : 9 + h]).astype(bf16)
        message_ref[head(h), :] = dot(unit, tailed, ((0,), (0,)))


def recur(lh_query, lh_key, lh_value, lh_step):
    return pl.pallas_call(
        recur_kernel,
        out_shape=(
            jax.ShapeDtypeStruct((ROWS, HEADS * HD), f32),
            jax.ShapeDtypeStruct((ROWS, HD), f32),
            jax.ShapeDtypeStruct((STATE_ROWS, HD), f32),
        ),
        in_specs=[VMEM] * 4,
        out_specs=(VMEM,) * 3,
        scratch_shapes=[pltpu.VMEM((8, ROWS), f32)]
,
        compiler_params=params(16),
        cost_estimate=cost(0.2),
        name="recur",
    )(lh_query, lh_key, lh_value, lh_step.T)


def beside_kernel(key_ref, value_ref, out_ref):
    out_ref[:, :HD] = key_ref[...]
    out_ref[:, HD:] = value_ref[...]


def beside(key, value):
    return pl.pallas_call(
        beside_kernel,
        out_shape=jax.ShapeDtypeStruct((ROWS, 2 * HD), bf16),
        in_specs=[VMEM, VMEM],
        out_specs=VMEM,
        compiler_params=params(14),
        name="beside",
    )(key, value)


def stack_kernel(one_ref, two_ref, out_ref):
    out_ref[:ROWS, :] = one_ref[...]
    out_ref[ROWS:, :] = two_ref[...]


def stack(one, two):
    return pl.pallas_call(
        stack_kernel,
        out_shape=jax.ShapeDtypeStruct((2 * ROWS, 2 * HD), bf16),
        in_specs=[VMEM, VMEM],
        out_specs=VMEM,
        compiler_params=params(14),
        name="stack",
    )(one, two)


def follow(early, late):
    logs = early[1] + late[1]
    states = [jnp.exp2(late[1][h : h + 1, :]) * early[0][h] + late[0][h] for h in range(HEADS)]
    return states, logs


def state_of(ref, wanted=None):
    states = [ref[head(h), :] for h in range(HEADS)]
    logs = ref[HEADS * HD :, :]
    if wanted is None:
        return states, logs
    return [jnp.where(wanted, state, 0.0) for state in states], jnp.where(wanted, logs, 0.0)


def put_state(ref, value):
    for h in range(HEADS):
        ref[head(h), :] = value[0][h]
    ref[HEADS * HD :, :] = value[1]


def join_kernel(bit, mine_ref, own_ref, other_ref, out_ref):
    own_first = (mine_ref[0] // bit) % 2 == 0
    own, other = state_of(own_ref), state_of(other_ref)

    def pick(one, two):
        return [jnp.where(own_first, a, b) for a, b in zip(one[0], two[0])], jnp.where(own_first, one[1], two[1])

    put_state(out_ref, follow(pick(own, other), pick(other, own)))


def join(bit, mine, own, other):
    return pl.pallas_call(
        functools.partial(join_kernel, bit),
        out_shape=jax.ShapeDtypeStruct((STATE_ROWS, HD), f32),
        in_specs=[SMEM, VMEM, VMEM],
        out_specs=VMEM,
        compiler_params=params(14),
        cost_estimate=cost(0.2),
        name="join",
    )(mine, own, other)


def hand_kernel(mine_ref, behind_ref, beyond_ref, out_ref):
    plane, core = mine_ref[0] // 4, mine_ref[0] % 2
    behind = state_of(behind_ref, (plane == 3) | (core == 0))
    beyond = state_of(beyond_ref, (plane >= 2) & (core == 1))
    put_state(out_ref, follow(behind, beyond))


def hand(mine, behind, beyond):
    return pl.pallas_call(
        hand_kernel,
        out_shape=jax.ShapeDtypeStruct((STATE_ROWS, HD), f32),
        in_specs=[SMEM, VMEM, VMEM],
        out_specs=VMEM,
        compiler_params=params(14),
        cost_estimate=cost(0.2),
        name="hand",
    )(mine, behind, beyond)


def attend_kernel(first, last, numbers_of, buffers, kept_numbers_of, kept, mine_ref, query_ref, own_ref, *refs):
    mine = mine_ref[0]
    refs = list(refs)

    def take(count):
        return [refs.pop(0) for _ in range(count)]

    if not first:
        carry_ref, count_ref, top_in_ref = take(3)
    block_refs = take(buffers)
    kept_refs = take(kept)
    if last:
        out_ref, square_ref, sums, keys, values, top_ref, tops = refs
    else:
        numerator_ref, counted_ref, top_ref, sums, keys, values = refs

    def highest_of(part):
        return jnp.max(jnp.abs(part).reshape(-1, 16, HD), 0)

    def fill(blocks, numbers):
        filled = jnp.int32(0)
        for block, number in zip(blocks, numbers):
            rows = block.shape[0]
            takes = number < mine
            place = filled

            @pl.when(takes)
            def _():
                at = pl.ds(pl.multiple_of(place * ROWS, ROWS), rows)
                keys[at, :] = block[:, :HD]
                values[at, :HD] = block[:, HD:]
                top_ref[16:32, :] = jnp.maximum(top_ref[16:32, :], highest_of(block[:, :HD]))

            filled = filled + jnp.where(takes, rows // ROWS, 0)
        return filled

    if first:
        top_ref[16:32, :] = highest_of(own_ref[:, :HD])
        longest = jnp.zeros((ROWS, HD), f32)
        ones = jnp.ones((HD, HD), bf16)
        for h in range(HEADS):
            query = query_ref[:, head(h)].astype(f32)
            longest = jnp.maximum(longest, dot((query * query).astype(bf16), ones))
        top_ref[0:16, :] = jnp.max(longest.reshape(-1, 16, HD), 0).astype(bf16)
    else:
        top_ref[...] = top_in_ref[...]
    values[:, HD:] = jnp.ones((values.shape[0], HD), bf16)
    filled = fill(block_refs, numbers_of(mine))
    sums[...] = jnp.zeros_like(sums)

    def visit(start, count):
        at = pl.ds(pl.multiple_of(start, ROWS), count)
        block_keys = keys[at, :]
        block_values = values[at, :]
        for h in range(HEADS):
            for a in range(0, ROWS, TILE):
                scores = dot(query_ref[a : a + TILE, head(h)], block_keys, ((1,), (1,)))
                weights = jnp.exp2(scores * SCORE_SCALE).astype(bf16)
                sums[h, a : a + TILE, :] += dot(weights, block_values)

    def pair(n, _):
        visit(n * 2 * ROWS, 2 * ROWS)
        return 0

    lax.fori_loop(0, filled // 2, pair, 0)

    if first:

        @pl.when(filled % 2 == 1)
        def _():
            visit((filled - 1) * ROWS, ROWS)

        at_row = lax.broadcasted_iota(jnp.int32, (TILE, TILE), 0)
        at_column = lax.broadcasted_iota(jnp.int32, (TILE, TILE), 1)
        seen = at_column <= at_row
        values[:ROWS, :HD] = own_ref[:, HD:]
        for h in range(HEADS):
            for a in range(0, ROWS, TILE):
                for b in range(0, a + TILE, TILE):
                    scores = dot(query_ref[a : a + TILE, head(h)], own_ref[b : b + TILE, :HD], ((1,), (1,)))
                    weights = jnp.exp2(scores * SCORE_SCALE)
                    if a == b:
                        weights = jnp.where(seen, weights, 0.0)
                    sums[h, a : a + TILE, :] += dot(weights.astype(bf16), values[b : b + TILE, :])
            numerator_ref[:, head(h)] = sums[h, :, :HD]
            counted_ref[:, h : h + 1] = sums[h, :, HD : HD + 1]
    elif not last:
        for h in range(HEADS):
            numerator_ref[:, head(h)] = sums[h, :, :HD] + carry_ref[:, head(h)]
            counted_ref[:, h : h + 1] = sums[h, :, HD : HD + 1] + count_ref[:, h : h + 1]
    else:
        key_top = jnp.max(top_ref[16:32, :].astype(f32), 0, keepdims=True)
        bound = jnp.max(top_ref[0:16, :].astype(f32)) * jnp.sum(key_top * key_top) * SCORE_SCALE**2
        large = bound * 1.05 > SAFE_EXPONENT * SAFE_EXPONENT

        @pl.when(large)
        def _():
            before = fill(kept_refs + block_refs, kept_numbers_of(mine) + numbers_of(mine))
            at = pl.ds(pl.multiple_of(before * ROWS, ROWS), ROWS)
            keys[at, :] = own_ref[:, :HD]
            values[at, :HD] = own_ref[:, HD:]
            sums[...] = jnp.zeros_like(sums)
            tops[...] = jnp.full_like(tops, MASKED)

            def step(n, _):
                at = pl.ds(pl.multiple_of((n // (2 * HEADS)) * ROWS, ROWS), ROWS)
                h = (n % (2 * HEADS)) // 2
                a = (n % 2) * TILE
                rows = pl.ds(pl.multiple_of(a, TILE), TILE)
                query = query_ref[rows, pl.ds(pl.multiple_of(h * HD, HD), HD)]
                scores = dot(query, keys[at, :], ((1,), (1,))) * SCORE_SCALE
                row = lax.broadcasted_iota(jnp.int32, (TILE, ROWS), 0) + a
                column = lax.broadcasted_iota(jnp.int32, (TILE, ROWS), 1)
                column = column - jnp.where(n // (2 * HEADS) < before, ROWS, 0)
                visible = column <= row
                scores = jnp.where(visible, scores, MASKED)
                old = tops[h, rows, :]
                new = jnp.maximum(old[:, :1], jnp.max(scores, 1, keepdims=True))
                weights = jnp.where(visible, jnp.exp2(scores - new), 0.0).astype(bf16)
                sums[h, rows, :] = sums[h, rows, :] * jnp.exp2(old[:, :1] - new) + dot(weights, values[at, :])
                tops[h, rows, :] = jnp.broadcast_to(new, (TILE, HD))
                return 0

            lax.fori_loop(0, (before + 1) * 2 * HEADS, step, 0)

        squares = jnp.zeros((ROWS, HD), f32)
        for h in range(HEADS):
            count = sums[h, :, HD:] + jnp.where(large, 0.0, count_ref[:, h : h + 1])
            result = (sums[h, :, :HD] + jnp.where(large, 0.0, carry_ref[:, head(h)])) / count
            result = result.astype(bf16)
            out_ref[:, head(h)] = result
            result = result.astype(f32)
            squares = squares + result * result
        square_ref[...] = dot(jnp.ones((8, HD), f32), squares, ((1,), (1,)), highest)


def attend(mine, query, own, carry, blocks, numbers_of, kept=None, kept_numbers_of=None):
    first, last = carry is None, kept is not None
    kept = kept or []
    size = sum(block.shape[0] for block in blocks)
    size = 16 * ROWS if last else size
    operands = [query, own] + list(carry or []) + list(blocks) + kept
    top = (32, HD)
    scratch = [
        pltpu.VMEM((HEADS, ROWS, 2 * HD), f32),
        pltpu.VMEM((size, HD), bf16),
        pltpu.VMEM((size, 2 * HD), bf16),
    ]
    if last:
        out_shape = (
            jax.ShapeDtypeStruct((ROWS, HEADS * HD), bf16),
            jax.ShapeDtypeStruct((8, ROWS), f32),
        )
        scratch += [pltpu.VMEM(top, bf16), pltpu.VMEM((HEADS, ROWS, HD), f32)]
    else:
        out_shape = (
            jax.ShapeDtypeStruct((ROWS, HEADS * HD), f32),
            jax.ShapeDtypeStruct((ROWS, HD), f32),
            jax.ShapeDtypeStruct(top, bf16),
        )
    return pl.pallas_call(
        functools.partial(attend_kernel, first, last, numbers_of, len(blocks), kept_numbers_of, len(kept)),
        out_shape=out_shape,
        in_specs=[SMEM] + [VMEM] * len(operands),
        out_specs=(VMEM,) * len(out_shape),
        scratch_shapes=scratch,
        compiler_params=params(20),
        cost_estimate=cost(0.2),
        name="attend_first" if first else "attend_last" if last else "attend_middle",
    )(mine, *operands)


def carry_kernel(
    mine_ref,
    query_hbm,
    local_ref,
    grow_ref,
    kept_ref,
    handed_ref,
    chip_ref,
    core_ref,
    gain_ref,
    out_ref,
):
    mine = mine_ref[0]
    query_ref = query_hbm
    plane, side, core = mine // 4, (mine // 2) % 2, mine % 2
    kept, handed = state_of(kept_ref), state_of(handed_ref)

    def pick(one, two, wanted):
        states = [jnp.where(wanted, jnp.where(core == 0, a, b), 0.0) for a, b in zip(one[0], two[0])]
        return states, jnp.where(wanted, jnp.where(core == 0, one[1], two[1]), 0.0)

    entering = pick(handed, kept, plane >= 2)
    entering = follow(entering, pick(kept, handed, plane >= 1))
    entering = follow(entering, state_of(chip_ref, side == 1))
    entering = follow(entering, state_of(core_ref, core == 1))
    grow = grow_ref[...]
    for h in range(HEADS):
        state = entering[0][h]
        upper = state.astype(bf16)
        lower = (state - upper.astype(f32)).astype(bf16)
        both = dot(query_ref[:, head(h)], jnp.concatenate([upper, lower], 1))
        entered = both[:, :HD] + both[:, HD:]
        result = local_ref[:, head(h)] + entered * grow[:, h : h + 1]
        square = jnp.mean(result * result, -1, keepdims=True)
        out_ref[:, head(h)] = result * lax.rsqrt(square + EPS) * gain_ref[head(h)][None, :]


def finish_kernel(features, attention_ref, square_ref, other_ref, linear_ref, gain_ref, out_ref):
    factor = lax.rsqrt((square_ref[...] + other_ref[...]) / features + EPS)
    factor = dot(factor, jnp.full((8, HD), 0.125, f32), ((0,), (0,)), highest)
    for h in range(HEADS):
        part = attention_ref[:, head(h)].astype(f32) * factor * gain_ref[head(h)][None, :]
        out_ref[:, head(h)] = (part + linear_ref[:, head(h)]).astype(bf16)


def carry_in(place, lh_query, *operands):
    return pl.pallas_call(
        carry_kernel,
        out_shape=jax.ShapeDtypeStruct((ROWS, HEADS * HD), f32),
        in_specs=[SMEM, VMEM] + [VMEM] * len(operands),
        out_specs=VMEM,
        compiler_params=params(14),
        cost_estimate=cost(0.2),
        name="carry",
    )(place, lh_query, *operands)


def finish(features, *operands):
    return pl.pallas_call(
        functools.partial(finish_kernel, features),
        out_shape=jax.ShapeDtypeStruct((ROWS, HEADS * HD), bf16),
        in_specs=[VMEM] * len(operands),
        out_specs=VMEM,
        compiler_params=params(14),
        cost_estimate=cost(0.2),
        name="finish",
    )(*operands)


def body(att_query, att_key, att_value, lh_query, lh_key, lh_value, lh_step, att_gain, lh_gain):
    mine = lax.axis_index("ctx")
    place = mine.reshape(1).astype(jnp.int32)

    def move(value, pairs):
        return lax.ppermute(value, "ctx", pairs)

    every = range(16)
    sibling = [(i, i ^ 1) for i in every]
    sideways = [(i, i ^ 2) for i in every]
    last_plane = [(i, i + 4) for i in every if i % 2 == 0 and i < 12] + [(i, i + 12) for i in (1, 3)]
    plane_before = [(i, i + 8) for i in every if i % 2 == 1 and i < 8]

    def tied(*values):
        return lax.optimization_barrier(values)

    lh_query, lh_key, lh_value, far_query, att_key, att_value = [
        array
        for array in (lh_query, lh_key, lh_value, att_query, att_key, att_value)
    ]
    near_query = att_query
    lh_query, lh_key, lh_value, att_key, att_value = [
        pltpu.with_memory_space_constraint(array, pltpu.HBM)
        for array in (lh_query, lh_key, lh_value, att_key, att_value)
    ]
    own = beside(att_key, att_value)
    across = move(own, [(i, i ^ 2) for i in every if i < 4 or i % 4 < 2])
    near = move(own, sibling)
    chip = stack(own, near)
    chip, lh_step = tied(chip, lh_step)
    behind = move(chip, last_plane)

    local, grow, message = recur(lh_query, lh_key, lh_value, lh_step)
    chip, across, behind, message = tied(chip, across, behind, message)
    beyond = move(chip, plane_before)
    across_near = move(across, sibling)
    first = move(message, sibling)
    behind_near = move(behind, sibling)
    level = move(behind, [(i, j) for i, j in sideways if (i % 2 == 0 and i >= 4) or i >= 12])

    def where(number, wanted):
        return jnp.where(wanted, number, NEVER)

    def parts(mine):
        return mine // 4, (mine // 2) % 2, mine % 2, mine - mine % 2

    def brought(mine, core):
        plane, _, _, even = parts(mine)
        if core == 0:
            return where(even - 4, plane >= 1)
        return where(even - 12, plane == 3)

    def behind_numbers(mine):
        _, _, core, _ = parts(mine)
        zero, one = brought(mine, 0), brought(mine, 1)
        return [jnp.where(core == 0, zero, one), jnp.where(core == 0, one, zero)]

    def beyond_numbers(mine):
        plane, _, core, even = parts(mine)
        number = where(even - 8, plane >= 2)
        return [where(number, core == 1), where(number, core == 0)]

    def first_numbers(mine):
        _, side, core, even = parts(mine)
        near_numbers = [where(mine - 1, core == 1)] + [where(even - 2, side == 1)] * 2
        return near_numbers + behind_numbers(mine)

    def middle_numbers(mine):
        return behind_numbers(mine) + beyond_numbers(mine)

    first_blocks = [near, across, across_near, behind, behind_near]
    carry = attend(place, near_query, own, None, first_blocks, first_numbers)
    carry, first, beyond, level = tied(carry, first, beyond, level)
    of_chip = join(1, place, message, first)
    other_chip = move(of_chip, sideways)
    level_beyond = move(beyond, [(i, j) for i, j in sideways if i % 2 == 1 and i >= 8])
    beyond_near = move(beyond, sibling)
    level_near = move(level, sibling)
    middle_blocks = [level, level_near, beyond, beyond_near]
    middle_blocks, of_chip = tied(middle_blocks, of_chip)
    carry = attend(place, near_query, own, carry, middle_blocks, middle_numbers)
    carry, level_beyond, other_chip = tied(carry, level_beyond, other_chip)
    level_beyond_near = move(level_beyond, sibling)
    of_plane = join(2, place, of_chip, other_chip)
    state_behind = move(of_plane, last_plane)
    state_beyond = move(of_plane, plane_before)
    last_blocks = [level_beyond, level_beyond_near]
    last_blocks, of_plane = tied(last_blocks, of_plane)
    attention, squares = attend(
        place,
        near_query,
        own,
        carry,
        last_blocks,
        beyond_numbers,
        first_blocks + middle_blocks,
        lambda mine: first_numbers(mine) + middle_numbers(mine),
    )

    def over(value, bit):
        return lax.ppermute(value, "tp", [(i, i ^ bit) for i in range(8)])

    squares, state_behind, state_beyond = tied(squares, state_behind, state_beyond)
    others = [over(squares, bit) for bit in (2, 4, 6)]
    kept = hand(place, state_behind, state_beyond)
    handed = move(kept, sibling)
    linear = carry_in(place, lh_query, local, grow, kept, handed, other_chip, first, lh_gain)
    others, linear = tied(others, linear)
    squares = squares + others[0] + others[1] + others[2]
    features = HEADS * HD * lax.axis_size("tp")
    return finish(float(features), attention, squares, over(squares, 1), linear, att_gain)


def solution(mesh):
    placed = (P("ctx", "tp"),) * 7 + (P("tp"), P("tp"))
    return jax.shard_map(body, mesh=mesh, in_specs=placed, out_specs=P("ctx", "tp"), check_vma=False)
```

```python
import functools
import math

import jax
import jax.numpy as jnp
from jax import lax
from jax.experimental import pallas as pl
from jax.experimental.pallas import tpu as pltpu
from jax.sharding import PartitionSpec as P

HD = 128
ROWS = 512
HEADS = 6
TILE = 256
EPS = 1e-06
MASKED = -1e30
LOG2E = math.log2(math.e)
SCORE_SCALE = LOG2E / math.sqrt(HD)
SAFE_EXPONENT = 100.0
STATE_ROWS = HEADS * HD + 8
NEVER = 1 << 20

VMEM = pl.BlockSpec(memory_space=pltpu.VMEM)
SMEM = pl.BlockSpec(memory_space=pltpu.SMEM)
f32 = jnp.float32
bf16 = jnp.bfloat16
highest = lax.Precision.HIGHEST


def dot(a, b, contract=((1,), (0,)), precision=None):
    return lax.dot_general(a, b, (contract, ((), ())), precision=precision, preferred_element_type=f32)


def params(megabytes):
    return pltpu.CompilerParams(vmem_limit_bytes=megabytes << 20)


def cost(us):
    return pl.CostEstimate(flops=int(us * 1e9), bytes_accessed=int(us * 1e6), transcendentals=int(us * 1e6))


def head(h):
    return slice(h * HD, (h + 1) * HD)


def recur_kernel(
    q_hbm, k_hbm, v_hbm, step_ref, local_ref, grow_ref, message_ref, padded
):
    k_ref, q_ref, v_ref = k_hbm, q_hbm, v_hbm
    padded[...] = jnp.full((8, ROWS), 0.5, f32)
    padded[:HEADS, :] = step_ref[...]
    step = padded[...]
    rate = step / (1.0 + step)
    total = -jnp.log(1.0 + step) * LOG2E
    place = lax.broadcasted_iota(jnp.int32, (8, ROWS), 1)
    reach = 1
    while reach < ROWS:
        total = total + jnp.where(place >= reach, pltpu.roll(total, reach, 1), 0.0)
        reach *= 2
    source = jnp.log(rate) * LOG2E - total
    end = total[:, ROWS - 1 : ROWS]
    tail = jnp.exp2(end + source)
    rows = jnp.concatenate([total, tail, jnp.zeros((HD - 16, ROWS), f32)], 0)
    columns = jnp.transpose(rows)
    grow_ref[...] = jnp.exp2(columns)
    message_ref[HEADS * HD :, :] = jnp.broadcast_to(end, (8, HD))
    at_row = lax.broadcasted_iota(jnp.int32, (TILE, TILE), 0)
    at_column = lax.broadcasted_iota(jnp.int32, (TILE, TILE), 1)
    seen = at_column <= at_row
    for h in range(HEADS):
        keys = k_ref[:, head(h)].astype(f32)
        keys = keys * lax.rsqrt(jnp.sum(keys * keys, -1, keepdims=True) + EPS)
        unit = keys.astype(bf16)
        values = v_ref[:, head(h)]
        for a in range(0, ROWS, TILE):
            result = None
            for b in range(0, a + TILE, TILE):
                scores = dot(q_ref[a : a + TILE, head(h)], unit[b : b + TILE], ((1,), (1,)))
                decay = jnp.exp2(columns[a : a + TILE, h : h + 1] + source[h : h + 1, b : b + TILE])
                weights = scores * decay
                if a == b:
                    weights = jnp.where(seen, weights, 0.0)
                part = dot(weights.astype(bf16), values[b : b + TILE])
                result = part if result is None else result + part
            local_ref[a : a + TILE, head(h)] = result
        tailed = (values.astype(f32) * columns[:, 8 + h : 9 + h]).astype(bf16)
        message_ref[head(h), :] = dot(unit, tailed, ((0,), (0,)))


def recur(lh_query, lh_key, lh_value, lh_step):
    return pl.pallas_call(
        recur_kernel,
        out_shape=(
            jax.ShapeDtypeStruct((ROWS, HEADS * HD), f32),
            jax.ShapeDtypeStruct((ROWS, HD), f32),
            jax.ShapeDtypeStruct((STATE_ROWS, HD), f32),
        ),
        in_specs=[VMEM] * 4,
        out_specs=(VMEM,) * 3,
        scratch_shapes=[pltpu.VMEM((8, ROWS), f32)]
,
        compiler_params=params(16),
        cost_estimate=cost(0.2),
        name="recur",
    )(lh_query, lh_key, lh_value, lh_step)


def beside_kernel(key_ref, value_ref, out_ref):
    out_ref[:, :HD] = key_ref[...]
    out_ref[:, HD:] = value_ref[...]


def beside(key, value):
    return pl.pallas_call(
        beside_kernel,
        out_shape=jax.ShapeDtypeStruct((ROWS, 2 * HD), bf16),
        in_specs=[VMEM, VMEM],
        out_specs=VMEM,
        compiler_params=params(14),
        name="beside",
    )(key, value)


def stack_kernel(one_ref, two_ref, out_ref):
    out_ref[:ROWS, :] = one_ref[...]
    out_ref[ROWS:, :] = two_ref[...]


def stack(one, two):
    return pl.pallas_call(
        stack_kernel,
        out_shape=jax.ShapeDtypeStruct((2 * ROWS, 2 * HD), bf16),
        in_specs=[VMEM, VMEM],
        out_specs=VMEM,
        compiler_params=params(14),
        name="stack",
    )(one, two)


def follow(early, late):
    logs = early[1] + late[1]
    states = [jnp.exp2(late[1][h : h + 1, :]) * early[0][h] + late[0][h] for h in range(HEADS)]
    return states, logs


def state_of(ref, wanted=None):
    states = [ref[head(h), :] for h in range(HEADS)]
    logs = ref[HEADS * HD :, :]
    if wanted is None:
        return states, logs
    return [jnp.where(wanted, state, 0.0) for state in states], jnp.where(wanted, logs, 0.0)


def put_state(ref, value):
    for h in range(HEADS):
        ref[head(h), :] = value[0][h]
    ref[HEADS * HD :, :] = value[1]


def join_cores_kernel(mine_ref, own_ref, other_ref, out_ref):
    own, other = state_of(own_ref), state_of(other_ref)
    put_state(out_ref, follow_in_order(mine_ref[0] % 2 == 0, own, other))


def join_sides_kernel(mine_ref, own_ref, even_ref, odd_ref, out_ref, other_ref):
    mine = mine_ref[0]
    own, even, odd = state_of(own_ref), state_of(even_ref), state_of(odd_ref)
    other = select(mine % 2 == 0, even, odd)
    put_state(other_ref, other)
    put_state(out_ref, follow_in_order((mine // 2) % 2 == 0, own, other))


def select(wanted, one, two):
    return [jnp.where(wanted, a, b) for a, b in zip(one[0], two[0])], jnp.where(wanted, one[1], two[1])


def follow_in_order(own_first, own, other):
    return follow(select(own_first, own, other), select(own_first, other, own))


def join(kernel, outputs, mine, *messages):
    return pl.pallas_call(
        kernel,
        out_shape=(jax.ShapeDtypeStruct((STATE_ROWS, HD), f32),) * outputs,
        in_specs=[SMEM] + [VMEM] * len(messages),
        out_specs=(VMEM,) * outputs,
        compiler_params=params(14),
        cost_estimate=cost(0.2),
        name="join",
    )(mine, *messages)


def hand_kernel(mine_ref, behind_ref, beyond_ref, out_ref):
    plane, core = mine_ref[0] // 4, mine_ref[0] % 2
    behind = state_of(behind_ref, (plane == 3) | (core == 0))
    beyond = state_of(beyond_ref, (plane >= 2) & (core == 1))
    put_state(out_ref, follow(behind, beyond))


def hand(mine, behind, beyond):
    return pl.pallas_call(
        hand_kernel,
        out_shape=jax.ShapeDtypeStruct((STATE_ROWS, HD), f32),
        in_specs=[SMEM, VMEM, VMEM],
        out_specs=VMEM,
        compiler_params=params(14),
        cost_estimate=cost(0.2),
        name="hand",
    )(mine, behind, beyond)


def attend_kernel(first, last, numbers_of, buffers, kept_numbers_of, kept, mine_ref, query_ref, own_ref, *refs):
    mine = mine_ref[0]
    refs = list(refs)

    def take(count):
        return [refs.pop(0) for _ in range(count)]

    if not first:
        carry_ref, count_ref, top_in_ref = take(3)
    block_refs = take(buffers)
    kept_refs = take(kept)
    if last:
        out_ref, square_ref, sums, keys, values, top_ref, tops = refs
    else:
        if first:
            (passed_ref,) = take(1)
            passed_ref[...] = query_ref[...]
        numerator_ref, counted_ref, top_ref, sums, keys, values = refs

    def highest_of(part):
        return jnp.max(jnp.abs(part).reshape(-1, 16, HD), 0)

    def fill(blocks, numbers):
        filled = jnp.int32(0)
        for block, number in zip(blocks, numbers):
            rows = block.shape[0]
            takes = number < mine
            place = filled

            @pl.when(takes)
            def _():
                at = pl.ds(pl.multiple_of(place * ROWS, ROWS), rows)
                keys[at, :] = block[:, :HD]
                values[at, :HD] = block[:, HD:]
                top_ref[16:32, :] = jnp.maximum(top_ref[16:32, :], highest_of(block[:, :HD]))

            filled = filled + jnp.where(takes, rows // ROWS, 0)
        return filled

    if first:
        top_ref[16:32, :] = highest_of(own_ref[:, :HD])
        longest = jnp.zeros((ROWS, HD), f32)
        ones = jnp.ones((HD, HD), bf16)
        for h in range(HEADS):
            query = query_ref[:, head(h)].astype(f32)
            longest = jnp.maximum(longest, dot((query * query).astype(bf16), ones))
        top_ref[0:16, :] = jnp.max(longest.reshape(-1, 16, HD), 0).astype(bf16)
    else:
        top_ref[...] = top_in_ref[...]
    values[:, HD:] = jnp.ones((values.shape[0], HD), bf16)
    filled = fill(block_refs, numbers_of(mine))
    sums[...] = jnp.zeros_like(sums)

    def visit(start, count):
        at = pl.ds(pl.multiple_of(start, ROWS), count)
        block_keys = keys[at, :]
        block_values = values[at, :]
        for h in range(HEADS):
            for a in range(0, ROWS, TILE):
                scores = dot(query_ref[a : a + TILE, head(h)], block_keys, ((1,), (1,)))
                weights = jnp.exp2(scores * SCORE_SCALE).astype(bf16)
                sums[h, a : a + TILE, :] += dot(weights, block_values)

    def pair(n, _):
        visit(n * 2 * ROWS, 2 * ROWS)
        return 0

    lax.fori_loop(0, filled // 2, pair, 0)

    if first:

        @pl.when(filled % 2 == 1)
        def _():
            visit((filled - 1) * ROWS, ROWS)

        at_row = lax.broadcasted_iota(jnp.int32, (TILE, TILE), 0)
        at_column = lax.broadcasted_iota(jnp.int32, (TILE, TILE), 1)
        seen = at_column <= at_row
        values[:ROWS, :HD] = own_ref[:, HD:]
        for h in range(HEADS):
            for a in range(0, ROWS, TILE):
                for b in range(0, a + TILE, TILE):
                    scores = dot(query_ref[a : a + TILE, head(h)], own_ref[b : b + TILE, :HD], ((1,), (1,)))
                    weights = jnp.exp2(scores * SCORE_SCALE)
                    if a == b:
                        weights = jnp.where(seen, weights, 0.0)
                    sums[h, a : a + TILE, :] += dot(weights.astype(bf16), values[b : b + TILE, :])
            numerator_ref[:, head(h)] = sums[h, :, :HD]
            counted_ref[:, h : h + 1] = sums[h, :, HD : HD + 1]
    elif not last:
        for h in range(HEADS):
            numerator_ref[:, head(h)] = sums[h, :, :HD] + carry_ref[:, head(h)]
            counted_ref[:, h : h + 1] = sums[h, :, HD : HD + 1] + count_ref[:, h : h + 1]
    else:
        key_top = jnp.max(top_ref[16:32, :].astype(f32), 0, keepdims=True)
        bound = jnp.max(top_ref[0:16, :].astype(f32)) * jnp.sum(key_top * key_top) * SCORE_SCALE**2
        large = bound * 1.05 > SAFE_EXPONENT * SAFE_EXPONENT

        @pl.when(large)
        def _():
            before = fill(kept_refs + block_refs, kept_numbers_of(mine) + numbers_of(mine))
            at = pl.ds(pl.multiple_of(before * ROWS, ROWS), ROWS)
            keys[at, :] = own_ref[:, :HD]
            values[at, :HD] = own_ref[:, HD:]
            sums[...] = jnp.zeros_like(sums)
            tops[...] = jnp.full_like(tops, MASKED)

            def step(n, _):
                at = pl.ds(pl.multiple_of((n // (2 * HEADS)) * ROWS, ROWS), ROWS)
                h = (n % (2 * HEADS)) // 2
                a = (n % 2) * TILE
                rows = pl.ds(pl.multiple_of(a, TILE), TILE)
                query = query_ref[rows, pl.ds(pl.multiple_of(h * HD, HD), HD)]
                scores = dot(query, keys[at, :], ((1,), (1,))) * SCORE_SCALE
                row = lax.broadcasted_iota(jnp.int32, (TILE, ROWS), 0) + a
                column = lax.broadcasted_iota(jnp.int32, (TILE, ROWS), 1)
                column = column - jnp.where(n // (2 * HEADS) < before, ROWS, 0)
                visible = column <= row
                scores = jnp.where(visible, scores, MASKED)
                old = tops[h, rows, :]
                new = jnp.maximum(old[:, :1], jnp.max(scores, 1, keepdims=True))
                weights = jnp.where(visible, jnp.exp2(scores - new), 0.0).astype(bf16)
                sums[h, rows, :] = sums[h, rows, :] * jnp.exp2(old[:, :1] - new) + dot(weights, values[at, :])
                tops[h, rows, :] = jnp.broadcast_to(new, (TILE, HD))
                return 0

            lax.fori_loop(0, (before + 1) * 2 * HEADS, step, 0)

        squares = jnp.zeros((ROWS, HD), f32)
        for h in range(HEADS):
            count = sums[h, :, HD:] + jnp.where(large, 0.0, count_ref[:, h : h + 1])
            result = (sums[h, :, :HD] + jnp.where(large, 0.0, carry_ref[:, head(h)])) / count
            result = result.astype(bf16)
            out_ref[:, head(h)] = result
            result = result.astype(f32)
            squares = squares + result * result
        square_ref[...] = dot(jnp.ones((8, HD), f32), squares, ((1,), (1,)), highest)


def attend(mine, query, own, carry, blocks, numbers_of, kept=None, kept_numbers_of=None):
    first, last = carry is None, kept is not None
    kept = kept or []
    size = sum(block.shape[0] for block in blocks)
    size = 16 * ROWS if last else size
    operands = [query, own] + list(carry or []) + list(blocks) + kept
    top = (32, HD)
    scratch = [
        pltpu.VMEM((HEADS, ROWS, 2 * HD), f32),
        pltpu.VMEM((size, HD), bf16),
        pltpu.VMEM((size, 2 * HD), bf16),
    ]
    if last:
        out_shape = (
            jax.ShapeDtypeStruct((ROWS, HEADS * HD), bf16),
            jax.ShapeDtypeStruct((8, ROWS), f32),
        )
        scratch += [pltpu.VMEM(top, bf16), pltpu.VMEM((HEADS, ROWS, HD), f32)]
    else:
        out_shape = (
            jax.ShapeDtypeStruct((ROWS, HEADS * HD), f32),
            jax.ShapeDtypeStruct((ROWS, HD), f32),
            jax.ShapeDtypeStruct(top, bf16),
        )
        if first:
            out_shape = (jax.ShapeDtypeStruct((ROWS, HEADS * HD), bf16),) + out_shape
    return pl.pallas_call(
        functools.partial(attend_kernel, first, last, numbers_of, len(blocks), kept_numbers_of, len(kept)),
        out_shape=out_shape,
        in_specs=[SMEM] + [VMEM] * len(operands),
        out_specs=(VMEM,) * len(out_shape),
        scratch_shapes=scratch,
        compiler_params=params(20),
        cost_estimate=cost(0.2),
        name="attend_first" if first else "attend_last" if last else "attend_middle",
    )(mine, *operands)


def carry_kernel(
    mine_ref,
    query_hbm,
    local_ref,
    grow_ref,
    kept_ref,
    handed_ref,
    chip_ref,
    core_ref,
    gain_ref,
    out_ref,
):
    mine = mine_ref[0]
    query_ref = query_hbm
    plane, side, core = mine // 4, (mine // 2) % 2, mine % 2
    kept, handed = state_of(kept_ref), state_of(handed_ref)

    def pick(one, two, wanted):
        states = [jnp.where(wanted, jnp.where(core == 0, a, b), 0.0) for a, b in zip(one[0], two[0])]
        return states, jnp.where(wanted, jnp.where(core == 0, one[1], two[1]), 0.0)

    entering = pick(handed, kept, plane >= 2)
    entering = follow(entering, pick(kept, handed, plane >= 1))
    entering = follow(entering, state_of(chip_ref, side == 1))
    entering = follow(entering, state_of(core_ref, core == 1))
    grow = grow_ref[...]
    for h in range(HEADS):
        state = entering[0][h]
        upper = state.astype(bf16)
        lower = (state - upper.astype(f32)).astype(bf16)
        both = dot(query_ref[:, head(h)], jnp.concatenate([upper, lower], 1))
        entered = both[:, :HD] + both[:, HD:]
        result = local_ref[:, head(h)] + entered * grow[:, h : h + 1]
        square = jnp.mean(result * result, -1, keepdims=True)
        out_ref[:, head(h)] = result * lax.rsqrt(square + EPS) * gain_ref[head(h)][None, :]


def finish_kernel(features, attention_ref, square_ref, other_ref, linear_ref, gain_ref, out_ref):
    factor = lax.rsqrt((square_ref[...] + other_ref[...]) / features + EPS)
    factor = dot(factor, jnp.full((8, HD), 0.125, f32), ((0,), (0,)), highest)
    for h in range(HEADS):
        part = attention_ref[:, head(h)].astype(f32) * factor * gain_ref[head(h)][None, :]
        out_ref[:, head(h)] = (part + linear_ref[:, head(h)]).astype(bf16)


def carry_in(place, lh_query, *operands):
    return pl.pallas_call(
        carry_kernel,
        out_shape=jax.ShapeDtypeStruct((ROWS, HEADS * HD), f32),
        in_specs=[SMEM, VMEM] + [VMEM] * len(operands),
        out_specs=VMEM,
        compiler_params=params(14),
        cost_estimate=cost(0.2),
        name="carry",
    )(place, lh_query, *operands)


def finish(features, *operands):
    return pl.pallas_call(
        functools.partial(finish_kernel, features),
        out_shape=jax.ShapeDtypeStruct((ROWS, HEADS * HD), bf16),
        in_specs=[VMEM] * len(operands),
        out_specs=VMEM,
        compiler_params=params(14),
        cost_estimate=cost(0.2),
        name="finish",
    )(*operands)


def body(att_query, att_key, att_value, lh_query, lh_key, lh_value, lh_step, att_gain, lh_gain):
    mine = lax.axis_index("ctx")
    place = mine.reshape(1).astype(jnp.int32)

    def move(value, pairs):
        return lax.ppermute(value, "ctx", pairs)

    every = range(16)
    sibling = [(i, i ^ 1) for i in every]
    sideways = [(i, i ^ 2) for i in every]
    last_plane = [(i, i + 4) for i in every if i % 2 == 0 and i < 12] + [(i, i + 12) for i in (1, 3)]
    plane_before = [(i, i + 8) for i in every if i % 2 == 1 and i < 8]

    def tied(*values):
        return lax.optimization_barrier(values)

    lh_query, lh_key, lh_value, far_query, att_key, att_value = [
        array
        for array in (lh_query, lh_key, lh_value, att_query, att_key, att_value)
    ]
    lh_step = lh_step.T
    att_query, lh_query, lh_key, lh_value, att_key, att_value = [
        pltpu.with_memory_space_constraint(array, pltpu.HBM)
        for array in (att_query, lh_query, lh_key, lh_value, att_key, att_value)
    ]
    own = beside(att_key, att_value)
    across = move(own, [(i, i ^ 2) for i in every if i < 4 or i % 4 < 2])
    near = move(own, sibling)
    chip = stack(own, near)
    chip, lh_step = tied(chip, lh_step)
    lh_step = pltpu.with_memory_space_constraint(lh_step, pltpu.HBM)
    behind = move(chip, last_plane)

    local, grow, message = recur(lh_query, lh_key, lh_value, lh_step)
    chip, across, behind, message = tied(chip, across, behind, message)
    beyond = move(chip, plane_before)
    across_near = move(across, sibling)
    first = move(message, sibling)
    (of_chip,) = join(join_cores_kernel, 1, place, message, first)
    other_even = move(of_chip, [(i, j) for i, j in sideways if i % 2 == 0])
    behind_near = move(behind, sibling)
    level = move(behind, [(i, j) for i, j in sideways if (i % 2 == 0 and i >= 4) or i >= 12])

    def where(number, wanted):
        return jnp.where(wanted, number, NEVER)

    def parts(mine):
        return mine // 4, (mine // 2) % 2, mine % 2, mine - mine % 2

    def brought(mine, core):
        plane, _, _, even = parts(mine)
        if core == 0:
            return where(even - 4, plane >= 1)
        return where(even - 12, plane == 3)

    def behind_numbers(mine):
        _, _, core, _ = parts(mine)
        zero, one = brought(mine, 0), brought(mine, 1)
        return [jnp.where(core == 0, zero, one), jnp.where(core == 0, one, zero)]

    def beyond_numbers(mine):
        plane, _, core, even = parts(mine)
        number = where(even - 8, plane >= 2)
        return [where(number, core == 1), where(number, core == 0)]

    def first_numbers(mine):
        _, side, core, even = parts(mine)
        near_numbers = [where(mine - 1, core == 1)] + [where(even - 2, side == 1)] * 2
        return near_numbers + behind_numbers(mine)

    def middle_numbers(mine):
        return behind_numbers(mine) + beyond_numbers(mine)

    first_blocks = [near, across, across_near, behind, behind_near]
    first_blocks, of_chip = tied(first_blocks, of_chip)
    near_query, *carry = attend(place, att_query, own, None, first_blocks, first_numbers)
    carry, other_even, beyond, level = tied(carry, other_even, beyond, level)
    other_odd = move(other_even, [(i, j) for i, j in sibling if i % 2 == 0])
    level_beyond = move(beyond, [(i, j) for i, j in sideways if i % 2 == 1 and i >= 8])
    beyond_near = move(beyond, sibling)
    level_near = move(level, sibling)
    middle_blocks = [level, level_near, beyond, beyond_near]
    of_plane, other_chip = join(join_sides_kernel, 2, place, of_chip, other_even, other_odd)
    state_behind = move(of_plane, last_plane)
    state_beyond = move(of_plane, plane_before)
    middle_blocks, of_plane = tied(middle_blocks, of_plane)
    carry = attend(place, near_query, own, carry, middle_blocks, middle_numbers)
    carry, level_beyond, state_behind, state_beyond = tied(carry, level_beyond, state_behind, state_beyond)
    level_beyond_near = move(level_beyond, sibling)
    kept = hand(place, state_behind, state_beyond)
    handed = move(kept, sibling)
    last_blocks = [level_beyond, level_beyond_near]
    last_blocks, kept = tied(last_blocks, kept)
    attention, squares = attend(
        place,
        near_query,
        own,
        carry,
        last_blocks,
        beyond_numbers,
        first_blocks + middle_blocks,
        lambda mine: first_numbers(mine) + middle_numbers(mine),
    )

    def over(value, bit):
        return lax.ppermute(value, "tp", [(i, i ^ bit) for i in range(8)])

    squares, handed = tied(squares, handed)
    others = [over(squares, bit) for bit in (2, 4, 6)]
    linear = carry_in(place, lh_query, local, grow, kept, handed, other_chip, first, lh_gain)
    others, linear = tied(others, linear)
    squares = squares + others[0] + others[1] + others[2]
    features = HEADS * HD * lax.axis_size("tp")
    return finish(float(features), attention, squares, over(squares, 1), linear, att_gain)


def solution(mesh):
    placed = (P("ctx", "tp"),) * 7 + (P("tp"), P("tp"))
    return jax.shard_map(body, mesh=mesh, in_specs=placed, out_specs=P("ctx", "tp"), check_vma=False)
```

```python
import functools
import math

import jax
import jax.numpy as jnp
from jax import lax
from jax.experimental import pallas as pl
from jax.experimental.pallas import tpu as pltpu
from jax.sharding import PartitionSpec as P

HD = 128
ROWS = 512
HEADS = 6
TILE = 256
EPS = 1e-06
MASKED = -1e30
LOG2E = math.log2(math.e)
SCORE_SCALE = LOG2E / math.sqrt(HD)
SAFE_EXPONENT = 100.0
STATE_ROWS = HEADS * HD + 8
NEVER = 1 << 20

VMEM = pl.BlockSpec(memory_space=pltpu.VMEM)
SMEM = pl.BlockSpec(memory_space=pltpu.SMEM)
f32 = jnp.float32
bf16 = jnp.bfloat16
highest = lax.Precision.HIGHEST


def dot(a, b, contract=((1,), (0,)), precision=None):
    return lax.dot_general(a, b, (contract, ((), ())), precision=precision, preferred_element_type=f32)


def params(megabytes):
    return pltpu.CompilerParams(vmem_limit_bytes=megabytes << 20)


def cost(us):
    return pl.CostEstimate(flops=int(us * 1e9), bytes_accessed=int(us * 1e6), transcendentals=int(us * 1e6))


def head(h):
    return slice(h * HD, (h + 1) * HD)


def recur_kernel(
    q_hbm, k_hbm, v_hbm, step_ref, local_ref, grow_ref, message_ref, padded
):
    k_ref, q_ref, v_ref = k_hbm, q_hbm, v_hbm
    padded[...] = jnp.full((8, ROWS), 0.5, f32)
    padded[:HEADS, :] = step_ref[...]
    step = padded[...]
    rate = step / (1.0 + step)
    total = -jnp.log(1.0 + step) * LOG2E
    place = lax.broadcasted_iota(jnp.int32, (8, ROWS), 1)
    reach = 1
    while reach < ROWS:
        total = total + jnp.where(place >= reach, pltpu.roll(total, reach, 1), 0.0)
        reach *= 2
    source = jnp.log(rate) * LOG2E - total
    end = total[:, ROWS - 1 : ROWS]
    tail = jnp.exp2(end + source)
    rows = jnp.concatenate([total, tail, jnp.zeros((HD - 16, ROWS), f32)], 0)
    columns = jnp.transpose(rows)
    grow_ref[...] = jnp.exp2(columns)
    message_ref[HEADS * HD :, :] = jnp.broadcast_to(end, (8, HD))
    at_row = lax.broadcasted_iota(jnp.int32, (TILE, TILE), 0)
    at_column = lax.broadcasted_iota(jnp.int32, (TILE, TILE), 1)
    seen = at_column <= at_row
    for h in range(HEADS):
        keys = k_ref[:, head(h)].astype(f32)
        keys = keys * lax.rsqrt(jnp.sum(keys * keys, -1, keepdims=True) + EPS)
        unit = keys.astype(bf16)
        values = v_ref[:, head(h)]
        for a in range(0, ROWS, TILE):
            result = None
            for b in range(0, a + TILE, TILE):
                scores = dot(q_ref[a : a + TILE, head(h)], unit[b : b + TILE], ((1,), (1,)))
                decay = jnp.exp2(columns[a : a + TILE, h : h + 1] + source[h : h + 1, b : b + TILE])
                weights = scores * decay
                if a == b:
                    weights = jnp.where(seen, weights, 0.0)
                part = dot(weights.astype(bf16), values[b : b + TILE])
                result = part if result is None else result + part
            local_ref[a : a + TILE, head(h)] = result
        tailed = (values.astype(f32) * columns[:, 8 + h : 9 + h]).astype(bf16)
        message_ref[head(h), :] = dot(unit, tailed, ((0,), (0,)))


def recur(lh_query, lh_key, lh_value, lh_step):
    return pl.pallas_call(
        recur_kernel,
        out_shape=(
            jax.ShapeDtypeStruct((ROWS, HEADS * HD), f32),
            jax.ShapeDtypeStruct((ROWS, HD), f32),
            jax.ShapeDtypeStruct((STATE_ROWS, HD), f32),
        ),
        in_specs=[VMEM] * 4,
        out_specs=(VMEM,) * 3,
        scratch_shapes=[pltpu.VMEM((8, ROWS), f32)]
,
        compiler_params=params(16),
        cost_estimate=cost(0.2),
        name="recur",
    )(lh_query, lh_key, lh_value, lh_step)


def beside_kernel(key_ref, value_ref, out_ref):
    out_ref[:, :HD] = key_ref[...]
    out_ref[:, HD:] = value_ref[...]


def beside(key, value):
    return pl.pallas_call(
        beside_kernel,
        out_shape=jax.ShapeDtypeStruct((ROWS, 2 * HD), bf16),
        in_specs=[VMEM, VMEM],
        out_specs=VMEM,
        compiler_params=params(14),
        name="beside",
    )(key, value)


def stack_kernel(one_ref, two_ref, out_ref):
    out_ref[:ROWS, :] = one_ref[...]
    out_ref[ROWS:, :] = two_ref[...]


def stack(one, two):
    return pl.pallas_call(
        stack_kernel,
        out_shape=jax.ShapeDtypeStruct((2 * ROWS, 2 * HD), bf16),
        in_specs=[VMEM, VMEM],
        out_specs=VMEM,
        compiler_params=params(14),
        name="stack",
    )(one, two)


def follow(early, late):
    logs = early[1] + late[1]
    states = [jnp.exp2(late[1][h : h + 1, :]) * early[0][h] + late[0][h] for h in range(HEADS)]
    return states, logs


def state_of(ref, wanted=None):
    states = [ref[head(h), :] for h in range(HEADS)]
    logs = ref[HEADS * HD :, :]
    if wanted is None:
        return states, logs
    return [jnp.where(wanted, state, 0.0) for state in states], jnp.where(wanted, logs, 0.0)


def put_state(ref, value):
    for h in range(HEADS):
        ref[head(h), :] = value[0][h]
    ref[HEADS * HD :, :] = value[1]


def join_cores_kernel(mine_ref, own_ref, other_ref, out_ref):
    own, other = state_of(own_ref), state_of(other_ref)
    put_state(out_ref, follow_in_order(mine_ref[0] % 2 == 0, own, other))


def join_sides_kernel(mine_ref, own_ref, even_ref, odd_ref, out_ref, other_ref):
    mine = mine_ref[0]
    own, even, odd = state_of(own_ref), state_of(even_ref), state_of(odd_ref)
    other = select(mine % 2 == 0, even, odd)
    put_state(other_ref, other)
    put_state(out_ref, follow_in_order((mine // 2) % 2 == 0, own, other))


def select(wanted, one, two):
    return [jnp.where(wanted, a, b) for a, b in zip(one[0], two[0])], jnp.where(wanted, one[1], two[1])


def follow_in_order(own_first, own, other):
    return follow(select(own_first, own, other), select(own_first, other, own))


def join(kernel, outputs, mine, *messages):
    return pl.pallas_call(
        kernel,
        out_shape=(jax.ShapeDtypeStruct((STATE_ROWS, HD), f32),) * outputs,
        in_specs=[SMEM] + [VMEM] * len(messages),
        out_specs=(VMEM,) * outputs,
        compiler_params=params(14),
        cost_estimate=cost(0.2),
        name="join",
    )(mine, *messages)


def hand_kernel(mine_ref, behind_ref, beyond_ref, out_ref):
    plane, core = mine_ref[0] // 4, mine_ref[0] % 2
    behind = state_of(behind_ref, (plane == 3) | (core == 0))
    beyond = state_of(beyond_ref, (plane >= 2) & (core == 1))
    put_state(out_ref, follow(behind, beyond))


def hand(mine, behind, beyond):
    return pl.pallas_call(
        hand_kernel,
        out_shape=jax.ShapeDtypeStruct((STATE_ROWS, HD), f32),
        in_specs=[SMEM, VMEM, VMEM],
        out_specs=VMEM,
        compiler_params=params(14),
        cost_estimate=cost(0.2),
        name="hand",
    )(mine, behind, beyond)


def attend_kernel(first, last, numbers_of, buffers, kept_numbers_of, kept, mine_ref, query_ref, own_ref, *refs):
    mine = mine_ref[0]
    refs = list(refs)

    def take(count):
        return [refs.pop(0) for _ in range(count)]

    if not first:
        carry_ref, count_ref, top_in_ref = take(3)
    block_refs = take(buffers)
    kept_refs = take(kept)
    if last:
        out_ref, square_ref, sums, keys, values, top_ref, tops = refs
    else:
        if first:
            (passed_ref,) = take(1)
            passed_ref[...] = query_ref[...]
        numerator_ref, counted_ref, top_ref, sums, keys, values = refs

    def highest_of(part):
        return jnp.max(jnp.abs(part).reshape(-1, 16, HD), 0)

    def fill(blocks, numbers):
        filled = jnp.int32(0)
        for block, number in zip(blocks, numbers):
            rows = block.shape[0]
            takes = number < mine
            place = filled

            @pl.when(takes)
            def _():
                at = pl.ds(pl.multiple_of(place * ROWS, ROWS), rows)
                keys[at, :] = block[:, :HD]
                values[at, :HD] = block[:, HD:]
                top_ref[16:32, :] = jnp.maximum(top_ref[16:32, :], highest_of(block[:, :HD]))

            filled = filled + jnp.where(takes, rows // ROWS, 0)
        return filled

    if first:
        top_ref[16:32, :] = highest_of(own_ref[:, :HD])
        longest = jnp.zeros((ROWS, HD), f32)
        ones = jnp.ones((HD, HD), bf16)
        for h in range(HEADS):
            query = query_ref[:, head(h)].astype(f32)
            longest = jnp.maximum(longest, dot((query * query).astype(bf16), ones))
        top_ref[0:16, :] = jnp.max(longest.reshape(-1, 16, HD), 0).astype(bf16)
    else:
        top_ref[...] = top_in_ref[...]
    values[:, HD:] = jnp.ones((values.shape[0], HD), bf16)
    filled = fill(block_refs, numbers_of(mine))
    sums[...] = jnp.zeros_like(sums)

    def visit(start, count):
        at = pl.ds(pl.multiple_of(start, ROWS), count)
        block_keys = keys[at, :]
        block_values = values[at, :]
        for h in range(HEADS):
            for a in range(0, ROWS, TILE):
                scores = dot(query_ref[a : a + TILE, head(h)], block_keys, ((1,), (1,)))
                weights = jnp.exp2(scores * SCORE_SCALE).astype(bf16)
                sums[h, a : a + TILE, :] += dot(weights, block_values)

    def pair(n, _):
        visit(n * 2 * ROWS, 2 * ROWS)
        return 0

    if not first:
        lax.fori_loop(0, filled // 2, pair, 0)

    if first:

        @pl.when(filled > 0)
        def _():
            visit(0, ROWS)

        at_row = lax.broadcasted_iota(jnp.int32, (TILE, TILE), 0)
        at_column = lax.broadcasted_iota(jnp.int32, (TILE, TILE), 1)
        seen = at_column <= at_row
        values[:ROWS, :HD] = own_ref[:, HD:]
        for h in range(HEADS):
            for a in range(0, ROWS, TILE):
                for b in range(0, a + TILE, TILE):
                    scores = dot(query_ref[a : a + TILE, head(h)], own_ref[b : b + TILE, :HD], ((1,), (1,)))
                    weights = jnp.exp2(scores * SCORE_SCALE)
                    if a == b:
                        weights = jnp.where(seen, weights, 0.0)
                    sums[h, a : a + TILE, :] += dot(weights.astype(bf16), values[b : b + TILE, :])
            numerator_ref[:, head(h)] = sums[h, :, :HD]
            counted_ref[:, h : h + 1] = sums[h, :, HD : HD + 1]
    elif not last:
        for h in range(HEADS):
            numerator_ref[:, head(h)] = sums[h, :, :HD] + carry_ref[:, head(h)]
            counted_ref[:, h : h + 1] = sums[h, :, HD : HD + 1] + count_ref[:, h : h + 1]
    else:
        key_top = jnp.max(top_ref[16:32, :].astype(f32), 0, keepdims=True)
        bound = jnp.max(top_ref[0:16, :].astype(f32)) * jnp.sum(key_top * key_top) * SCORE_SCALE**2
        large = bound * 1.05 > SAFE_EXPONENT * SAFE_EXPONENT

        @pl.when(large)
        def _():
            before = fill(kept_refs + block_refs, kept_numbers_of(mine) + numbers_of(mine))
            at = pl.ds(pl.multiple_of(before * ROWS, ROWS), ROWS)
            keys[at, :] = own_ref[:, :HD]
            values[at, :HD] = own_ref[:, HD:]
            sums[...] = jnp.zeros_like(sums)
            tops[...] = jnp.full_like(tops, MASKED)

            def step(n, _):
                at = pl.ds(pl.multiple_of((n // (2 * HEADS)) * ROWS, ROWS), ROWS)
                h = (n % (2 * HEADS)) // 2
                a = (n % 2) * TILE
                rows = pl.ds(pl.multiple_of(a, TILE), TILE)
                query = query_ref[rows, pl.ds(pl.multiple_of(h * HD, HD), HD)]
                scores = dot(query, keys[at, :], ((1,), (1,))) * SCORE_SCALE
                row = lax.broadcasted_iota(jnp.int32, (TILE, ROWS), 0) + a
                column = lax.broadcasted_iota(jnp.int32, (TILE, ROWS), 1)
                column = column - jnp.where(n // (2 * HEADS) < before, ROWS, 0)
                visible = column <= row
                scores = jnp.where(visible, scores, MASKED)
                old = tops[h, rows, :]
                new = jnp.maximum(old[:, :1], jnp.max(scores, 1, keepdims=True))
                weights = jnp.where(visible, jnp.exp2(scores - new), 0.0).astype(bf16)
                sums[h, rows, :] = sums[h, rows, :] * jnp.exp2(old[:, :1] - new) + dot(weights, values[at, :])
                tops[h, rows, :] = jnp.broadcast_to(new, (TILE, HD))
                return 0

            lax.fori_loop(0, (before + 1) * 2 * HEADS, step, 0)

        squares = jnp.zeros((ROWS, HD), f32)
        for h in range(HEADS):
            count = sums[h, :, HD:] + jnp.where(large, 0.0, count_ref[:, h : h + 1])
            result = (sums[h, :, :HD] + jnp.where(large, 0.0, carry_ref[:, head(h)])) / count
            result = result.astype(bf16)
            out_ref[:, head(h)] = result
            result = result.astype(f32)
            squares = squares + result * result
        square_ref[...] = dot(jnp.ones((8, HD), f32), squares, ((1,), (1,)), highest)


def attend(mine, query, own, carry, blocks, numbers_of, kept=None, kept_numbers_of=None):
    first, last = carry is None, kept is not None
    kept = kept or []
    size = sum(block.shape[0] for block in blocks)
    size = 16 * ROWS if last else size
    operands = [query, own] + list(carry or []) + list(blocks) + kept
    top = (32, HD)
    scratch = [
        pltpu.VMEM((HEADS, ROWS, 2 * HD), f32),
        pltpu.VMEM((size, HD), bf16),
        pltpu.VMEM((size, 2 * HD), bf16),
    ]
    if last:
        out_shape = (
            jax.ShapeDtypeStruct((ROWS, HEADS * HD), bf16),
            jax.ShapeDtypeStruct((8, ROWS), f32),
        )
        scratch += [pltpu.VMEM(top, bf16), pltpu.VMEM((HEADS, ROWS, HD), f32)]
    else:
        out_shape = (
            jax.ShapeDtypeStruct((ROWS, HEADS * HD), f32),
            jax.ShapeDtypeStruct((ROWS, HD), f32),
            jax.ShapeDtypeStruct(top, bf16),
        )
        if first:
            out_shape = (jax.ShapeDtypeStruct((ROWS, HEADS * HD), bf16),) + out_shape
    return pl.pallas_call(
        functools.partial(attend_kernel, first, last, numbers_of, len(blocks), kept_numbers_of, len(kept)),
        out_shape=out_shape,
        in_specs=[SMEM] + [VMEM] * len(operands),
        out_specs=(VMEM,) * len(out_shape),
        scratch_shapes=scratch,
        compiler_params=params(20),
        cost_estimate=cost(0.2),
        name="attend_first" if first else "attend_last" if last else "attend_middle",
    )(mine, *operands)


def carry_kernel(
    mine_ref,
    query_hbm,
    local_ref,
    grow_ref,
    kept_ref,
    handed_ref,
    chip_ref,
    core_ref,
    gain_ref,
    out_ref,
):
    mine = mine_ref[0]
    query_ref = query_hbm
    plane, side, core = mine // 4, (mine // 2) % 2, mine % 2
    kept, handed = state_of(kept_ref), state_of(handed_ref)

    def pick(one, two, wanted):
        states = [jnp.where(wanted, jnp.where(core == 0, a, b), 0.0) for a, b in zip(one[0], two[0])]
        return states, jnp.where(wanted, jnp.where(core == 0, one[1], two[1]), 0.0)

    entering = pick(handed, kept, plane >= 2)
    entering = follow(entering, pick(kept, handed, plane >= 1))
    entering = follow(entering, state_of(chip_ref, side == 1))
    entering = follow(entering, state_of(core_ref, core == 1))
    grow = grow_ref[...]
    for h in range(HEADS):
        state = entering[0][h]
        upper = state.astype(bf16)
        lower = (state - upper.astype(f32)).astype(bf16)
        both = dot(query_ref[:, head(h)], jnp.concatenate([upper, lower], 1))
        entered = both[:, :HD] + both[:, HD:]
        result = local_ref[:, head(h)] + entered * grow[:, h : h + 1]
        square = jnp.mean(result * result, -1, keepdims=True)
        out_ref[:, head(h)] = result * lax.rsqrt(square + EPS) * gain_ref[head(h)][None, :]


def finish_kernel(features, attention_ref, square_ref, other_ref, linear_ref, gain_ref, out_ref):
    factor = lax.rsqrt((square_ref[...] + other_ref[...]) / features + EPS)
    factor = dot(factor, jnp.full((8, HD), 0.125, f32), ((0,), (0,)), highest)
    for h in range(HEADS):
        part = attention_ref[:, head(h)].astype(f32) * factor * gain_ref[head(h)][None, :]
        out_ref[:, head(h)] = (part + linear_ref[:, head(h)]).astype(bf16)


def carry_in(place, lh_query, *operands):
    return pl.pallas_call(
        carry_kernel,
        out_shape=jax.ShapeDtypeStruct((ROWS, HEADS * HD), f32),
        in_specs=[SMEM, VMEM] + [VMEM] * len(operands),
        out_specs=VMEM,
        compiler_params=params(14),
        cost_estimate=cost(0.2),
        name="carry",
    )(place, lh_query, *operands)


def finish(features, *operands):
    return pl.pallas_call(
        functools.partial(finish_kernel, features),
        out_shape=jax.ShapeDtypeStruct((ROWS, HEADS * HD), bf16),
        in_specs=[VMEM] * len(operands),
        out_specs=VMEM,
        compiler_params=params(14),
        cost_estimate=cost(0.2),
        name="finish",
    )(*operands)


def body(att_query, att_key, att_value, lh_query, lh_key, lh_value, lh_step, att_gain, lh_gain):
    mine = lax.axis_index("ctx")
    place = mine.reshape(1).astype(jnp.int32)

    def move(value, pairs):
        return lax.ppermute(value, "ctx", pairs)

    every = range(16)
    sibling = [(i, i ^ 1) for i in every]
    sideways = [(i, i ^ 2) for i in every]
    last_plane = [(i, i + 4) for i in every if i % 2 == 0 and i < 12] + [(i, i + 12) for i in (1, 3)]
    plane_before = [(i, i + 8) for i in every if i % 2 == 1 and i < 8]

    def tied(*values):
        return lax.optimization_barrier(values)

    lh_query, lh_key, lh_value, far_query, att_key, att_value = [
        array
        for array in (lh_query, lh_key, lh_value, att_query, att_key, att_value)
    ]
    lh_step = lh_step.T
    att_query, lh_query, lh_key, lh_value, att_key, att_value = [
        pltpu.with_memory_space_constraint(array, pltpu.HBM)
        for array in (att_query, lh_query, lh_key, lh_value, att_key, att_value)
    ]
    own = beside(att_key, att_value)
    across = move(own, [(i, i ^ 2) for i in every if i < 4 or i % 4 < 2])
    near = move(own, sibling)
    chip = stack(own, near)
    chip, lh_step = tied(chip, lh_step)
    lh_step = pltpu.with_memory_space_constraint(lh_step, pltpu.HBM)
    behind = move(chip, last_plane)

    local, grow, message = recur(lh_query, lh_key, lh_value, lh_step)
    def where(number, wanted):
        return jnp.where(wanted, number, NEVER)

    def parts(mine):
        return mine // 4, (mine // 2) % 2, mine % 2, mine - mine % 2

    def brought(mine, core):
        plane, _, _, even = parts(mine)
        if core == 0:
            return where(even - 4, plane >= 1)
        return where(even - 12, plane == 3)

    def behind_numbers(mine):
        _, _, core, _ = parts(mine)
        zero, one = brought(mine, 0), brought(mine, 1)
        return [jnp.where(core == 0, zero, one), jnp.where(core == 0, one, zero)]

    def beyond_numbers(mine):
        plane, _, core, even = parts(mine)
        number = where(even - 8, plane >= 2)
        return [where(number, core == 1), where(number, core == 0)]

    def near_numbers(mine):
        return [where(mine - 1, mine % 2 == 1)]

    def across_numbers(mine):
        _, side, _, even = parts(mine)
        return [where(even - 2, side == 1)] * 2

    def behind_numbers(mine):
        _, _, core, _ = parts(mine)
        zero, one = brought(mine, 0), brought(mine, 1)
        return [jnp.where(core == 0, zero, one), jnp.where(core == 0, one, zero)]

    def beyond_numbers(mine):
        plane, _, core, even = parts(mine)
        number = where(even - 8, plane >= 2)
        return [where(number, core == 1), where(number, core == 0)]

    def first_numbers(mine):
        _, side, core, even = parts(mine)
        near_numbers = [where(mine - 1, core == 1)] + [where(even - 2, side == 1)] * 2
        return near_numbers + behind_numbers(mine)

    def middle_numbers(mine):
        return behind_numbers(mine) + beyond_numbers(mine)

    def last_numbers(mine):
        return across_numbers(mine) + beyond_numbers(mine)

    near_query, *carry = attend(place, att_query, own, None, [near], near_numbers)
    carry, message, across = tied(carry, message, across)
    first = move(message, sibling)
    (of_chip,) = join(join_cores_kernel, 1, place, message, first)
    other_even = move(of_chip, [(i, j) for i, j in sideways if i % 2 == 0])

    chip, behind, of_chip = tied(chip, behind, of_chip)
    behind_near = move(behind, sibling)
    level = move(behind, [(i, j) for i, j in sideways if (i % 2 == 0 and i >= 4) or i >= 12])
    beyond = move(chip, plane_before)
    carry = attend(place, near_query, own, carry, [behind, behind_near], behind_numbers)

    carry, other_even, across, beyond, level = tied(carry, other_even, across, beyond, level)
    other_odd = move(other_even, [(i, j) for i, j in sibling if i % 2 == 0])
    level_beyond = move(beyond, [(i, j) for i, j in sideways if i % 2 == 1 and i >= 8])
    across_near = move(across, sibling)
    beyond_near = move(beyond, sibling)
    level_near = move(level, sibling)
    of_plane, other_chip = join(join_sides_kernel, 2, place, of_chip, other_even, other_odd)
    state_behind = move(of_plane, last_plane)
    state_beyond = move(of_plane, plane_before)
    middle_blocks = [level, level_near, beyond, beyond_near]
    middle_blocks, of_plane = tied(middle_blocks, of_plane)
    carry = attend(place, near_query, own, carry, middle_blocks, middle_numbers)

    carry, level_beyond, state_behind, state_beyond = tied(carry, level_beyond, state_behind, state_beyond)
    level_beyond_near = move(level_beyond, sibling)
    kept = hand(place, state_behind, state_beyond)
    handed = move(kept, sibling)
    last_blocks = [across, across_near, level_beyond, level_beyond_near]
    last_blocks, kept = tied(last_blocks, kept)
    attention, squares = attend(
        place,
        near_query,
        own,
        carry,
        last_blocks,
        last_numbers,
        [near, behind, behind_near] + middle_blocks,
        lambda mine: near_numbers(mine) + behind_numbers(mine) + middle_numbers(mine),
    )

    def over(value, bit):
        return lax.ppermute(value, "tp", [(i, i ^ bit) for i in range(8)])

    squares, handed = tied(squares, handed)
    others = [over(squares, bit) for bit in (2, 4, 6)]
    linear = carry_in(place, lh_query, local, grow, kept, handed, other_chip, first, lh_gain)
    others, linear = tied(others, linear)
    squares = squares + others[0] + others[1] + others[2]
    features = HEADS * HD * lax.axis_size("tp")
    return finish(float(features), attention, squares, over(squares, 1), linear, att_gain)


def solution(mesh):
    placed = (P("ctx", "tp"),) * 7 + (P("tp"), P("tp"))
    return jax.shard_map(body, mesh=mesh, in_specs=placed, out_specs=P("ctx", "tp"), check_vma=False)
```

```python
import functools
import math

import jax
import jax.numpy as jnp
from jax import lax
from jax.experimental import pallas as pl
from jax.experimental.pallas import tpu as pltpu
from jax.sharding import PartitionSpec as P

HD = 128
ROWS = 512
HEADS = 6
TILE = 256
EPS = 1e-06
MASKED = -1e30
LOG2E = math.log2(math.e)
SCORE_SCALE = LOG2E / math.sqrt(HD)
SAFE_EXPONENT = 100.0
STATE_ROWS = HEADS * HD + 8
NEVER = 1 << 20

VMEM = pl.BlockSpec(memory_space=pltpu.VMEM)
SMEM = pl.BlockSpec(memory_space=pltpu.SMEM)
f32 = jnp.float32
bf16 = jnp.bfloat16
highest = lax.Precision.HIGHEST


def dot(a, b, contract=((1,), (0,)), precision=None):
    return lax.dot_general(a, b, (contract, ((), ())), precision=precision, preferred_element_type=f32)


def params(megabytes):
    return pltpu.CompilerParams(vmem_limit_bytes=megabytes << 20)


def cost(us):
    return pl.CostEstimate(flops=int(us * 1e9), bytes_accessed=int(us * 1e6), transcendentals=int(us * 1e6))


def head(h):
    return slice(h * HD, (h + 1) * HD)


def recur_kernel(
    q_hbm, k_hbm, v_hbm, step_ref, local_ref, grow_ref, message_ref, padded
):
    k_ref, q_ref, v_ref = k_hbm, q_hbm, v_hbm
    padded[...] = jnp.full((8, ROWS), 0.5, f32)
    padded[:HEADS, :] = step_ref[...]
    step = padded[...]
    rate = step / (1.0 + step)
    total = -jnp.log(1.0 + step) * LOG2E
    place = lax.broadcasted_iota(jnp.int32, (8, ROWS), 1)
    reach = 1
    while reach < ROWS:
        total = total + jnp.where(place >= reach, pltpu.roll(total, reach, 1), 0.0)
        reach *= 2
    source = jnp.log(rate) * LOG2E - total
    end = total[:, ROWS - 1 : ROWS]
    tail = jnp.exp2(end + source)
    rows = jnp.concatenate([total, tail, jnp.zeros((HD - 16, ROWS), f32)], 0)
    columns = jnp.transpose(rows)
    grow_ref[...] = jnp.exp2(columns)
    message_ref[HEADS * HD :, :] = jnp.broadcast_to(end, (8, HD))
    at_row = lax.broadcasted_iota(jnp.int32, (TILE, TILE), 0)
    at_column = lax.broadcasted_iota(jnp.int32, (TILE, TILE), 1)
    seen = at_column <= at_row
    for h in range(HEADS):
        keys = k_ref[:, head(h)].astype(f32)
        keys = keys * lax.rsqrt(jnp.sum(keys * keys, -1, keepdims=True) + EPS)
        unit = keys.astype(bf16)
        values = v_ref[:, head(h)]
        for a in range(0, ROWS, TILE):
            result = None
            for b in range(0, a + TILE, TILE):
                scores = dot(q_ref[a : a + TILE, head(h)], unit[b : b + TILE], ((1,), (1,)))
                decay = jnp.exp2(columns[a : a + TILE, h : h + 1] + source[h : h + 1, b : b + TILE])
                weights = scores * decay
                if a == b:
                    weights = jnp.where(seen, weights, 0.0)
                part = dot(weights.astype(bf16), values[b : b + TILE])
                result = part if result is None else result + part
            local_ref[a : a + TILE, head(h)] = result
        tailed = (values.astype(f32) * columns[:, 8 + h : 9 + h]).astype(bf16)
        message_ref[head(h), :] = dot(unit, tailed, ((0,), (0,)))


def recur(lh_query, lh_key, lh_value, lh_step):
    return pl.pallas_call(
        recur_kernel,
        out_shape=(
            jax.ShapeDtypeStruct((ROWS, HEADS * HD), f32),
            jax.ShapeDtypeStruct((ROWS, HD), f32),
            jax.ShapeDtypeStruct((STATE_ROWS, HD), f32),
        ),
        in_specs=[VMEM] * 4,
        out_specs=(VMEM,) * 3,
        scratch_shapes=[pltpu.VMEM((8, ROWS), f32)]
,
        compiler_params=params(16),
        cost_estimate=cost(0.2),
        name="recur",
    )(lh_query, lh_key, lh_value, lh_step)


def beside_kernel(key_ref, value_ref, out_ref):
    out_ref[:, :HD] = key_ref[...]
    out_ref[:, HD:] = value_ref[...]


def beside(key, value):
    return pl.pallas_call(
        beside_kernel,
        out_shape=jax.ShapeDtypeStruct((ROWS, 2 * HD), bf16),
        in_specs=[VMEM, VMEM],
        out_specs=VMEM,
        compiler_params=params(14),
        name="beside",
    )(key, value)


def stack_kernel(*refs):
    *parts, out_ref = refs
    at = 0
    for part in parts:
        out_ref[at : at + part.shape[0], :] = part[...]
        at += part.shape[0]


def stack(*parts):
    return pl.pallas_call(
        stack_kernel,
        out_shape=jax.ShapeDtypeStruct((sum(part.shape[0] for part in parts), 2 * HD), bf16),
        in_specs=[VMEM] * len(parts),
        out_specs=VMEM,
        compiler_params=params(14),
        name="stack",
    )(*parts)


def follow(early, late):
    logs = early[1] + late[1]
    states = [jnp.exp2(late[1][h : h + 1, :]) * early[0][h] + late[0][h] for h in range(HEADS)]
    return states, logs


def state_of(ref, wanted=None):
    states = [ref[head(h), :] for h in range(HEADS)]
    logs = ref[HEADS * HD :, :]
    if wanted is None:
        return states, logs
    return [jnp.where(wanted, state, 0.0) for state in states], jnp.where(wanted, logs, 0.0)


def put_state(ref, value):
    for h in range(HEADS):
        ref[head(h), :] = value[0][h]
    ref[HEADS * HD :, :] = value[1]


def join_cores_kernel(mine_ref, own_ref, other_ref, out_ref):
    own, other = state_of(own_ref), state_of(other_ref)
    put_state(out_ref, follow_in_order(mine_ref[0] % 2 == 0, own, other))


def join_sides_kernel(mine_ref, own_ref, even_ref, odd_ref, out_ref, other_ref):
    mine = mine_ref[0]
    own, even, odd = state_of(own_ref), state_of(even_ref), state_of(odd_ref)
    other = select(mine % 2 == 0, even, odd)
    put_state(other_ref, other)
    put_state(out_ref, follow_in_order((mine // 2) % 2 == 0, own, other))


def select(wanted, one, two):
    return [jnp.where(wanted, a, b) for a, b in zip(one[0], two[0])], jnp.where(wanted, one[1], two[1])


def follow_in_order(own_first, own, other):
    return follow(select(own_first, own, other), select(own_first, other, own))


def join(kernel, outputs, mine, *messages):
    return pl.pallas_call(
        kernel,
        out_shape=(jax.ShapeDtypeStruct((STATE_ROWS, HD), f32),) * outputs,
        in_specs=[SMEM] + [VMEM] * len(messages),
        out_specs=(VMEM,) * outputs,
        compiler_params=params(14),
        cost_estimate=cost(0.2),
        name="join",
    )(mine, *messages)


def hand_kernel(mine_ref, behind_ref, beyond_ref, out_ref):
    plane, core = mine_ref[0] // 4, mine_ref[0] % 2
    behind = state_of(behind_ref, (plane == 3) | (core == 0))
    beyond = state_of(beyond_ref, (plane >= 2) & (core == 1))
    put_state(out_ref, follow(behind, beyond))


def hand(mine, behind, beyond):
    return pl.pallas_call(
        hand_kernel,
        out_shape=jax.ShapeDtypeStruct((STATE_ROWS, HD), f32),
        in_specs=[SMEM, VMEM, VMEM],
        out_specs=VMEM,
        compiler_params=params(14),
        cost_estimate=cost(0.2),
        name="hand",
    )(mine, behind, beyond)


def attend_kernel(first, last, numbers_of, pieces, kept_numbers_of, kept, mine_ref, query_ref, own_ref, *refs):
    mine = mine_ref[0]
    refs = list(refs)

    def take(count):
        return [refs.pop(0) for _ in range(count)]

    if not first:
        carry_ref, count_ref, top_in_ref = take(3)
    block_refs = [(ref, *piece) for ref, piece in zip(take(len(pieces)), pieces)]
    kept_refs = [(ref, *piece) for ref, piece in zip(take(len(kept)), kept)]
    if last:
        out_ref, square_ref, sums, keys, values, top_ref, tops = refs
    else:
        if first:
            (passed_ref,) = take(1)
            passed_ref[...] = query_ref[...]
        numerator_ref, counted_ref, top_ref, sums, keys, values = refs

    def highest_of(part):
        return jnp.max(jnp.abs(part).reshape(-1, 16, HD), 0)

    def fill(blocks, numbers):
        filled = jnp.int32(0)
        for (block, start, rows), number in zip(blocks, numbers):
            takes = number < mine
            place = filled

            @pl.when(takes)
            def _():
                at = pl.ds(pl.multiple_of(place * ROWS, ROWS), rows)
                block_keys = block[start : start + rows, :HD]
                keys[at, :] = block_keys
                values[at, :HD] = block[start : start + rows, HD:]
                top_ref[16:32, :] = jnp.maximum(top_ref[16:32, :], highest_of(block_keys))

            filled = filled + jnp.where(takes, rows // ROWS, 0)
        return filled

    if first:
        top_ref[16:32, :] = highest_of(own_ref[:, :HD])
        longest = jnp.zeros((ROWS, HD), f32)
        ones = jnp.ones((HD, HD), bf16)
        for h in range(HEADS):
            query = query_ref[:, head(h)].astype(f32)
            longest = jnp.maximum(longest, dot((query * query).astype(bf16), ones))
        top_ref[0:16, :] = jnp.max(longest.reshape(-1, 16, HD), 0).astype(bf16)
    else:
        top_ref[...] = top_in_ref[...]
    values[:, HD:] = jnp.ones((values.shape[0], HD), bf16)
    filled = fill(block_refs, numbers_of(mine))
    sums[...] = jnp.zeros_like(sums)

    def visit(start, count):
        at = pl.ds(pl.multiple_of(start, ROWS), count)
        block_keys = keys[at, :]
        block_values = values[at, :]
        for h in range(HEADS):
            for a in range(0, ROWS, TILE):
                scores = dot(query_ref[a : a + TILE, head(h)], block_keys, ((1,), (1,)))
                weights = jnp.exp2(scores * SCORE_SCALE).astype(bf16)
                sums[h, a : a + TILE, :] += dot(weights, block_values)

    def pair(n, _):
        visit(n * 2 * ROWS, 2 * ROWS)
        return 0

    if not first:
        lax.fori_loop(0, filled // 2, pair, 0)

    if first:

        @pl.when(filled > 0)
        def _():
            visit(0, ROWS)

        at_row = lax.broadcasted_iota(jnp.int32, (TILE, TILE), 0)
        at_column = lax.broadcasted_iota(jnp.int32, (TILE, TILE), 1)
        seen = at_column <= at_row
        values[:ROWS, :HD] = own_ref[:, HD:]
        for h in range(HEADS):
            for a in range(0, ROWS, TILE):
                for b in range(0, a + TILE, TILE):
                    scores = dot(query_ref[a : a + TILE, head(h)], own_ref[b : b + TILE, :HD], ((1,), (1,)))
                    weights = jnp.exp2(scores * SCORE_SCALE)
                    if a == b:
                        weights = jnp.where(seen, weights, 0.0)
                    sums[h, a : a + TILE, :] += dot(weights.astype(bf16), values[b : b + TILE, :])
            numerator_ref[:, head(h)] = sums[h, :, :HD]
            counted_ref[:, h : h + 1] = sums[h, :, HD : HD + 1]
    elif not last:
        for h in range(HEADS):
            numerator_ref[:, head(h)] = sums[h, :, :HD] + carry_ref[:, head(h)]
            counted_ref[:, h : h + 1] = sums[h, :, HD : HD + 1] + count_ref[:, h : h + 1]
    else:
        key_top = jnp.max(top_ref[16:32, :].astype(f32), 0, keepdims=True)
        bound = jnp.max(top_ref[0:16, :].astype(f32)) * jnp.sum(key_top * key_top) * SCORE_SCALE**2
        large = bound * 1.05 > SAFE_EXPONENT * SAFE_EXPONENT

        @pl.when(large)
        def _():
            before = fill(kept_refs + block_refs, kept_numbers_of(mine) + numbers_of(mine))
            at = pl.ds(pl.multiple_of(before * ROWS, ROWS), ROWS)
            keys[at, :] = own_ref[:, :HD]
            values[at, :HD] = own_ref[:, HD:]
            sums[...] = jnp.zeros_like(sums)
            tops[...] = jnp.full_like(tops, MASKED)

            def step(n, _):
                at = pl.ds(pl.multiple_of((n // (2 * HEADS)) * ROWS, ROWS), ROWS)
                h = (n % (2 * HEADS)) // 2
                a = (n % 2) * TILE
                rows = pl.ds(pl.multiple_of(a, TILE), TILE)
                query = query_ref[rows, pl.ds(pl.multiple_of(h * HD, HD), HD)]
                scores = dot(query, keys[at, :], ((1,), (1,))) * SCORE_SCALE
                row = lax.broadcasted_iota(jnp.int32, (TILE, ROWS), 0) + a
                column = lax.broadcasted_iota(jnp.int32, (TILE, ROWS), 1)
                column = column - jnp.where(n // (2 * HEADS) < before, ROWS, 0)
                visible = column <= row
                scores = jnp.where(visible, scores, MASKED)
                old = tops[h, rows, :]
                new = jnp.maximum(old[:, :1], jnp.max(scores, 1, keepdims=True))
                weights = jnp.where(visible, jnp.exp2(scores - new), 0.0).astype(bf16)
                sums[h, rows, :] = sums[h, rows, :] * jnp.exp2(old[:, :1] - new) + dot(weights, values[at, :])
                tops[h, rows, :] = jnp.broadcast_to(new, (TILE, HD))
                return 0

            lax.fori_loop(0, (before + 1) * 2 * HEADS, step, 0)

        squares = jnp.zeros((ROWS, HD), f32)
        for h in range(HEADS):
            count = sums[h, :, HD:] + jnp.where(large, 0.0, count_ref[:, h : h + 1])
            result = (sums[h, :, :HD] + jnp.where(large, 0.0, carry_ref[:, head(h)])) / count
            result = result.astype(bf16)
            out_ref[:, head(h)] = result
            result = result.astype(f32)
            squares = squares + result * result
        square_ref[...] = dot(jnp.ones((8, HD), f32), squares, ((1,), (1,)), highest)


def attend(mine, query, own, carry, blocks, numbers_of, kept=None, kept_numbers_of=None):
    first, last = carry is None, kept is not None
    kept = kept or []
    size = 16 * ROWS if last else sum(rows for _, _, rows in blocks)
    operands = [query, own] + list(carry or []) + [block for block, _, _ in blocks + kept]
    top = (32, HD)
    scratch = [
        pltpu.VMEM((HEADS, ROWS, 2 * HD), f32),
        pltpu.VMEM((size, HD), bf16),
        pltpu.VMEM((size, 2 * HD), bf16),
    ]
    if last:
        out_shape = (
            jax.ShapeDtypeStruct((ROWS, HEADS * HD), bf16),
            jax.ShapeDtypeStruct((8, ROWS), f32),
        )
        scratch += [pltpu.VMEM(top, bf16), pltpu.VMEM((HEADS, ROWS, HD), f32)]
    else:
        out_shape = (
            jax.ShapeDtypeStruct((ROWS, HEADS * HD), f32),
            jax.ShapeDtypeStruct((ROWS, HD), f32),
            jax.ShapeDtypeStruct(top, bf16),
        )
        if first:
            out_shape = (jax.ShapeDtypeStruct((ROWS, HEADS * HD), bf16),) + out_shape
    return pl.pallas_call(
        functools.partial(
            attend_kernel,
            first,
            last,
            numbers_of,
            [block[1:] for block in blocks],
            kept_numbers_of,
            [block[1:] for block in kept],
        ),
        out_shape=out_shape,
        in_specs=[SMEM] + [VMEM] * len(operands),
        out_specs=(VMEM,) * len(out_shape),
        scratch_shapes=scratch,
        compiler_params=params(20),
        cost_estimate=cost(0.2),
        name="attend_first" if first else "attend_last" if last else "attend_middle",
    )(mine, *operands)


def carry_kernel(
    mine_ref,
    query_hbm,
    local_ref,
    grow_ref,
    kept_ref,
    handed_ref,
    chip_ref,
    core_ref,
    gain_ref,
    out_ref,
):
    mine = mine_ref[0]
    query_ref = query_hbm
    plane, side, core = mine // 4, (mine // 2) % 2, mine % 2
    kept, handed = state_of(kept_ref), state_of(handed_ref)

    def pick(one, two, wanted):
        states = [jnp.where(wanted, jnp.where(core == 0, a, b), 0.0) for a, b in zip(one[0], two[0])]
        return states, jnp.where(wanted, jnp.where(core == 0, one[1], two[1]), 0.0)

    entering = pick(handed, kept, plane >= 2)
    entering = follow(entering, pick(kept, handed, plane >= 1))
    entering = follow(entering, state_of(chip_ref, side == 1))
    entering = follow(entering, state_of(core_ref, core == 1))
    grow = grow_ref[...]
    for h in range(HEADS):
        state = entering[0][h]
        upper = state.astype(bf16)
        lower = (state - upper.astype(f32)).astype(bf16)
        both = dot(query_ref[:, head(h)], jnp.concatenate([upper, lower], 1))
        entered = both[:, :HD] + both[:, HD:]
        result = local_ref[:, head(h)] + entered * grow[:, h : h + 1]
        square = jnp.mean(result * result, -1, keepdims=True)
        out_ref[:, head(h)] = result * lax.rsqrt(square + EPS) * gain_ref[head(h)][None, :]


def finish_kernel(features, attention_ref, square_ref, other_ref, linear_ref, gain_ref, out_ref):
    factor = lax.rsqrt((square_ref[...] + other_ref[...]) / features + EPS)
    factor = dot(factor, jnp.full((8, HD), 0.125, f32), ((0,), (0,)), highest)
    for h in range(HEADS):
        part = attention_ref[:, head(h)].astype(f32) * factor * gain_ref[head(h)][None, :]
        out_ref[:, head(h)] = (part + linear_ref[:, head(h)]).astype(bf16)


def carry_in(place, lh_query, *operands):
    return pl.pallas_call(
        carry_kernel,
        out_shape=jax.ShapeDtypeStruct((ROWS, HEADS * HD), f32),
        in_specs=[SMEM, VMEM] + [VMEM] * len(operands),
        out_specs=VMEM,
        compiler_params=params(14),
        cost_estimate=cost(0.2),
        name="carry",
    )(place, lh_query, *operands)


def finish(features, *operands):
    return pl.pallas_call(
        functools.partial(finish_kernel, features),
        out_shape=jax.ShapeDtypeStruct((ROWS, HEADS * HD), bf16),
        in_specs=[VMEM] * len(operands),
        out_specs=VMEM,
        compiler_params=params(14),
        cost_estimate=cost(0.2),
        name="finish",
    )(*operands)


def body(att_query, att_key, att_value, lh_query, lh_key, lh_value, lh_step, att_gain, lh_gain):
    mine = lax.axis_index("ctx")
    place = mine.reshape(1).astype(jnp.int32)

    def move(value, pairs):
        return lax.ppermute(value, "ctx", pairs)

    every = range(16)
    sibling = [(i, i ^ 1) for i in every]
    sideways = [(i, i ^ 2) for i in every]
    onward = [(i, i + 4) for i in every if i % 2 == 0 and i < 12] + [(i, i + 8) for i in every if i % 2 == 1 and i < 8]
    wrapping = [(i, i + 12) for i in range(4)]
    last_plane = [(i, i + 4) for i in every if i % 2 == 0 and i < 12] + [(i, i + 12) for i in (1, 3)]
    plane_before = [(i, i + 8) for i in every if i % 2 == 1 and i < 8]

    def tied(*values):
        return lax.optimization_barrier(values)

    lh_query, lh_key, lh_value, far_query, att_key, att_value = [
        array
        for array in (lh_query, lh_key, lh_value, att_query, att_key, att_value)
    ]
    lh_step = lh_step.T
    att_query, lh_query, lh_key, lh_value, att_key, att_value = [
        pltpu.with_memory_space_constraint(array, pltpu.HBM)
        for array in (att_query, lh_query, lh_key, lh_value, att_key, att_value)
    ]
    own = beside(att_key, att_value)
    across = move(own, [(i, j) for i, j in sideways if i < 4 or i % 4 < 2])
    wrapped = move(own, wrapping)
    near = move(own, sibling)
    chip = stack(own, near)
    chip, lh_step = tied(chip, lh_step)
    lh_step = pltpu.with_memory_space_constraint(lh_step, pltpu.HBM)
    ring = move(chip, onward)

    local, grow, message = recur(lh_query, lh_key, lh_value, lh_step)

    def where(number, wanted):
        return jnp.where(wanted, number, NEVER)

    def parts(mine):
        return mine // 4, (mine // 2) % 2, mine % 2, mine - mine % 2

    def near_numbers(mine):
        return [where(mine - 1, mine % 2 == 1)]

    def ring_numbers(mine):
        plane, _, core, even = parts(mine)
        one, two = where(even - 4, plane >= 1), where(even - 8, plane >= 2)
        return [jnp.where(core == 0, one, two), jnp.where(core == 0, two, one)]

    def wrapped_numbers(mine):
        plane, _, _, even = parts(mine)
        return [where(even - 12, plane == 3)] * 2

    def across_numbers(mine):
        _, side, _, even = parts(mine)
        return [where(even - 2, side == 1)] * 2

    def middle_numbers(mine):
        return ring_numbers(mine) + wrapped_numbers(mine)

    def last_numbers(mine):
        return ring_numbers(mine) + across_numbers(mine) + wrapped_numbers(mine)

    first_pieces = [(near, 0, ROWS)]
    near_query, *carry = attend(place, att_query, own, None, first_pieces, near_numbers)
    carry, message, across, wrapped = tied(carry, message, across, wrapped)
    first = move(message, sibling)
    wrapped_side = move(across, wrapping)
    (of_chip,) = join(join_cores_kernel, 1, place, message, first)
    ring, of_chip = tied(ring, of_chip)
    level = move(ring, [(i, j) for i, j in sideways if (i % 2 == 0 and i >= 4) or i >= 8])
    other_even = move(of_chip, [(i, j) for i, j in sideways if i % 2 == 0])
    bundle = stack(ring, wrapped)
    bundle_near = move(bundle, sibling)
    middle_pieces = [
        (ring, 0, 2 * ROWS),
        (bundle_near, 0, 2 * ROWS),
        (wrapped, 0, ROWS),
        (bundle_near, 2 * ROWS, ROWS),
    ]
    carry = attend(place, near_query, own, carry, middle_pieces, middle_numbers)

    carry, other_even, across, wrapped_side, level = tied(carry, other_even, across, wrapped_side, level)
    other_odd = move(other_even, [(i, j) for i, j in sibling if i % 2 == 0])
    level_near = move(level, sibling)
    rest = stack(across, wrapped_side)
    rest_near = move(rest, sibling)
    of_plane, other_chip = join(join_sides_kernel, 2, place, of_chip, other_even, other_odd)
    state_behind = move(of_plane, last_plane)
    state_beyond = move(of_plane, plane_before)
    last_pieces = [
        (level, 0, 2 * ROWS),
        (level_near, 0, 2 * ROWS),
        (across, 0, ROWS),
        (rest_near, 0, ROWS),
        (wrapped_side, 0, ROWS),
        (rest_near, ROWS, ROWS),
    ]
    carry, of_plane = tied(carry, of_plane)
    attention, squares = attend(
        place,
        near_query,
        own,
        carry,
        last_pieces,
        last_numbers,
        first_pieces + middle_pieces,
        lambda mine: near_numbers(mine) + middle_numbers(mine),
    )

    def over(value, bit):
        return lax.ppermute(value, "tp", [(i, i ^ bit) for i in range(8)])

    others = [over(squares, bit) for bit in (2, 4, 6)]
    others, state_behind, state_beyond = tied(others, state_behind, state_beyond)
    kept = hand(place, state_behind, state_beyond)
    handed = move(kept, sibling)
    linear = carry_in(place, lh_query, local, grow, kept, handed, other_chip, first, lh_gain)
    squares = squares + others[0] + others[1] + others[2]
    features = HEADS * HD * lax.axis_size("tp")
    return finish(float(features), attention, squares, over(squares, 1), linear, att_gain)


def solution(mesh):
    placed = (P("ctx", "tp"),) * 7 + (P("tp"), P("tp"))
    return jax.shard_map(body, mesh=mesh, in_specs=placed, out_specs=P("ctx", "tp"), check_vma=False)
```

```python
import functools
import math

import jax
import jax.numpy as jnp
from jax import lax
from jax.experimental import pallas as pl
from jax.experimental.pallas import tpu as pltpu
from jax.sharding import PartitionSpec as P

HD = 128
ROWS = 512
HEADS = 6
TILE = 256
EPS = 1e-06
MASKED = -1e30
LOG2E = math.log2(math.e)
SCORE_SCALE = LOG2E / math.sqrt(HD)
SAFE_EXPONENT = 100.0
STATE_ROWS = HEADS * HD + 8
HALF = HEADS // 2
BLOCKS = 2 * ROWS
NEVER = 1 << 20

VMEM = pl.BlockSpec(memory_space=pltpu.VMEM)
SMEM = pl.BlockSpec(memory_space=pltpu.SMEM)
f32 = jnp.float32
bf16 = jnp.bfloat16
highest = lax.Precision.HIGHEST


def dot(a, b, contract=((1,), (0,)), precision=None):
    return lax.dot_general(a, b, (contract, ((), ())), precision=precision, preferred_element_type=f32)


def params(megabytes):
    return pltpu.CompilerParams(vmem_limit_bytes=megabytes << 20)


def cost(us):
    return pl.CostEstimate(flops=int(us * 1e9), bytes_accessed=int(us * 1e6), transcendentals=int(us * 1e6))


def head(h):
    return slice(h * HD, (h + 1) * HD)


def recur_kernel(
    q_hbm, k_hbm, v_hbm, step_ref, local_ref, grow_ref, message_ref, padded
):
    k_ref, q_ref, v_ref = k_hbm, q_hbm, v_hbm
    padded[...] = jnp.full((8, ROWS), 0.5, f32)
    padded[:HEADS, :] = step_ref[...]
    step = padded[...]
    rate = step / (1.0 + step)
    total = -jnp.log(1.0 + step) * LOG2E
    place = lax.broadcasted_iota(jnp.int32, (8, ROWS), 1)
    reach = 1
    while reach < ROWS:
        total = total + jnp.where(place >= reach, pltpu.roll(total, reach, 1), 0.0)
        reach *= 2
    source = jnp.log(rate) * LOG2E - total
    end = total[:, ROWS - 1 : ROWS]
    tail = jnp.exp2(end + source)
    rows = jnp.concatenate([total, tail, jnp.zeros((HD - 16, ROWS), f32)], 0)
    columns = jnp.transpose(rows)
    grow_ref[...] = jnp.exp2(columns)
    message_ref[HEADS * HD :, :] = jnp.broadcast_to(end, (8, HD))
    at_row = lax.broadcasted_iota(jnp.int32, (TILE, TILE), 0)
    at_column = lax.broadcasted_iota(jnp.int32, (TILE, TILE), 1)
    seen = at_column <= at_row
    for h in range(HEADS):
        keys = k_ref[:, head(h)].astype(f32)
        keys = keys * lax.rsqrt(jnp.sum(keys * keys, -1, keepdims=True) + EPS)
        unit = keys.astype(bf16)
        values = v_ref[:, head(h)]
        for a in range(0, ROWS, TILE):
            result = None
            for b in range(0, a + TILE, TILE):
                scores = dot(q_ref[a : a + TILE, head(h)], unit[b : b + TILE], ((1,), (1,)))
                decay = jnp.exp2(columns[a : a + TILE, h : h + 1] + source[h : h + 1, b : b + TILE])
                weights = scores * decay
                if a == b:
                    weights = jnp.where(seen, weights, 0.0)
                part = dot(weights.astype(bf16), values[b : b + TILE])
                result = part if result is None else result + part
            local_ref[a : a + TILE, head(h)] = result
        tailed = (values.astype(f32) * columns[:, 8 + h : 9 + h]).astype(bf16)
        message_ref[head(h), :] = dot(unit, tailed, ((0,), (0,)))


def recur(lh_query, lh_key, lh_value, lh_step):
    return pl.pallas_call(
        recur_kernel,
        out_shape=(
            jax.ShapeDtypeStruct((ROWS, HEADS * HD), f32),
            jax.ShapeDtypeStruct((ROWS, HD), f32),
            jax.ShapeDtypeStruct((STATE_ROWS, HD), f32),
        ),
        in_specs=[VMEM] * 4,
        out_specs=(VMEM,) * 3,
        scratch_shapes=[pltpu.VMEM((8, ROWS), f32)]
,
        compiler_params=params(16),
        cost_estimate=cost(0.2),
        name="recur",
    )(lh_query, lh_key, lh_value, lh_step)


def beside_kernel(key_ref, value_ref, out_ref):
    out_ref[:, :HD] = key_ref[...]
    out_ref[:, HD:] = value_ref[...]


def beside(key, value):
    return pl.pallas_call(
        beside_kernel,
        out_shape=jax.ShapeDtypeStruct((ROWS, 2 * HD), bf16),
        in_specs=[VMEM, VMEM],
        out_specs=VMEM,
        compiler_params=params(14),
        name="beside",
    )(key, value)


def stack_kernel(*refs):
    *parts, out_ref = refs
    at = 0
    for part in parts:
        out_ref[at : at + part.shape[0], :] = part[...]
        at += part.shape[0]


def stack(*parts):
    return pl.pallas_call(
        stack_kernel,
        out_shape=jax.ShapeDtypeStruct((sum(part.shape[0] for part in parts), 2 * HD), bf16),
        in_specs=[VMEM] * len(parts),
        out_specs=VMEM,
        compiler_params=params(14),
        name="stack",
    )(*parts)


def follow(early, late):
    logs = early[1] + late[1]
    states = [jnp.exp2(late[1][h : h + 1, :]) * early[0][h] + late[0][h] for h in range(HEADS)]
    return states, logs


def state_of(ref, wanted=None):
    states = [ref[head(h), :] for h in range(HEADS)]
    logs = ref[HEADS * HD :, :]
    if wanted is None:
        return states, logs
    return [jnp.where(wanted, state, 0.0) for state in states], jnp.where(wanted, logs, 0.0)


def put_state(ref, value):
    for h in range(HEADS):
        ref[head(h), :] = value[0][h]
    ref[HEADS * HD :, :] = value[1]


def select(wanted, one, two):
    return [jnp.where(wanted, a, b) for a, b in zip(one[0], two[0])], jnp.where(wanted, one[1], two[1])


def follow_in_order(own_first, own, other):
    return follow(select(own_first, own, other), select(own_first, other, own))


def split(value):
    upper = value.astype(bf16)
    return jnp.concatenate([upper, (value - upper.astype(f32)).astype(bf16)], 1)


def merge(both):
    return both[:, :HD].astype(f32) + both[:, HD:].astype(f32)


def join_cores_kernel(mine_ref, own_ref, other_ref, blocks_ref, out_ref, message_ref):
    even = mine_ref[0] % 2 == 0
    joined = follow_in_order(even, state_of(own_ref), state_of(other_ref))
    put_state(out_ref, joined)
    message_ref[:BLOCKS, :] = blocks_ref[...]
    for h in range(HALF):
        at = BLOCKS + h * HD
        message_ref[at : at + HD, :] = split(jnp.where(even, joined[0][h], joined[0][HALF + h]))
    logs = jnp.concatenate([joined[1], jnp.zeros((8, HD), f32)], 0)
    message_ref[BLOCKS + HALF * HD :, :] = split(logs)


def join_cores(mine, own, other, blocks):
    return pl.pallas_call(
        join_cores_kernel,
        out_shape=(
            jax.ShapeDtypeStruct((STATE_ROWS, HD), f32),
            jax.ShapeDtypeStruct((BLOCKS + HALF * HD + 16, 2 * HD), bf16),
        ),
        in_specs=[SMEM] + [VMEM] * 3,
        out_specs=(VMEM,) * 2,
        compiler_params=params(14),
        cost_estimate=cost(0.2),
        name="join_cores",
    )(mine, own, other, blocks)


def join_sides_kernel(mine_ref, own_ref, level_ref, level_near_ref, out_ref, other_ref):
    mine = mine_ref[0]
    even = mine % 2 == 0
    states = [None] * HEADS
    for h in range(HALF):
        at = slice(BLOCKS + h * HD, BLOCKS + (h + 1) * HD)
        here, there = merge(level_ref[at, :]), merge(level_near_ref[at, :])
        states[h] = jnp.where(even, here, there)
        states[HALF + h] = jnp.where(even, there, here)
    logs = merge(level_ref[BLOCKS + HALF * HD :, :])[:8, :]
    other = states, logs
    put_state(other_ref, other)
    put_state(out_ref, follow_in_order((mine // 2) % 2 == 0, state_of(own_ref), other))


def join_sides(mine, own, level, level_near):
    return pl.pallas_call(
        join_sides_kernel,
        out_shape=(jax.ShapeDtypeStruct((STATE_ROWS, HD), f32),) * 2,
        in_specs=[SMEM] + [VMEM] * 3,
        out_specs=(VMEM,) * 2,
        compiler_params=params(14),
        cost_estimate=cost(0.2),
        name="join_sides",
    )(mine, own, level, level_near)


def hand_kernel(mine_ref, behind_ref, beyond_ref, out_ref):
    plane, core = mine_ref[0] // 4, mine_ref[0] % 2
    behind = state_of(behind_ref, (plane == 3) | (core == 0))
    beyond = state_of(beyond_ref, (plane >= 2) & (core == 1))
    put_state(out_ref, follow(behind, beyond))


def hand(mine, behind, beyond):
    return pl.pallas_call(
        hand_kernel,
        out_shape=jax.ShapeDtypeStruct((STATE_ROWS, HD), f32),
        in_specs=[SMEM, VMEM, VMEM],
        out_specs=VMEM,
        compiler_params=params(14),
        cost_estimate=cost(0.2),
        name="hand",
    )(mine, behind, beyond)


def attend_kernel(first, last, numbers_of, pieces, kept_numbers_of, kept, mine_ref, query_ref, own_ref, *refs):
    mine = mine_ref[0]
    refs = list(refs)

    def take(count):
        return [refs.pop(0) for _ in range(count)]

    if not first:
        carry_ref, count_ref, top_in_ref = take(3)
    block_refs = [(ref, *piece) for ref, piece in zip(take(len(pieces)), pieces)]
    kept_refs = [(ref, *piece) for ref, piece in zip(take(len(kept)), kept)]
    if last:
        out_ref, square_ref, sums, keys, values, top_ref, tops = refs
    else:
        if first:
            (passed_ref,) = take(1)
            passed_ref[...] = query_ref[...]
        numerator_ref, counted_ref, top_ref, sums, keys, values = refs

    def highest_of(part):
        return jnp.max(jnp.abs(part).reshape(-1, 16, HD), 0)

    def fill(blocks, numbers):
        filled = jnp.int32(0)
        for (block, start, rows), number in zip(blocks, numbers):
            takes = number < mine
            place = filled

            @pl.when(takes)
            def _():
                at = pl.ds(pl.multiple_of(place * ROWS, ROWS), rows)
                block_keys = block[start : start + rows, :HD]
                keys[at, :] = block_keys
                values[at, :HD] = block[start : start + rows, HD:]
                top_ref[16:32, :] = jnp.maximum(top_ref[16:32, :], highest_of(block_keys))

            filled = filled + jnp.where(takes, rows // ROWS, 0)
        return filled

    if first:
        top_ref[16:32, :] = highest_of(own_ref[:, :HD])
        longest = jnp.zeros((ROWS, HD), f32)
        ones = jnp.ones((HD, HD), bf16)
        for h in range(HEADS):
            query = query_ref[:, head(h)].astype(f32)
            longest = jnp.maximum(longest, dot((query * query).astype(bf16), ones))
        top_ref[0:16, :] = jnp.max(longest.reshape(-1, 16, HD), 0).astype(bf16)
    else:
        top_ref[...] = top_in_ref[...]
    values[:, HD:] = jnp.ones((values.shape[0], HD), bf16)
    filled = fill(block_refs, numbers_of(mine))
    sums[...] = jnp.zeros_like(sums)

    def visit(start, count):
        at = pl.ds(pl.multiple_of(start, ROWS), count)
        block_keys = keys[at, :]
        block_values = values[at, :]
        for h in range(HEADS):
            for a in range(0, ROWS, TILE):
                scores = dot(query_ref[a : a + TILE, head(h)], block_keys, ((1,), (1,)))
                weights = jnp.exp2(scores * SCORE_SCALE).astype(bf16)
                sums[h, a : a + TILE, :] += dot(weights, block_values)

    def pair(n, _):
        visit(n * 2 * ROWS, 2 * ROWS)
        return 0

    if not first:
        lax.fori_loop(0, filled // 2, pair, 0)

    if first:

        @pl.when(filled > 0)
        def _():
            visit(0, ROWS)

        at_row = lax.broadcasted_iota(jnp.int32, (TILE, TILE), 0)
        at_column = lax.broadcasted_iota(jnp.int32, (TILE, TILE), 1)
        seen = at_column <= at_row
        values[:ROWS, :HD] = own_ref[:, HD:]
        for h in range(HEADS):
            for a in range(0, ROWS, TILE):
                for b in range(0, a + TILE, TILE):
                    scores = dot(query_ref[a : a + TILE, head(h)], own_ref[b : b + TILE, :HD], ((1,), (1,)))
                    weights = jnp.exp2(scores * SCORE_SCALE)
                    if a == b:
                        weights = jnp.where(seen, weights, 0.0)
                    sums[h, a : a + TILE, :] += dot(weights.astype(bf16), values[b : b + TILE, :])
            numerator_ref[:, head(h)] = sums[h, :, :HD]
            counted_ref[:, h : h + 1] = sums[h, :, HD : HD + 1]
    elif not last:
        for h in range(HEADS):
            numerator_ref[:, head(h)] = sums[h, :, :HD] + carry_ref[:, head(h)]
            counted_ref[:, h : h + 1] = sums[h, :, HD : HD + 1] + count_ref[:, h : h + 1]
    else:
        key_top = jnp.max(top_ref[16:32, :].astype(f32), 0, keepdims=True)
        bound = jnp.max(top_ref[0:16, :].astype(f32)) * jnp.sum(key_top * key_top) * SCORE_SCALE**2
        large = bound * 1.05 > SAFE_EXPONENT * SAFE_EXPONENT

        @pl.when(large)
        def _():
            before = fill(kept_refs + block_refs, kept_numbers_of(mine) + numbers_of(mine))
            at = pl.ds(pl.multiple_of(before * ROWS, ROWS), ROWS)
            keys[at, :] = own_ref[:, :HD]
            values[at, :HD] = own_ref[:, HD:]
            sums[...] = jnp.zeros_like(sums)
            tops[...] = jnp.full_like(tops, MASKED)

            def step(n, _):
                at = pl.ds(pl.multiple_of((n // (2 * HEADS)) * ROWS, ROWS), ROWS)
                h = (n % (2 * HEADS)) // 2
                a = (n % 2) * TILE
                rows = pl.ds(pl.multiple_of(a, TILE), TILE)
                query = query_ref[rows, pl.ds(pl.multiple_of(h * HD, HD), HD)]
                scores = dot(query, keys[at, :], ((1,), (1,))) * SCORE_SCALE
                row = lax.broadcasted_iota(jnp.int32, (TILE, ROWS), 0) + a
                column = lax.broadcasted_iota(jnp.int32, (TILE, ROWS), 1)
                column = column - jnp.where(n // (2 * HEADS) < before, ROWS, 0)
                visible = column <= row
                scores = jnp.where(visible, scores, MASKED)
                old = tops[h, rows, :]
                new = jnp.maximum(old[:, :1], jnp.max(scores, 1, keepdims=True))
                weights = jnp.where(visible, jnp.exp2(scores - new), 0.0).astype(bf16)
                sums[h, rows, :] = sums[h, rows, :] * jnp.exp2(old[:, :1] - new) + dot(weights, values[at, :])
                tops[h, rows, :] = jnp.broadcast_to(new, (TILE, HD))
                return 0

            lax.fori_loop(0, (before + 1) * 2 * HEADS, step, 0)

        squares = jnp.zeros((ROWS, HD), f32)
        for h in range(HEADS):
            count = sums[h, :, HD:] + jnp.where(large, 0.0, count_ref[:, h : h + 1])
            result = (sums[h, :, :HD] + jnp.where(large, 0.0, carry_ref[:, head(h)])) / count
            result = result.astype(bf16)
            out_ref[:, head(h)] = result
            result = result.astype(f32)
            squares = squares + result * result
        square_ref[...] = dot(jnp.ones((8, HD), f32), squares, ((1,), (1,)), highest)


def attend(mine, query, own, carry, blocks, numbers_of, kept=None, kept_numbers_of=None):
    first, last = carry is None, kept is not None
    kept = kept or []
    size = 16 * ROWS if last else sum(rows for _, _, rows in blocks)
    operands = [query, own] + list(carry or []) + [block for block, _, _ in blocks + kept]
    top = (32, HD)
    scratch = [
        pltpu.VMEM((HEADS, ROWS, 2 * HD), f32),
        pltpu.VMEM((size, HD), bf16),
        pltpu.VMEM((size, 2 * HD), bf16),
    ]
    if last:
        out_shape = (
            jax.ShapeDtypeStruct((ROWS, HEADS * HD), bf16),
            jax.ShapeDtypeStruct((8, ROWS), f32),
        )
        scratch += [pltpu.VMEM(top, bf16), pltpu.VMEM((HEADS, ROWS, HD), f32)]
    else:
        out_shape = (
            jax.ShapeDtypeStruct((ROWS, HEADS * HD), f32),
            jax.ShapeDtypeStruct((ROWS, HD), f32),
            jax.ShapeDtypeStruct(top, bf16),
        )
        if first:
            out_shape = (jax.ShapeDtypeStruct((ROWS, HEADS * HD), bf16),) + out_shape
    return pl.pallas_call(
        functools.partial(
            attend_kernel,
            first,
            last,
            numbers_of,
            [block[1:] for block in blocks],
            kept_numbers_of,
            [block[1:] for block in kept],
        ),
        out_shape=out_shape,
        in_specs=[SMEM] + [VMEM] * len(operands),
        out_specs=(VMEM,) * len(out_shape),
        scratch_shapes=scratch,
        compiler_params=params(20),
        cost_estimate=cost(0.2),
        name="attend_first" if first else "attend_last" if last else "attend_middle",
    )(mine, *operands)


def carry_kernel(
    mine_ref,
    query_hbm,
    local_ref,
    grow_ref,
    kept_ref,
    handed_ref,
    chip_ref,
    core_ref,
    gain_ref,
    out_ref,
):
    mine = mine_ref[0]
    query_ref = query_hbm
    plane, side, core = mine // 4, (mine // 2) % 2, mine % 2
    kept, handed = state_of(kept_ref), state_of(handed_ref)

    def pick(one, two, wanted):
        states = [jnp.where(wanted, jnp.where(core == 0, a, b), 0.0) for a, b in zip(one[0], two[0])]
        return states, jnp.where(wanted, jnp.where(core == 0, one[1], two[1]), 0.0)

    entering = pick(handed, kept, plane >= 2)
    entering = follow(entering, pick(kept, handed, plane >= 1))
    entering = follow(entering, state_of(chip_ref, side == 1))
    entering = follow(entering, state_of(core_ref, core == 1))
    grow = grow_ref[...]
    for h in range(HEADS):
        state = entering[0][h]
        upper = state.astype(bf16)
        lower = (state - upper.astype(f32)).astype(bf16)
        both = dot(query_ref[:, head(h)], jnp.concatenate([upper, lower], 1))
        entered = both[:, :HD] + both[:, HD:]
        result = local_ref[:, head(h)] + entered * grow[:, h : h + 1]
        square = jnp.mean(result * result, -1, keepdims=True)
        out_ref[:, head(h)] = result * lax.rsqrt(square + EPS) * gain_ref[head(h)][None, :]


def finish_kernel(features, attention_ref, square_ref, other_ref, linear_ref, gain_ref, out_ref):
    factor = lax.rsqrt((square_ref[...] + other_ref[...]) / features + EPS)
    factor = dot(factor, jnp.full((8, HD), 0.125, f32), ((0,), (0,)), highest)
    for h in range(HEADS):
        part = attention_ref[:, head(h)].astype(f32) * factor * gain_ref[head(h)][None, :]
        out_ref[:, head(h)] = (part + linear_ref[:, head(h)]).astype(bf16)


def carry_in(place, lh_query, *operands):
    return pl.pallas_call(
        carry_kernel,
        out_shape=jax.ShapeDtypeStruct((ROWS, HEADS * HD), f32),
        in_specs=[SMEM, VMEM] + [VMEM] * len(operands),
        out_specs=VMEM,
        compiler_params=params(14),
        cost_estimate=cost(0.2),
        name="carry",
    )(place, lh_query, *operands)


def finish(features, *operands):
    return pl.pallas_call(
        functools.partial(finish_kernel, features),
        out_shape=jax.ShapeDtypeStruct((ROWS, HEADS * HD), bf16),
        in_specs=[VMEM] * len(operands),
        out_specs=VMEM,
        compiler_params=params(14),
        cost_estimate=cost(0.2),
        name="finish",
    )(*operands)


def body(att_query, att_key, att_value, lh_query, lh_key, lh_value, lh_step, att_gain, lh_gain):
    mine = lax.axis_index("ctx")
    place = mine.reshape(1).astype(jnp.int32)

    def move(value, pairs):
        return lax.ppermute(value, "ctx", pairs)

    every = range(16)
    sibling = [(i, i ^ 1) for i in every]
    sideways = [(i, i ^ 2) for i in every]
    onward = [(i, i + 4) for i in every if i % 2 == 0 and i < 12] + [(i, i + 8) for i in every if i % 2 == 1 and i < 8]
    wrapping = [(i, i + 12) for i in range(4)]
    last_plane = [(i, i + 4) for i in every if i % 2 == 0 and i < 12] + [(i, i + 12) for i in (1, 3)]
    plane_before = [(i, i + 8) for i in every if i % 2 == 1 and i < 8]

    def tied(*values):
        return lax.optimization_barrier(values)

    lh_query, lh_key, lh_value, far_query, att_key, att_value = [
        array
        for array in (lh_query, lh_key, lh_value, att_query, att_key, att_value)
    ]
    lh_step = lh_step.T
    att_query, lh_query, lh_key, lh_value, att_key, att_value = [
        pltpu.with_memory_space_constraint(array, pltpu.HBM)
        for array in (att_query, lh_query, lh_key, lh_value, att_key, att_value)
    ]
    own = beside(att_key, att_value)
    across = move(own, [(i, j) for i, j in sideways if i < 4 or i % 4 < 2])
    wrapped = move(own, wrapping)
    near = move(own, sibling)
    chip = stack(own, near)
    chip, lh_step = tied(chip, lh_step)
    lh_step = pltpu.with_memory_space_constraint(lh_step, pltpu.HBM)
    ring = move(chip, onward)

    local, grow, message = recur(lh_query, lh_key, lh_value, lh_step)

    def where(number, wanted):
        return jnp.where(wanted, number, NEVER)

    def parts(mine):
        return mine // 4, (mine // 2) % 2, mine % 2, mine - mine % 2

    def near_numbers(mine):
        return [where(mine - 1, mine % 2 == 1)]

    def ring_numbers(mine):
        plane, _, core, even = parts(mine)
        one, two = where(even - 4, plane >= 1), where(even - 8, plane >= 2)
        return [jnp.where(core == 0, one, two), jnp.where(core == 0, two, one)]

    def wrapped_numbers(mine):
        plane, _, _, even = parts(mine)
        return [where(even - 12, plane == 3)] * 2

    def across_numbers(mine):
        _, side, _, even = parts(mine)
        return [where(even - 2, side == 1)] * 2

    def middle_numbers(mine):
        return ring_numbers(mine) + wrapped_numbers(mine)

    def last_numbers(mine):
        return ring_numbers(mine) + across_numbers(mine) + wrapped_numbers(mine)

    first_pieces = [(near, 0, ROWS)]
    near_query, *carry = attend(place, att_query, own, None, first_pieces, near_numbers)
    first = move(message, sibling)
    carry, first = tied(carry, first)
    of_chip, leveled = join_cores(place, message, first, ring)
    level = move(leveled, sideways)
    of_chip, wrapped, across = tied(of_chip, wrapped, across)
    wrapped_side = move(across, wrapping)
    bundle = stack(ring, wrapped)
    bundle_near = move(bundle, sibling)
    middle_pieces = [
        (ring, 0, 2 * ROWS),
        (bundle_near, 0, 2 * ROWS),
        (wrapped, 0, ROWS),
        (bundle_near, 2 * ROWS, ROWS),
    ]
    carry = attend(place, near_query, own, carry, middle_pieces, middle_numbers)

    carry, across, wrapped_side, level = tied(carry, across, wrapped_side, level)
    level_near = move(level, sibling)
    rest = stack(across, wrapped_side)
    rest_near = move(rest, sibling)
    of_plane, other_chip = join_sides(place, of_chip, level, level_near)
    state_behind = move(of_plane, last_plane)
    state_beyond = move(of_plane, plane_before)
    last_pieces = [
        (level, 0, 2 * ROWS),
        (level_near, 0, 2 * ROWS),
        (across, 0, ROWS),
        (rest_near, 0, ROWS),
        (wrapped_side, 0, ROWS),
        (rest_near, ROWS, ROWS),
    ]
    carry, of_plane = tied(carry, of_plane)
    attention, squares = attend(
        place,
        near_query,
        own,
        carry,
        last_pieces,
        last_numbers,
        first_pieces + middle_pieces,
        lambda mine: near_numbers(mine) + middle_numbers(mine),
    )

    def over(value, bit):
        return lax.ppermute(value, "tp", [(i, i ^ bit) for i in range(8)])

    squares, state_behind, state_beyond = tied(squares, state_behind, state_beyond)
    others = [over(squares, bit) for bit in (2, 4, 6)]
    kept = hand(place, state_behind, state_beyond)
    handed = move(kept, sibling)
    linear = carry_in(place, lh_query, local, grow, kept, handed, other_chip, first, lh_gain)
    others, linear = tied(others, linear)
    squares = squares + others[0] + others[1] + others[2]
    features = HEADS * HD * lax.axis_size("tp")
    return finish(float(features), attention, squares, over(squares, 1), linear, att_gain)


def solution(mesh):
    placed = (P("ctx", "tp"),) * 7 + (P("tp"), P("tp"))
    return jax.shard_map(body, mesh=mesh, in_specs=placed, out_specs=P("ctx", "tp"), check_vma=False)
```

```python
import functools
import math

import jax
import jax.numpy as jnp
from jax import lax
from jax.experimental import pallas as pl
from jax.experimental.pallas import tpu as pltpu
from jax.sharding import PartitionSpec as P

HD = 128
ROWS = 512
HEADS = 6
TILE = 256
EPS = 1e-06
MASKED = -1e30
LOG2E = math.log2(math.e)
SCORE_SCALE = LOG2E / math.sqrt(HD)
SAFE_EXPONENT = 100.0
STATE_ROWS = HEADS * HD + 8
HALF = HEADS // 2
BLOCKS = 2 * ROWS
NEVER = 1 << 20

VMEM = pl.BlockSpec(memory_space=pltpu.VMEM)
SMEM = pl.BlockSpec(memory_space=pltpu.SMEM)
f32 = jnp.float32
bf16 = jnp.bfloat16
highest = lax.Precision.HIGHEST


def dot(a, b, contract=((1,), (0,)), precision=None):
    return lax.dot_general(a, b, (contract, ((), ())), precision=precision, preferred_element_type=f32)


def params(megabytes):
    return pltpu.CompilerParams(vmem_limit_bytes=megabytes << 20)


def cost(us):
    return pl.CostEstimate(flops=int(us * 1e9), bytes_accessed=int(us * 1e6), transcendentals=int(us * 1e6))


def head(h):
    return slice(h * HD, (h + 1) * HD)


def recur_kernel(
    q_hbm, k_hbm, v_hbm, step_ref, local_ref, grow_ref, message_ref, padded
):
    k_ref, q_ref, v_ref = k_hbm, q_hbm, v_hbm
    padded[...] = jnp.full((8, ROWS), 0.5, f32)
    padded[:HEADS, :] = step_ref[...]
    step = padded[...]
    rate = step / (1.0 + step)
    total = -jnp.log(1.0 + step) * LOG2E
    place = lax.broadcasted_iota(jnp.int32, (8, ROWS), 1)
    reach = 1
    while reach < ROWS:
        total = total + jnp.where(place >= reach, pltpu.roll(total, reach, 1), 0.0)
        reach *= 2
    source = jnp.log(rate) * LOG2E - total
    end = total[:, ROWS - 1 : ROWS]
    tail = jnp.exp2(end + source)
    rows = jnp.concatenate([total, tail, jnp.zeros((HD - 16, ROWS), f32)], 0)
    columns = jnp.transpose(rows)
    grow_ref[...] = jnp.exp2(columns)
    message_ref[HEADS * HD :, :] = jnp.broadcast_to(end, (8, HD))
    at_row = lax.broadcasted_iota(jnp.int32, (TILE, TILE), 0)
    at_column = lax.broadcasted_iota(jnp.int32, (TILE, TILE), 1)
    seen = at_column <= at_row
    for h in range(HEADS):
        keys = k_ref[:, head(h)].astype(f32)
        keys = keys * lax.rsqrt(jnp.sum(keys * keys, -1, keepdims=True) + EPS)
        unit = keys.astype(bf16)
        values = v_ref[:, head(h)]
        for a in range(0, ROWS, TILE):
            result = None
            for b in range(0, a + TILE, TILE):
                scores = dot(q_ref[a : a + TILE, head(h)], unit[b : b + TILE], ((1,), (1,)))
                decay = jnp.exp2(columns[a : a + TILE, h : h + 1] + source[h : h + 1, b : b + TILE])
                weights = scores * decay
                if a == b:
                    weights = jnp.where(seen, weights, 0.0)
                part = dot(weights.astype(bf16), values[b : b + TILE])
                result = part if result is None else result + part
            local_ref[a : a + TILE, head(h)] = result
        tailed = (values.astype(f32) * columns[:, 8 + h : 9 + h]).astype(bf16)
        message_ref[head(h), :] = dot(unit, tailed, ((0,), (0,)))


def recur(lh_query, lh_key, lh_value, lh_step):
    return pl.pallas_call(
        recur_kernel,
        out_shape=(
            jax.ShapeDtypeStruct((ROWS, HEADS * HD), f32),
            jax.ShapeDtypeStruct((ROWS, HD), f32),
            jax.ShapeDtypeStruct((STATE_ROWS, HD), f32),
        ),
        in_specs=[VMEM] * 4,
        out_specs=(VMEM,) * 3,
        scratch_shapes=[pltpu.VMEM((8, ROWS), f32)]
,
        compiler_params=params(16),
        cost_estimate=cost(0.2),
        name="recur",
    )(lh_query, lh_key, lh_value, lh_step)


def beside_kernel(key_ref, value_ref, out_ref):
    out_ref[:, :HD] = key_ref[...]
    out_ref[:, HD:] = value_ref[...]


def beside(key, value):
    return pl.pallas_call(
        beside_kernel,
        out_shape=jax.ShapeDtypeStruct((ROWS, 2 * HD), bf16),
        in_specs=[VMEM, VMEM],
        out_specs=VMEM,
        compiler_params=params(14),
        name="beside",
    )(key, value)


def stack_kernel(*refs):
    *parts, out_ref = refs
    at = 0
    for part in parts:
        out_ref[at : at + part.shape[0], :] = part[...]
        at += part.shape[0]


def stack(*parts):
    return pl.pallas_call(
        stack_kernel,
        out_shape=jax.ShapeDtypeStruct((sum(part.shape[0] for part in parts), 2 * HD), bf16),
        in_specs=[VMEM] * len(parts),
        out_specs=VMEM,
        compiler_params=params(14),
        name="stack",
    )(*parts)


def follow(early, late):
    logs = early[1] + late[1]
    states = [jnp.exp2(late[1][h : h + 1, :]) * early[0][h] + late[0][h] for h in range(HEADS)]
    return states, logs


def state_of(ref, wanted=None):
    states = [ref[head(h), :] for h in range(HEADS)]
    logs = ref[HEADS * HD :, :]
    if wanted is None:
        return states, logs
    return [jnp.where(wanted, state, 0.0) for state in states], jnp.where(wanted, logs, 0.0)


def put_state(ref, value):
    for h in range(HEADS):
        ref[head(h), :] = value[0][h]
    ref[HEADS * HD :, :] = value[1]


def select(wanted, one, two):
    return [jnp.where(wanted, a, b) for a, b in zip(one[0], two[0])], jnp.where(wanted, one[1], two[1])


def follow_in_order(own_first, own, other):
    return follow(select(own_first, own, other), select(own_first, other, own))


def split(value):
    upper = value.astype(bf16)
    return jnp.concatenate([upper, (value - upper.astype(f32)).astype(bf16)], 1)


def merge(both):
    return both[:, :HD].astype(f32) + both[:, HD:].astype(f32)


def join_cores_kernel(mine_ref, own_ref, other_ref, blocks_ref, out_ref, message_ref):
    even = mine_ref[0] % 2 == 0
    joined = follow_in_order(even, state_of(own_ref), state_of(other_ref))
    put_state(out_ref, joined)
    message_ref[:BLOCKS, :] = blocks_ref[...]
    for h in range(HALF):
        at = BLOCKS + h * HD
        message_ref[at : at + HD, :] = split(jnp.where(even, joined[0][h], joined[0][HALF + h]))
    logs = jnp.concatenate([joined[1], jnp.zeros((8, HD), f32)], 0)
    message_ref[BLOCKS + HALF * HD :, :] = split(logs)


def join_cores(mine, own, other, blocks):
    return pl.pallas_call(
        join_cores_kernel,
        out_shape=(
            jax.ShapeDtypeStruct((STATE_ROWS, HD), f32),
            jax.ShapeDtypeStruct((BLOCKS + HALF * HD + 16, 2 * HD), bf16),
        ),
        in_specs=[SMEM] + [VMEM] * 3,
        out_specs=(VMEM,) * 2,
        compiler_params=params(14),
        cost_estimate=cost(0.2),
        name="join_cores",
    )(mine, own, other, blocks)


def join_sides_kernel(mine_ref, own_ref, level_ref, level_near_ref, out_ref, other_ref):
    mine = mine_ref[0]
    even = mine % 2 == 0
    states = [None] * HEADS
    for h in range(HALF):
        at = slice(BLOCKS + h * HD, BLOCKS + (h + 1) * HD)
        here, there = merge(level_ref[at, :]), merge(level_near_ref[at, :])
        states[h] = jnp.where(even, here, there)
        states[HALF + h] = jnp.where(even, there, here)
    logs = merge(level_ref[BLOCKS + HALF * HD :, :])[:8, :]
    other = states, logs
    put_state(other_ref, other)
    put_state(out_ref, follow_in_order((mine // 2) % 2 == 0, state_of(own_ref), other))


def join_sides(mine, own, level, level_near):
    return pl.pallas_call(
        join_sides_kernel,
        out_shape=(jax.ShapeDtypeStruct((STATE_ROWS, HD), f32),) * 2,
        in_specs=[SMEM] + [VMEM] * 3,
        out_specs=(VMEM,) * 2,
        compiler_params=params(14),
        cost_estimate=cost(0.2),
        name="join_sides",
    )(mine, own, level, level_near)


def hand_kernel(mine_ref, behind_ref, beyond_ref, out_ref):
    plane, core = mine_ref[0] // 4, mine_ref[0] % 2
    behind = state_of(behind_ref, (plane == 3) | (core == 0))
    beyond = state_of(beyond_ref, (plane >= 2) & (core == 1))
    put_state(out_ref, follow(behind, beyond))


def hand(mine, behind, beyond):
    return pl.pallas_call(
        hand_kernel,
        out_shape=jax.ShapeDtypeStruct((STATE_ROWS, HD), f32),
        in_specs=[SMEM, VMEM, VMEM],
        out_specs=VMEM,
        compiler_params=params(14),
        cost_estimate=cost(0.2),
        name="hand",
    )(mine, behind, beyond)


def attend_kernel(first, last, numbers_of, pieces, kept_numbers_of, kept, mine_ref, query_ref, own_ref, *refs):
    mine = mine_ref[0]
    refs = list(refs)

    def take(count):
        return [refs.pop(0) for _ in range(count)]

    if not first:
        carry_ref, count_ref, top_in_ref = take(3)
    block_refs = [(ref, *piece) for ref, piece in zip(take(len(pieces)), pieces)]
    kept_refs = [(ref, *piece) for ref, piece in zip(take(len(kept)), kept)]
    if last:
        out_ref, square_ref, sums, keys, values, top_ref, tops = refs
    else:
        if first:
            (passed_ref,) = take(1)
            passed_ref[...] = query_ref[...]
        numerator_ref, counted_ref, top_ref, sums, keys, values = refs

    def highest_of(part):
        return jnp.max(jnp.abs(part).reshape(-1, 16, HD), 0)

    def fill(blocks, numbers):
        filled = jnp.int32(0)
        for (block, start, rows), number in zip(blocks, numbers):
            takes = number < mine
            place = filled

            @pl.when(takes)
            def _():
                at = pl.ds(pl.multiple_of(place * ROWS, ROWS), rows)
                block_keys = block[start : start + rows, :HD]
                keys[at, :] = block_keys
                values[at, :HD] = block[start : start + rows, HD:]
                top_ref[16:32, :] = jnp.maximum(top_ref[16:32, :], highest_of(block_keys))

            filled = filled + jnp.where(takes, rows // ROWS, 0)
        return filled

    if first:
        top_ref[16:32, :] = highest_of(own_ref[:, :HD])
        longest = jnp.zeros((ROWS, HD), f32)
        ones = jnp.ones((HD, HD), bf16)
        for h in range(HEADS):
            query = query_ref[:, head(h)].astype(f32)
            longest = jnp.maximum(longest, dot((query * query).astype(bf16), ones))
        top_ref[0:16, :] = jnp.max(longest.reshape(-1, 16, HD), 0).astype(bf16)
    else:
        top_ref[...] = top_in_ref[...]
    values[:, HD:] = jnp.ones((values.shape[0], HD), bf16)
    filled = fill(block_refs, numbers_of(mine))
    sums[...] = jnp.zeros_like(sums)

    def visit(start, count):
        at = pl.ds(pl.multiple_of(start, ROWS), count)
        block_keys = keys[at, :]
        block_values = values[at, :]
        for h in range(HEADS):
            for a in range(0, ROWS, TILE):
                scores = dot(query_ref[a : a + TILE, head(h)], block_keys, ((1,), (1,)))
                weights = jnp.exp2(scores * SCORE_SCALE).astype(bf16)
                sums[h, a : a + TILE, :] += dot(weights, block_values)

    def pair(n, _):
        visit(n * 2 * ROWS, 2 * ROWS)
        return 0

    if not first:
        lax.fori_loop(0, filled // 2, pair, 0)

    if first:

        @pl.when(filled > 0)
        def _():
            visit(0, ROWS)

        at_row = lax.broadcasted_iota(jnp.int32, (TILE, TILE), 0)
        at_column = lax.broadcasted_iota(jnp.int32, (TILE, TILE), 1)
        seen = at_column <= at_row
        values[:ROWS, :HD] = own_ref[:, HD:]
        for h in range(HEADS):
            for a in range(0, ROWS, TILE):
                for b in range(0, a + TILE, TILE):
                    scores = dot(query_ref[a : a + TILE, head(h)], own_ref[b : b + TILE, :HD], ((1,), (1,)))
                    weights = jnp.exp2(scores * SCORE_SCALE)
                    if a == b:
                        weights = jnp.where(seen, weights, 0.0)
                    sums[h, a : a + TILE, :] += dot(weights.astype(bf16), values[b : b + TILE, :])
            numerator_ref[:, head(h)] = sums[h, :, :HD]
            counted_ref[:, h : h + 1] = sums[h, :, HD : HD + 1]
    elif not last:
        for h in range(HEADS):
            numerator_ref[:, head(h)] = sums[h, :, :HD] + carry_ref[:, head(h)]
            counted_ref[:, h : h + 1] = sums[h, :, HD : HD + 1] + count_ref[:, h : h + 1]
    else:
        key_top = jnp.max(top_ref[16:32, :].astype(f32), 0, keepdims=True)
        bound = jnp.max(top_ref[0:16, :].astype(f32)) * jnp.sum(key_top * key_top) * SCORE_SCALE**2
        large = bound * 1.05 > SAFE_EXPONENT * SAFE_EXPONENT

        @pl.when(large)
        def _():
            before = fill(kept_refs + block_refs, kept_numbers_of(mine) + numbers_of(mine))
            at = pl.ds(pl.multiple_of(before * ROWS, ROWS), ROWS)
            keys[at, :] = own_ref[:, :HD]
            values[at, :HD] = own_ref[:, HD:]
            sums[...] = jnp.zeros_like(sums)
            tops[...] = jnp.full_like(tops, MASKED)

            def step(n, _):
                at = pl.ds(pl.multiple_of((n // (2 * HEADS)) * ROWS, ROWS), ROWS)
                h = (n % (2 * HEADS)) // 2
                a = (n % 2) * TILE
                rows = pl.ds(pl.multiple_of(a, TILE), TILE)
                query = query_ref[rows, pl.ds(pl.multiple_of(h * HD, HD), HD)]
                scores = dot(query, keys[at, :], ((1,), (1,))) * SCORE_SCALE
                row = lax.broadcasted_iota(jnp.int32, (TILE, ROWS), 0) + a
                column = lax.broadcasted_iota(jnp.int32, (TILE, ROWS), 1)
                column = column - jnp.where(n // (2 * HEADS) < before, ROWS, 0)
                visible = column <= row
                scores = jnp.where(visible, scores, MASKED)
                old = tops[h, rows, :]
                new = jnp.maximum(old[:, :1], jnp.max(scores, 1, keepdims=True))
                weights = jnp.where(visible, jnp.exp2(scores - new), 0.0).astype(bf16)
                sums[h, rows, :] = sums[h, rows, :] * jnp.exp2(old[:, :1] - new) + dot(weights, values[at, :])
                tops[h, rows, :] = jnp.broadcast_to(new, (TILE, HD))
                return 0

            lax.fori_loop(0, (before + 1) * 2 * HEADS, step, 0)

        squares = jnp.zeros((ROWS, HD), f32)
        for h in range(HEADS):
            count = sums[h, :, HD:] + jnp.where(large, 0.0, count_ref[:, h : h + 1])
            result = (sums[h, :, :HD] + jnp.where(large, 0.0, carry_ref[:, head(h)])) / count
            result = result.astype(bf16)
            out_ref[:, head(h)] = result
            result = result.astype(f32)
            squares = squares + result * result
        square_ref[...] = dot(jnp.ones((8, HD), f32), squares, ((1,), (1,)), highest)


def attend(mine, query, own, carry, blocks, numbers_of, kept=None, kept_numbers_of=None):
    first, last = carry is None, kept is not None
    kept = kept or []
    size = 16 * ROWS if last else sum(rows for _, _, rows in blocks)
    operands = [query, own] + list(carry or []) + [block for block, _, _ in blocks + kept]
    top = (32, HD)
    scratch = [
        pltpu.VMEM((HEADS, ROWS, 2 * HD), f32),
        pltpu.VMEM((size, HD), bf16),
        pltpu.VMEM((size, 2 * HD), bf16),
    ]
    if last:
        out_shape = (
            jax.ShapeDtypeStruct((ROWS, HEADS * HD), bf16),
            jax.ShapeDtypeStruct((8, ROWS), f32),
        )
        scratch += [pltpu.VMEM(top, bf16), pltpu.VMEM((HEADS, ROWS, HD), f32)]
    else:
        out_shape = (
            jax.ShapeDtypeStruct((ROWS, HEADS * HD), f32),
            jax.ShapeDtypeStruct((ROWS, HD), f32),
            jax.ShapeDtypeStruct(top, bf16),
        )
        if first:
            out_shape = (jax.ShapeDtypeStruct((ROWS, HEADS * HD), bf16),) + out_shape
    return pl.pallas_call(
        functools.partial(
            attend_kernel,
            first,
            last,
            numbers_of,
            [block[1:] for block in blocks],
            kept_numbers_of,
            [block[1:] for block in kept],
        ),
        out_shape=out_shape,
        in_specs=[SMEM] + [VMEM] * len(operands),
        out_specs=(VMEM,) * len(out_shape),
        scratch_shapes=scratch,
        compiler_params=params(20),
        cost_estimate=cost(0.2),
        name="attend_first" if first else "attend_last" if last else "attend_middle",
    )(mine, *operands)


def carry_kernel(
    mine_ref,
    query_hbm,
    local_ref,
    grow_ref,
    kept_ref,
    handed_ref,
    chip_ref,
    core_ref,
    gain_ref,
    out_ref,
):
    mine = mine_ref[0]
    query_ref = query_hbm
    plane, side, core = mine // 4, (mine // 2) % 2, mine % 2
    kept, handed = state_of(kept_ref), state_of(handed_ref)

    def pick(one, two, wanted):
        states = [jnp.where(wanted, jnp.where(core == 0, a, b), 0.0) for a, b in zip(one[0], two[0])]
        return states, jnp.where(wanted, jnp.where(core == 0, one[1], two[1]), 0.0)

    entering = pick(handed, kept, plane >= 2)
    entering = follow(entering, pick(kept, handed, plane >= 1))
    entering = follow(entering, state_of(chip_ref, side == 1))
    entering = follow(entering, state_of(core_ref, core == 1))
    grow = grow_ref[...]
    for h in range(HEADS):
        state = entering[0][h]
        upper = state.astype(bf16)
        lower = (state - upper.astype(f32)).astype(bf16)
        both = dot(query_ref[:, head(h)], jnp.concatenate([upper, lower], 1))
        entered = both[:, :HD] + both[:, HD:]
        result = local_ref[:, head(h)] + entered * grow[:, h : h + 1]
        square = jnp.mean(result * result, -1, keepdims=True)
        out_ref[:, head(h)] = result * lax.rsqrt(square + EPS) * gain_ref[head(h)][None, :]


def finish_kernel(features, attention_ref, square_ref, other_ref, linear_ref, gain_ref, out_ref):
    factor = lax.rsqrt((square_ref[...] + other_ref[...]) / features + EPS)
    factor = dot(factor, jnp.full((8, HD), 0.125, f32), ((0,), (0,)), highest)
    for h in range(HEADS):
        part = attention_ref[:, head(h)].astype(f32) * factor * gain_ref[head(h)][None, :]
        out_ref[:, head(h)] = (part + linear_ref[:, head(h)]).astype(bf16)


def carry_in(place, lh_query, *operands):
    return pl.pallas_call(
        carry_kernel,
        out_shape=jax.ShapeDtypeStruct((ROWS, HEADS * HD), f32),
        in_specs=[SMEM, VMEM] + [VMEM] * len(operands),
        out_specs=VMEM,
        compiler_params=params(14),
        cost_estimate=cost(0.2),
        name="carry",
    )(place, lh_query, *operands)


def finish(features, *operands):
    return pl.pallas_call(
        functools.partial(finish_kernel, features),
        out_shape=jax.ShapeDtypeStruct((ROWS, HEADS * HD), bf16),
        in_specs=[VMEM] * len(operands),
        out_specs=VMEM,
        compiler_params=params(14),
        cost_estimate=cost(0.2),
        name="finish",
    )(*operands)


def body(att_query, att_key, att_value, lh_query, lh_key, lh_value, lh_step, att_gain, lh_gain):
    mine = lax.axis_index("ctx")
    place = mine.reshape(1).astype(jnp.int32)

    def move(value, pairs):
        return lax.ppermute(value, "ctx", pairs)

    every = range(16)
    sibling = [(i, i ^ 1) for i in every]
    sideways = [(i, i ^ 2) for i in every]
    onward = [(i, i + 4) for i in every if i % 2 == 0 and i < 12] + [(i, i + 8) for i in every if i % 2 == 1 and i < 8]
    wrapping = [(i, i + 12) for i in range(4)]
    last_plane = [(i, i + 4) for i in every if i % 2 == 0 and i < 12] + [(i, i + 12) for i in (1, 3)]
    plane_before = [(i, i + 8) for i in every if i % 2 == 1 and i < 8]

    def tied(*values):
        return lax.optimization_barrier(values)

    lh_query, lh_key, lh_value, far_query, att_key, att_value = [
        array
        for array in (lh_query, lh_key, lh_value, att_query, att_key, att_value)
    ]
    lh_step = lh_step.T
    att_query, lh_query, lh_key, lh_value, att_key, att_value = [
        pltpu.with_memory_space_constraint(array, pltpu.HBM)
        for array in (att_query, lh_query, lh_key, lh_value, att_key, att_value)
    ]
    own = beside(att_key, att_value)
    across = move(own, [(i, j) for i, j in sideways if i < 4 or i % 4 < 2])
    wrapped = move(own, wrapping)
    near = move(own, sibling)
    chip = stack(own, near)
    chip, lh_step = tied(chip, lh_step)
    lh_step = pltpu.with_memory_space_constraint(lh_step, pltpu.HBM)
    ring = move(chip, onward)

    local, grow, message = recur(lh_query, lh_key, lh_value, lh_step)

    def where(number, wanted):
        return jnp.where(wanted, number, NEVER)

    def parts(mine):
        return mine // 4, (mine // 2) % 2, mine % 2, mine - mine % 2

    def near_numbers(mine):
        return [where(mine - 1, mine % 2 == 1)]

    def ring_numbers(mine):
        plane, _, core, even = parts(mine)
        one, two = where(even - 4, plane >= 1), where(even - 8, plane >= 2)
        return [jnp.where(core == 0, one, two), jnp.where(core == 0, two, one)]

    def wrapped_numbers(mine):
        plane, _, _, even = parts(mine)
        return [where(even - 12, plane == 3)] * 2

    def across_numbers(mine):
        _, side, _, even = parts(mine)
        return [where(even - 2, side == 1)] * 2

    def middle_numbers(mine):
        return ring_numbers(mine) + wrapped_numbers(mine)

    def last_numbers(mine):
        return ring_numbers(mine) + across_numbers(mine) + wrapped_numbers(mine)

    first_pieces = [(near, 0, ROWS)]
    near_query, *carry = attend(place, att_query, own, None, first_pieces, near_numbers)
    carry, message, across, wrapped = tied(carry, message, across, wrapped)
    first = move(message, sibling)
    of_chip, leveled = join_cores(place, message, first, ring)
    level = move(leveled, sideways)
    wrapped_side = move(across, wrapping)
    bundle = stack(ring, wrapped)
    bundle_near = move(bundle, sibling)
    middle_pieces = [
        (ring, 0, 2 * ROWS),
        (bundle_near, 0, 2 * ROWS),
        (wrapped, 0, ROWS),
        (bundle_near, 2 * ROWS, ROWS),
    ]
    carry = attend(place, near_query, own, carry, middle_pieces, middle_numbers)

    carry, across, wrapped_side, level = tied(carry, across, wrapped_side, level)
    level_near = move(level, sibling)
    rest = stack(across, wrapped_side)
    rest_near = move(rest, sibling)
    of_plane, other_chip = join_sides(place, of_chip, level, level_near)
    state_behind = move(of_plane, last_plane)
    state_beyond = move(of_plane, plane_before)
    last_pieces = [
        (level, 0, 2 * ROWS),
        (level_near, 0, 2 * ROWS),
        (across, 0, ROWS),
        (rest_near, 0, ROWS),
        (wrapped_side, 0, ROWS),
        (rest_near, ROWS, ROWS),
    ]
    carry, of_plane = tied(carry, of_plane)
    attention, squares = attend(
        place,
        near_query,
        own,
        carry,
        last_pieces,
        last_numbers,
        first_pieces + middle_pieces,
        lambda mine: near_numbers(mine) + middle_numbers(mine),
    )

    def over(value, bit):
        return lax.ppermute(value, "tp", [(i, i ^ bit) for i in range(8)])

    squares, state_behind, state_beyond = tied(squares, state_behind, state_beyond)
    others = [over(squares, bit) for bit in (2, 4, 6)]
    kept = hand(place, state_behind, state_beyond)
    handed = move(kept, sibling)
    linear = carry_in(place, lh_query, local, grow, kept, handed, other_chip, first, lh_gain)
    others, linear = tied(others, linear)
    squares = squares + others[0] + others[1] + others[2]
    features = HEADS * HD * lax.axis_size("tp")
    return finish(float(features), attention, squares, over(squares, 1), linear, att_gain)


def solution(mesh):
    placed = (P("ctx", "tp"),) * 7 + (P("tp"), P("tp"))
    return jax.shard_map(body, mesh=mesh, in_specs=placed, out_specs=P("ctx", "tp"), check_vma=False)
```

```python
import functools
import math

import jax
import jax.numpy as jnp
from jax import lax
from jax.experimental import pallas as pl
from jax.experimental.pallas import tpu as pltpu
from jax.sharding import PartitionSpec as P

HD = 128
ROWS = 512
HEADS = 6
TILE = 256
EPS = 1e-06
MASKED = -1e30
LOG2E = math.log2(math.e)
SCORE_SCALE = LOG2E / math.sqrt(HD)
SAFE_EXPONENT = 100.0
STATE_ROWS = HEADS * HD + 8
NEVER = 1 << 20

VMEM = pl.BlockSpec(memory_space=pltpu.VMEM)
SMEM = pl.BlockSpec(memory_space=pltpu.SMEM)
f32 = jnp.float32
bf16 = jnp.bfloat16
highest = lax.Precision.HIGHEST


def dot(a, b, contract=((1,), (0,)), precision=None):
    return lax.dot_general(a, b, (contract, ((), ())), precision=precision, preferred_element_type=f32)


def params(megabytes):
    return pltpu.CompilerParams(vmem_limit_bytes=megabytes << 20)


def cost(us):
    return pl.CostEstimate(flops=int(us * 1e9), bytes_accessed=int(us * 1e6), transcendentals=int(us * 1e6))


def head(h):
    return slice(h * HD, (h + 1) * HD)


def recur_kernel(
    q_hbm, k_hbm, v_hbm, step_ref, local_ref, grow_ref, message_ref, padded
):
    k_ref, q_ref, v_ref = k_hbm, q_hbm, v_hbm
    padded[...] = jnp.full((8, ROWS), 0.5, f32)
    padded[:HEADS, :] = step_ref[...]
    step = padded[...]
    rate = step / (1.0 + step)
    total = -jnp.log(1.0 + step) * LOG2E
    place = lax.broadcasted_iota(jnp.int32, (8, ROWS), 1)
    reach = 1
    while reach < ROWS:
        total = total + jnp.where(place >= reach, pltpu.roll(total, reach, 1), 0.0)
        reach *= 2
    source = jnp.log(rate) * LOG2E - total
    end = total[:, ROWS - 1 : ROWS]
    tail = jnp.exp2(end + source)
    rows = jnp.concatenate([total, tail, jnp.zeros((HD - 16, ROWS), f32)], 0)
    columns = jnp.transpose(rows)
    grow_ref[...] = jnp.exp2(columns)
    message_ref[HEADS * HD :, :] = jnp.broadcast_to(end, (8, HD))
    at_row = lax.broadcasted_iota(jnp.int32, (TILE, TILE), 0)
    at_column = lax.broadcasted_iota(jnp.int32, (TILE, TILE), 1)
    seen = at_column <= at_row
    for h in range(HEADS):
        keys = k_ref[:, head(h)].astype(f32)
        keys = keys * lax.rsqrt(jnp.sum(keys * keys, -1, keepdims=True) + EPS)
        unit = keys.astype(bf16)
        values = v_ref[:, head(h)]
        for a in range(0, ROWS, TILE):
            result = None
            for b in range(0, a + TILE, TILE):
                scores = dot(q_ref[a : a + TILE, head(h)], unit[b : b + TILE], ((1,), (1,)))
                decay = jnp.exp2(columns[a : a + TILE, h : h + 1] + source[h : h + 1, b : b + TILE])
                weights = scores * decay
                if a == b:
                    weights = jnp.where(seen, weights, 0.0)
                part = dot(weights.astype(bf16), values[b : b + TILE])
                result = part if result is None else result + part
            local_ref[a : a + TILE, head(h)] = result
        tailed = (values.astype(f32) * columns[:, 8 + h : 9 + h]).astype(bf16)
        message_ref[head(h), :] = dot(unit, tailed, ((0,), (0,)))


def recur(lh_query, lh_key, lh_value, lh_step):
    return pl.pallas_call(
        recur_kernel,
        out_shape=(
            jax.ShapeDtypeStruct((ROWS, HEADS * HD), f32),
            jax.ShapeDtypeStruct((ROWS, HD), f32),
            jax.ShapeDtypeStruct((STATE_ROWS, HD), f32),
        ),
        in_specs=[VMEM] * 4,
        out_specs=(VMEM,) * 3,
        scratch_shapes=[pltpu.VMEM((8, ROWS), f32)]
,
        compiler_params=params(16),
        cost_estimate=cost(0.2),
        name="recur",
    )(lh_query, lh_key, lh_value, lh_step)


def beside_kernel(key_ref, value_ref, out_ref):
    out_ref[:, :HD] = key_ref[...]
    out_ref[:, HD:] = value_ref[...]


def beside(key, value):
    return pl.pallas_call(
        beside_kernel,
        out_shape=jax.ShapeDtypeStruct((ROWS, 2 * HD), bf16),
        in_specs=[VMEM, VMEM],
        out_specs=VMEM,
        compiler_params=params(14),
        name="beside",
    )(key, value)


def stack_kernel(*refs):
    *parts, out_ref = refs
    at = 0
    for part in parts:
        out_ref[at : at + part.shape[0], :] = part[...]
        at += part.shape[0]


def stack(*parts):
    return pl.pallas_call(
        stack_kernel,
        out_shape=jax.ShapeDtypeStruct((sum(part.shape[0] for part in parts), 2 * HD), bf16),
        in_specs=[VMEM] * len(parts),
        out_specs=VMEM,
        compiler_params=params(14),
        name="stack",
    )(*parts)


def follow(early, late):
    logs = early[1] + late[1]
    states = [jnp.exp2(late[1][h : h + 1, :]) * early[0][h] + late[0][h] for h in range(HEADS)]
    return states, logs


def state_of(ref, wanted=None):
    states = [ref[head(h), :] for h in range(HEADS)]
    logs = ref[HEADS * HD :, :]
    if wanted is None:
        return states, logs
    return [jnp.where(wanted, state, 0.0) for state in states], jnp.where(wanted, logs, 0.0)


def put_state(ref, value):
    for h in range(HEADS):
        ref[head(h), :] = value[0][h]
    ref[HEADS * HD :, :] = value[1]


def select(wanted, one, two):
    return [jnp.where(wanted, a, b) for a, b in zip(one[0], two[0])], jnp.where(wanted, one[1], two[1])


def follow_in_order(own_first, own, other):
    return follow(select(own_first, own, other), select(own_first, other, own))


def split(value):
    upper = value.astype(bf16)
    return jnp.concatenate([upper, (value - upper.astype(f32)).astype(bf16)], 1)


def merge(both):
    return both[:, :HD].astype(f32) + both[:, HD:].astype(f32)


def join_cores_kernel(mine_ref, own_ref, other_ref, blocks_ref, out_ref, message_ref):
    even = mine_ref[0] % 2 == 0
    joined = follow_in_order(even, state_of(own_ref), state_of(other_ref))
    put_state(out_ref, joined)
    message_ref[...] = blocks_ref[...]

    @pl.when(even)
    def _():
        for h in range(HEADS):
            message_ref[head(h), :] = split(joined[0][h])
        logs = jnp.concatenate([joined[1], jnp.zeros((8, HD), f32)], 0)
        message_ref[HEADS * HD : HEADS * HD + 16, :] = split(logs)


def join_cores(mine, own, other, blocks):
    return pl.pallas_call(
        join_cores_kernel,
        out_shape=(
            jax.ShapeDtypeStruct((STATE_ROWS, HD), f32),
            jax.ShapeDtypeStruct((2 * ROWS, 2 * HD), bf16),
        ),
        in_specs=[SMEM] + [VMEM] * 3,
        out_specs=(VMEM,) * 2,
        compiler_params=params(14),
        cost_estimate=cost(0.2),
        name="join_cores",
    )(mine, own, other, blocks)


def join_sides_kernel(mine_ref, own_ref, level_ref, level_near_ref, out_ref, other_ref):
    mine = mine_ref[0]
    even = mine % 2 == 0

    def brought(ref):
        logs = merge(ref[HEADS * HD : HEADS * HD + 16, :])[:8, :]
        return [merge(ref[head(h), :]) for h in range(HEADS)], logs

    other = select(even, brought(level_ref), brought(level_near_ref))
    put_state(other_ref, other)
    put_state(out_ref, follow_in_order((mine // 2) % 2 == 0, state_of(own_ref), other))


def join_sides(mine, own, level, level_near):
    return pl.pallas_call(
        join_sides_kernel,
        out_shape=(jax.ShapeDtypeStruct((STATE_ROWS, HD), f32),) * 2,
        in_specs=[SMEM] + [VMEM] * 3,
        out_specs=(VMEM,) * 2,
        compiler_params=params(14),
        cost_estimate=cost(0.2),
        name="join_sides",
    )(mine, own, level, level_near)


def hand_kernel(mine_ref, behind_ref, beyond_ref, out_ref):
    plane, core = mine_ref[0] // 4, mine_ref[0] % 2
    behind = state_of(behind_ref, (plane == 3) | (core == 0))
    beyond = state_of(beyond_ref, (plane >= 2) & (core == 1))
    put_state(out_ref, follow(behind, beyond))


def hand(mine, behind, beyond):
    return pl.pallas_call(
        hand_kernel,
        out_shape=jax.ShapeDtypeStruct((STATE_ROWS, HD), f32),
        in_specs=[SMEM, VMEM, VMEM],
        out_specs=VMEM,
        compiler_params=params(14),
        cost_estimate=cost(0.2),
        name="hand",
    )(mine, behind, beyond)


def attend_kernel(first, last, numbers_of, pieces, kept_numbers_of, kept, mine_ref, query_ref, own_ref, *refs):
    mine = mine_ref[0]
    refs = list(refs)

    def take(count):
        return [refs.pop(0) for _ in range(count)]

    if not first:
        carry_ref, count_ref, top_in_ref = take(3)
    block_refs = [(ref, *piece) for ref, piece in zip(take(len(pieces)), pieces)]
    kept_refs = [(ref, *piece) for ref, piece in zip(take(len(kept)), kept)]
    if last:
        out_ref, square_ref, sums, keys, values, top_ref, tops = refs
    else:
        if first:
            (passed_ref,) = take(1)
            passed_ref[...] = query_ref[...]
        numerator_ref, counted_ref, top_ref, sums, keys, values = refs

    def highest_of(part):
        return jnp.max(jnp.abs(part).reshape(-1, 16, HD), 0)

    def fill(blocks, numbers):
        filled = jnp.int32(0)
        for (block, start, rows), number in zip(blocks, numbers):
            takes = number < mine
            place = filled

            @pl.when(takes)
            def _():
                at = pl.ds(pl.multiple_of(place * ROWS, ROWS), rows)
                block_keys = block[start : start + rows, :HD]
                keys[at, :] = block_keys
                values[at, :HD] = block[start : start + rows, HD:]
                top_ref[16:32, :] = jnp.maximum(top_ref[16:32, :], highest_of(block_keys))

            filled = filled + jnp.where(takes, rows // ROWS, 0)
        return filled

    if first:
        top_ref[16:32, :] = highest_of(own_ref[:, :HD])
        longest = jnp.zeros((ROWS, HD), f32)
        ones = jnp.ones((HD, HD), bf16)
        for h in range(HEADS):
            query = query_ref[:, head(h)].astype(f32)
            longest = jnp.maximum(longest, dot((query * query).astype(bf16), ones))
        top_ref[0:16, :] = jnp.max(longest.reshape(-1, 16, HD), 0).astype(bf16)
    else:
        top_ref[...] = top_in_ref[...]
    values[:, HD:] = jnp.ones((values.shape[0], HD), bf16)
    filled = fill(block_refs, numbers_of(mine))
    sums[...] = jnp.zeros_like(sums)

    def visit(start, count):
        at = pl.ds(pl.multiple_of(start, ROWS), count)
        block_keys = keys[at, :]
        block_values = values[at, :]
        for h in range(HEADS):
            for a in range(0, ROWS, TILE):
                scores = dot(query_ref[a : a + TILE, head(h)], block_keys, ((1,), (1,)))
                weights = jnp.exp2(scores * SCORE_SCALE).astype(bf16)
                sums[h, a : a + TILE, :] += dot(weights, block_values)

    def pair(n, _):
        visit(n * 2 * ROWS, 2 * ROWS)
        return 0

    if not first:
        lax.fori_loop(0, filled // 2, pair, 0)

    if first:

        @pl.when(filled > 0)
        def _():
            visit(0, ROWS)

        at_row = lax.broadcasted_iota(jnp.int32, (TILE, TILE), 0)
        at_column = lax.broadcasted_iota(jnp.int32, (TILE, TILE), 1)
        seen = at_column <= at_row
        values[:ROWS, :HD] = own_ref[:, HD:]
        for h in range(HEADS):
            for a in range(0, ROWS, TILE):
                for b in range(0, a + TILE, TILE):
                    scores = dot(query_ref[a : a + TILE, head(h)], own_ref[b : b + TILE, :HD], ((1,), (1,)))
                    weights = jnp.exp2(scores * SCORE_SCALE)
                    if a == b:
                        weights = jnp.where(seen, weights, 0.0)
                    sums[h, a : a + TILE, :] += dot(weights.astype(bf16), values[b : b + TILE, :])
            numerator_ref[:, head(h)] = sums[h, :, :HD]
            counted_ref[:, h : h + 1] = sums[h, :, HD : HD + 1]
    elif not last:
        for h in range(HEADS):
            numerator_ref[:, head(h)] = sums[h, :, :HD] + carry_ref[:, head(h)]
            counted_ref[:, h : h + 1] = sums[h, :, HD : HD + 1] + count_ref[:, h : h + 1]
    else:
        key_top = jnp.max(top_ref[16:32, :].astype(f32), 0, keepdims=True)
        bound = jnp.max(top_ref[0:16, :].astype(f32)) * jnp.sum(key_top * key_top) * SCORE_SCALE**2
        large = bound * 1.05 > SAFE_EXPONENT * SAFE_EXPONENT

        @pl.when(large)
        def _():
            before = fill(kept_refs + block_refs, kept_numbers_of(mine) + numbers_of(mine))
            at = pl.ds(pl.multiple_of(before * ROWS, ROWS), ROWS)
            keys[at, :] = own_ref[:, :HD]
            values[at, :HD] = own_ref[:, HD:]
            sums[...] = jnp.zeros_like(sums)
            tops[...] = jnp.full_like(tops, MASKED)

            def step(n, _):
                at = pl.ds(pl.multiple_of((n // (2 * HEADS)) * ROWS, ROWS), ROWS)
                h = (n % (2 * HEADS)) // 2
                a = (n % 2) * TILE
                rows = pl.ds(pl.multiple_of(a, TILE), TILE)
                query = query_ref[rows, pl.ds(pl.multiple_of(h * HD, HD), HD)]
                scores = dot(query, keys[at, :], ((1,), (1,))) * SCORE_SCALE
                row = lax.broadcasted_iota(jnp.int32, (TILE, ROWS), 0) + a
                column = lax.broadcasted_iota(jnp.int32, (TILE, ROWS), 1)
                column = column - jnp.where(n // (2 * HEADS) < before, ROWS, 0)
                visible = column <= row
                scores = jnp.where(visible, scores, MASKED)
                old = tops[h, rows, :]
                new = jnp.maximum(old[:, :1], jnp.max(scores, 1, keepdims=True))
                weights = jnp.where(visible, jnp.exp2(scores - new), 0.0).astype(bf16)
                sums[h, rows, :] = sums[h, rows, :] * jnp.exp2(old[:, :1] - new) + dot(weights, values[at, :])
                tops[h, rows, :] = jnp.broadcast_to(new, (TILE, HD))
                return 0

            lax.fori_loop(0, (before + 1) * 2 * HEADS, step, 0)

        squares = jnp.zeros((ROWS, HD), f32)
        for h in range(HEADS):
            count = sums[h, :, HD:] + jnp.where(large, 0.0, count_ref[:, h : h + 1])
            result = (sums[h, :, :HD] + jnp.where(large, 0.0, carry_ref[:, head(h)])) / count
            result = result.astype(bf16)
            out_ref[:, head(h)] = result
            result = result.astype(f32)
            squares = squares + result * result
        square_ref[...] = dot(jnp.ones((8, HD), f32), squares, ((1,), (1,)), highest)


def attend(mine, query, own, carry, blocks, numbers_of, kept=None, kept_numbers_of=None):
    first, last = carry is None, kept is not None
    kept = kept or []
    size = 16 * ROWS if last else sum(rows for _, _, rows in blocks)
    operands = [query, own] + list(carry or []) + [block for block, _, _ in blocks + kept]
    top = (32, HD)
    scratch = [
        pltpu.VMEM((HEADS, ROWS, 2 * HD), f32),
        pltpu.VMEM((size, HD), bf16),
        pltpu.VMEM((size, 2 * HD), bf16),
    ]
    if last:
        out_shape = (
            jax.ShapeDtypeStruct((ROWS, HEADS * HD), bf16),
            jax.ShapeDtypeStruct((8, ROWS), f32),
        )
        scratch += [pltpu.VMEM(top, bf16), pltpu.VMEM((HEADS, ROWS, HD), f32)]
    else:
        out_shape = (
            jax.ShapeDtypeStruct((ROWS, HEADS * HD), f32),
            jax.ShapeDtypeStruct((ROWS, HD), f32),
            jax.ShapeDtypeStruct(top, bf16),
        )
        if first:
            out_shape = (jax.ShapeDtypeStruct((ROWS, HEADS * HD), bf16),) + out_shape
    return pl.pallas_call(
        functools.partial(
            attend_kernel,
            first,
            last,
            numbers_of,
            [block[1:] for block in blocks],
            kept_numbers_of,
            [block[1:] for block in kept],
        ),
        out_shape=out_shape,
        in_specs=[SMEM] + [VMEM] * len(operands),
        out_specs=(VMEM,) * len(out_shape),
        scratch_shapes=scratch,
        compiler_params=params(20),
        cost_estimate=cost(0.2),
        name="attend_first" if first else "attend_last" if last else "attend_middle",
    )(mine, *operands)


def carry_kernel(
    mine_ref,
    query_hbm,
    local_ref,
    grow_ref,
    kept_ref,
    handed_ref,
    chip_ref,
    core_ref,
    gain_ref,
    out_ref,
):
    mine = mine_ref[0]
    query_ref = query_hbm
    plane, side, core = mine // 4, (mine // 2) % 2, mine % 2
    kept, handed = state_of(kept_ref), state_of(handed_ref)

    def pick(one, two, wanted):
        states = [jnp.where(wanted, jnp.where(core == 0, a, b), 0.0) for a, b in zip(one[0], two[0])]
        return states, jnp.where(wanted, jnp.where(core == 0, one[1], two[1]), 0.0)

    entering = pick(handed, kept, plane >= 2)
    entering = follow(entering, pick(kept, handed, plane >= 1))
    entering = follow(entering, state_of(chip_ref, side == 1))
    entering = follow(entering, state_of(core_ref, core == 1))
    grow = grow_ref[...]
    for h in range(HEADS):
        state = entering[0][h]
        upper = state.astype(bf16)
        lower = (state - upper.astype(f32)).astype(bf16)
        both = dot(query_ref[:, head(h)], jnp.concatenate([upper, lower], 1))
        entered = both[:, :HD] + both[:, HD:]
        result = local_ref[:, head(h)] + entered * grow[:, h : h + 1]
        square = jnp.mean(result * result, -1, keepdims=True)
        out_ref[:, head(h)] = result * lax.rsqrt(square + EPS) * gain_ref[head(h)][None, :]


def finish_kernel(features, attention_ref, square_ref, other_ref, linear_ref, gain_ref, out_ref):
    factor = lax.rsqrt((square_ref[...] + other_ref[...]) / features + EPS)
    factor = dot(factor, jnp.full((8, HD), 0.125, f32), ((0,), (0,)), highest)
    for h in range(HEADS):
        part = attention_ref[:, head(h)].astype(f32) * factor * gain_ref[head(h)][None, :]
        out_ref[:, head(h)] = (part + linear_ref[:, head(h)]).astype(bf16)


def carry_in(place, lh_query, *operands):
    return pl.pallas_call(
        carry_kernel,
        out_shape=jax.ShapeDtypeStruct((ROWS, HEADS * HD), f32),
        in_specs=[SMEM, VMEM] + [VMEM] * len(operands),
        out_specs=VMEM,
        compiler_params=params(14),
        cost_estimate=cost(0.2),
        name="carry",
    )(place, lh_query, *operands)


def finish(features, *operands):
    return pl.pallas_call(
        functools.partial(finish_kernel, features),
        out_shape=jax.ShapeDtypeStruct((ROWS, HEADS * HD), bf16),
        in_specs=[VMEM] * len(operands),
        out_specs=VMEM,
        compiler_params=params(14),
        cost_estimate=cost(0.2),
        name="finish",
    )(*operands)


def body(att_query, att_key, att_value, lh_query, lh_key, lh_value, lh_step, att_gain, lh_gain):
    mine = lax.axis_index("ctx")
    place = mine.reshape(1).astype(jnp.int32)

    def move(value, pairs):
        return lax.ppermute(value, "ctx", pairs)

    every = range(16)
    sibling = [(i, i ^ 1) for i in every]
    sideways = [(i, i ^ 2) for i in every]
    onward = [(i, i + 4) for i in every if i % 2 == 0 and i < 12] + [(i, i + 8) for i in every if i % 2 == 1 and i < 8]
    wrapping = [(i, i + 12) for i in range(4)]
    last_plane = [(i, i + 4) for i in every if i % 2 == 0 and i < 12] + [(i, i + 12) for i in (1, 3)]
    plane_before = [(i, i + 8) for i in every if i % 2 == 1 and i < 8]

    def tied(*values):
        return lax.optimization_barrier(values)

    lh_query, lh_key, lh_value, far_query, att_key, att_value = [
        array
        for array in (lh_query, lh_key, lh_value, att_query, att_key, att_value)
    ]
    lh_step = lh_step.T
    att_query, lh_query, lh_key, lh_value, att_key, att_value = [
        pltpu.with_memory_space_constraint(array, pltpu.HBM)
        for array in (att_query, lh_query, lh_key, lh_value, att_key, att_value)
    ]
    own = beside(att_key, att_value)
    across = move(own, [(i, j) for i, j in sideways if i < 12 or i % 4 < 2])
    wrapped = move(own, wrapping)
    near = move(own, sibling)
    chip = stack(own, near)
    chip, lh_step = tied(chip, lh_step)
    lh_step = pltpu.with_memory_space_constraint(lh_step, pltpu.HBM)
    ring = move(chip, onward)

    local, grow, message = recur(lh_query, lh_key, lh_value, lh_step)

    def where(number, wanted):
        return jnp.where(wanted, number, NEVER)

    def parts(mine):
        return mine // 4, (mine // 2) % 2, mine % 2, mine - mine % 2

    def near_numbers(mine):
        return [where(mine - 1, mine % 2 == 1)]

    def ring_numbers(mine):
        plane, _, core, even = parts(mine)
        one, two = where(even - 4, plane >= 1), where(even - 8, plane >= 2)
        return [jnp.where(core == 0, one, two), jnp.where(core == 0, two, one)]

    def wrapped_numbers(mine):
        plane, _, _, even = parts(mine)
        return [where(even - 12, plane == 3)] * 2

    def across_numbers(mine):
        _, side, _, even = parts(mine)
        return [where(even - 2, side == 1)] * 2

    def middle_numbers(mine):
        return ring_numbers(mine) + wrapped_numbers(mine)

    def last_numbers(mine):
        plane, _, core, even = parts(mine)
        beyond, behind = where(even - 8, plane >= 2), where(even - 4, plane >= 1)
        level_numbers = [where(beyond, core == 1), where(beyond, core == 0)]
        return level_numbers + across_numbers(mine) + wrapped_numbers(mine) + [behind] * 2

    first_pieces = [(near, 0, ROWS)]
    near_query, *carry = attend(place, att_query, own, None, first_pieces, near_numbers)
    carry, message, across, wrapped = tied(carry, message, across, wrapped)
    first = move(message, sibling)
    of_chip, leveled = join_cores(place, message, first, ring)
    level = move(leveled, sideways)
    wrapped_side = move(across, wrapping)
    behind_side = move(across, [(i, i + 4) for i in range(12)])
    bundle = stack(ring, wrapped)
    bundle_near = move(bundle, sibling)
    middle_pieces = [
        (ring, 0, 2 * ROWS),
        (bundle_near, 0, 2 * ROWS),
        (wrapped, 0, ROWS),
        (bundle_near, 2 * ROWS, ROWS),
    ]
    carry = attend(place, near_query, own, carry, middle_pieces, middle_numbers)

    carry, across, wrapped_side, behind_side, level = tied(carry, across, wrapped_side, behind_side, level)
    level_near = move(level, sibling)
    rest = stack(across, wrapped_side, behind_side)
    rest_near = move(rest, sibling)
    of_plane, other_chip = join_sides(place, of_chip, level, level_near)
    state_behind = move(of_plane, last_plane)
    state_beyond = move(of_plane, plane_before)
    last_pieces = [
        (level, 0, 2 * ROWS),
        (level_near, 0, 2 * ROWS),
        (across, 0, ROWS),
        (rest_near, 0, ROWS),
        (wrapped_side, 0, ROWS),
        (rest_near, ROWS, ROWS),
        (behind_side, 0, ROWS),
        (rest_near, 2 * ROWS, ROWS),
    ]
    carry, of_plane = tied(carry, of_plane)
    attention, squares = attend(
        place,
        near_query,
        own,
        carry,
        last_pieces,
        last_numbers,
        first_pieces + middle_pieces,
        lambda mine: near_numbers(mine) + middle_numbers(mine),
    )

    def over(value, bit):
        return lax.ppermute(value, "tp", [(i, i ^ bit) for i in range(8)])

    squares, state_behind, state_beyond = tied(squares, state_behind, state_beyond)
    others = [over(squares, bit) for bit in (2, 4, 6)]
    kept = hand(place, state_behind, state_beyond)
    handed = move(kept, sibling)
    linear = carry_in(place, lh_query, local, grow, kept, handed, other_chip, first, lh_gain)
    others, linear = tied(others, linear)
    squares = squares + others[0] + others[1] + others[2]
    features = HEADS * HD * lax.axis_size("tp")
    return finish(float(features), attention, squares, over(squares, 1), linear, att_gain)


def solution(mesh):
    placed = (P("ctx", "tp"),) * 7 + (P("tp"), P("tp"))
    return jax.shard_map(body, mesh=mesh, in_specs=placed, out_specs=P("ctx", "tp"), check_vma=False)
```

```python
import functools
import math

import jax
import jax.numpy as jnp
from jax import lax
from jax.experimental import pallas as pl
from jax.experimental.pallas import tpu as pltpu
from jax.sharding import PartitionSpec as P

HD = 128
ROWS = 512
HEADS = 6
TILE = 256
EPS = 1e-06
MASKED = -1e30
LOG2E = math.log2(math.e)
SCORE_SCALE = LOG2E / math.sqrt(HD)
SAFE_EXPONENT = 100.0
STATE_ROWS = HEADS * HD + 8
NEVER = 1 << 20

VMEM = pl.BlockSpec(memory_space=pltpu.VMEM)
SMEM = pl.BlockSpec(memory_space=pltpu.SMEM)
f32 = jnp.float32
bf16 = jnp.bfloat16
highest = lax.Precision.HIGHEST


def dot(a, b, contract=((1,), (0,)), precision=None):
    return lax.dot_general(a, b, (contract, ((), ())), precision=precision, preferred_element_type=f32)


def params(megabytes):
    return pltpu.CompilerParams(vmem_limit_bytes=megabytes << 20)


def cost(us):
    return pl.CostEstimate(flops=int(us * 1e9), bytes_accessed=int(us * 1e6), transcendentals=int(us * 1e6))


def head(h):
    return slice(h * HD, (h + 1) * HD)


def recur_kernel(
    q_hbm, k_hbm, v_hbm, step_ref, local_ref, grow_ref, message_ref, padded
):
    k_ref, q_ref, v_ref = k_hbm, q_hbm, v_hbm
    padded[...] = jnp.full((8, ROWS), 0.5, f32)
    padded[:HEADS, :] = step_ref[...]
    step = padded[...]
    rate = step / (1.0 + step)
    total = -jnp.log(1.0 + step) * LOG2E
    place = lax.broadcasted_iota(jnp.int32, (8, ROWS), 1)
    reach = 1
    while reach < ROWS:
        total = total + jnp.where(place >= reach, pltpu.roll(total, reach, 1), 0.0)
        reach *= 2
    source = jnp.log(rate) * LOG2E - total
    end = total[:, ROWS - 1 : ROWS]
    tail = jnp.exp2(end + source)
    rows = jnp.concatenate([total, tail, jnp.zeros((HD - 16, ROWS), f32)], 0)
    columns = jnp.transpose(rows)
    grow_ref[...] = jnp.exp2(columns)
    message_ref[HEADS * HD :, :] = jnp.broadcast_to(end, (8, HD))
    at_row = lax.broadcasted_iota(jnp.int32, (TILE, TILE), 0)
    at_column = lax.broadcasted_iota(jnp.int32, (TILE, TILE), 1)
    seen = at_column <= at_row
    for h in range(HEADS):
        keys = k_ref[:, head(h)].astype(f32)
        keys = keys * lax.rsqrt(jnp.sum(keys * keys, -1, keepdims=True) + EPS)
        unit = keys.astype(bf16)
        values = v_ref[:, head(h)]
        for a in range(0, ROWS, TILE):
            result = None
            for b in range(0, a + TILE, TILE):
                scores = dot(q_ref[a : a + TILE, head(h)], unit[b : b + TILE], ((1,), (1,)))
                decay = jnp.exp2(columns[a : a + TILE, h : h + 1] + source[h : h + 1, b : b + TILE])
                weights = scores * decay
                if a == b:
                    weights = jnp.where(seen, weights, 0.0)
                part = dot(weights.astype(bf16), values[b : b + TILE])
                result = part if result is None else result + part
            local_ref[a : a + TILE, head(h)] = result
        tailed = (values.astype(f32) * columns[:, 8 + h : 9 + h]).astype(bf16)
        message_ref[head(h), :] = dot(unit, tailed, ((0,), (0,)))


def recur(lh_query, lh_key, lh_value, lh_step):
    return pl.pallas_call(
        recur_kernel,
        out_shape=(
            jax.ShapeDtypeStruct((ROWS, HEADS * HD), f32),
            jax.ShapeDtypeStruct((ROWS, HD), f32),
            jax.ShapeDtypeStruct((STATE_ROWS, HD), f32),
        ),
        in_specs=[VMEM] * 4,
        out_specs=(VMEM,) * 3,
        scratch_shapes=[pltpu.VMEM((8, ROWS), f32)]
,
        compiler_params=params(16),
        cost_estimate=cost(0.2),
        name="recur",
    )(lh_query, lh_key, lh_value, lh_step)


def beside_kernel(key_ref, value_ref, out_ref):
    out_ref[:, :HD] = key_ref[...]
    out_ref[:, HD:] = value_ref[...]


def beside(key, value):
    return pl.pallas_call(
        beside_kernel,
        out_shape=jax.ShapeDtypeStruct((ROWS, 2 * HD), bf16),
        in_specs=[VMEM, VMEM],
        out_specs=VMEM,
        compiler_params=params(14),
        name="beside",
    )(key, value)


def stack_kernel(*refs):
    *parts, out_ref = refs
    at = 0
    for part in parts:
        out_ref[at : at + part.shape[0], :] = part[...]
        at += part.shape[0]


def stack(*parts):
    return pl.pallas_call(
        stack_kernel,
        out_shape=jax.ShapeDtypeStruct((sum(part.shape[0] for part in parts), 2 * HD), bf16),
        in_specs=[VMEM] * len(parts),
        out_specs=VMEM,
        compiler_params=params(14),
        name="stack",
    )(*parts)


def follow(early, late):
    logs = early[1] + late[1]
    states = [jnp.exp2(late[1][h : h + 1, :]) * early[0][h] + late[0][h] for h in range(HEADS)]
    return states, logs


def state_of(ref, wanted=None):
    states = [ref[head(h), :] for h in range(HEADS)]
    logs = ref[HEADS * HD :, :]
    if wanted is None:
        return states, logs
    return [jnp.where(wanted, state, 0.0) for state in states], jnp.where(wanted, logs, 0.0)


def put_state(ref, value):
    for h in range(HEADS):
        ref[head(h), :] = value[0][h]
    ref[HEADS * HD :, :] = value[1]


def select(wanted, one, two):
    return [jnp.where(wanted, a, b) for a, b in zip(one[0], two[0])], jnp.where(wanted, one[1], two[1])


def follow_in_order(own_first, own, other):
    return follow(select(own_first, own, other), select(own_first, other, own))


def split(value):
    upper = value.astype(bf16)
    return jnp.concatenate([upper, (value - upper.astype(f32)).astype(bf16)], 1)


def merge(both):
    return both[:, :HD].astype(f32) + both[:, HD:].astype(f32)


def join_cores_kernel(mine_ref, own_ref, other_ref, blocks_ref, out_ref, message_ref):
    even = mine_ref[0] % 2 == 0
    joined = follow_in_order(even, state_of(own_ref), state_of(other_ref))
    put_state(out_ref, joined)
    message_ref[...] = blocks_ref[...]

    @pl.when(even)
    def _():
        for h in range(HEADS):
            message_ref[head(h), :] = split(joined[0][h])
        logs = jnp.concatenate([joined[1], jnp.zeros((8, HD), f32)], 0)
        message_ref[HEADS * HD : HEADS * HD + 16, :] = split(logs)


def join_cores(mine, own, other, blocks):
    return pl.pallas_call(
        join_cores_kernel,
        out_shape=(
            jax.ShapeDtypeStruct((STATE_ROWS, HD), f32),
            jax.ShapeDtypeStruct((2 * ROWS, 2 * HD), bf16),
        ),
        in_specs=[SMEM] + [VMEM] * 3,
        out_specs=(VMEM,) * 2,
        compiler_params=params(14),
        cost_estimate=cost(0.2),
        name="join_cores",
    )(mine, own, other, blocks)


def join_sides_kernel(mine_ref, own_ref, level_ref, level_near_ref, out_ref, other_ref):
    mine = mine_ref[0]
    even = mine % 2 == 0

    def brought(ref):
        logs = merge(ref[HEADS * HD : HEADS * HD + 16, :])[:8, :]
        return [merge(ref[head(h), :]) for h in range(HEADS)], logs

    other = select(even, brought(level_ref), brought(level_near_ref))
    put_state(other_ref, other)
    put_state(out_ref, follow_in_order((mine // 2) % 2 == 0, state_of(own_ref), other))


def join_sides(mine, own, level, level_near):
    return pl.pallas_call(
        join_sides_kernel,
        out_shape=(jax.ShapeDtypeStruct((STATE_ROWS, HD), f32),) * 2,
        in_specs=[SMEM] + [VMEM] * 3,
        out_specs=(VMEM,) * 2,
        compiler_params=params(14),
        cost_estimate=cost(0.2),
        name="join_sides",
    )(mine, own, level, level_near)


def hand_kernel(mine_ref, behind_ref, beyond_ref, out_ref):
    plane, core = mine_ref[0] // 4, mine_ref[0] % 2
    behind = state_of(behind_ref, (plane == 3) | (core == 0))
    beyond = state_of(beyond_ref, (plane >= 2) & (core == 1))
    put_state(out_ref, follow(behind, beyond))


def hand(mine, behind, beyond):
    return pl.pallas_call(
        hand_kernel,
        out_shape=jax.ShapeDtypeStruct((STATE_ROWS, HD), f32),
        in_specs=[SMEM, VMEM, VMEM],
        out_specs=VMEM,
        compiler_params=params(14),
        cost_estimate=cost(0.2),
        name="hand",
    )(mine, behind, beyond)


def attend_kernel(first, last, numbers_of, pieces, kept_numbers_of, kept, mine_ref, query_ref, own_ref, *refs):
    mine = mine_ref[0]
    refs = list(refs)

    def take(count):
        return [refs.pop(0) for _ in range(count)]

    if not first:
        carry_ref, count_ref, top_in_ref = take(3)
    block_refs = [(ref, *piece) for ref, piece in zip(take(len(pieces)), pieces)]
    kept_refs = [(ref, *piece) for ref, piece in zip(take(len(kept)), kept)]
    if last:
        out_ref, square_ref, sums, keys, values, top_ref, tops = refs
    else:
        if first:
            (passed_ref,) = take(1)
            passed_ref[...] = query_ref[...]
        numerator_ref, counted_ref, top_ref, sums, keys, values = refs

    def highest_of(part):
        return jnp.max(jnp.abs(part).reshape(-1, 16, HD), 0)

    def fill(blocks, numbers):
        filled = jnp.int32(0)
        for (block, start, rows), number in zip(blocks, numbers):
            takes = number < mine
            place = filled

            @pl.when(takes)
            def _():
                at = pl.ds(pl.multiple_of(place * ROWS, ROWS), rows)
                block_keys = block[start : start + rows, :HD]
                keys[at, :] = block_keys
                values[at, :HD] = block[start : start + rows, HD:]
                top_ref[16:32, :] = jnp.maximum(top_ref[16:32, :], highest_of(block_keys))

            filled = filled + jnp.where(takes, rows // ROWS, 0)
        return filled

    if first:
        top_ref[16:32, :] = highest_of(own_ref[:, :HD])
        longest = jnp.zeros((ROWS, HD), f32)
        ones = jnp.ones((HD, HD), bf16)
        for h in range(HEADS):
            query = query_ref[:, head(h)].astype(f32)
            longest = jnp.maximum(longest, dot((query * query).astype(bf16), ones))
        top_ref[0:16, :] = jnp.max(longest.reshape(-1, 16, HD), 0).astype(bf16)
    else:
        top_ref[...] = top_in_ref[...]
    values[:, HD:] = jnp.ones((values.shape[0], HD), bf16)
    filled = fill(block_refs, numbers_of(mine))
    sums[...] = jnp.zeros_like(sums)

    def visit(start, count):
        at = pl.ds(pl.multiple_of(start, ROWS), count)
        block_keys = keys[at, :]
        block_values = values[at, :]
        for h in range(HEADS):
            for a in range(0, ROWS, TILE):
                scores = dot(query_ref[a : a + TILE, head(h)], block_keys, ((1,), (1,)))
                weights = jnp.exp2(scores * SCORE_SCALE).astype(bf16)
                sums[h, a : a + TILE, :] += dot(weights, block_values)

    def pair(n, _):
        visit(n * 2 * ROWS, 2 * ROWS)
        return 0

    if not first:
        lax.fori_loop(0, filled // 2, pair, 0)

    if first:

        @pl.when(filled > 0)
        def _():
            visit(0, ROWS)

        at_row = lax.broadcasted_iota(jnp.int32, (TILE, TILE), 0)
        at_column = lax.broadcasted_iota(jnp.int32, (TILE, TILE), 1)
        seen = at_column <= at_row
        values[:ROWS, :HD] = own_ref[:, HD:]
        for h in range(HEADS):
            for a in range(0, ROWS, TILE):
                for b in range(0, a + TILE, TILE):
                    scores = dot(query_ref[a : a + TILE, head(h)], own_ref[b : b + TILE, :HD], ((1,), (1,)))
                    weights = jnp.exp2(scores * SCORE_SCALE)
                    if a == b:
                        weights = jnp.where(seen, weights, 0.0)
                    sums[h, a : a + TILE, :] += dot(weights.astype(bf16), values[b : b + TILE, :])
            numerator_ref[:, head(h)] = sums[h, :, :HD]
            counted_ref[:, h : h + 1] = sums[h, :, HD : HD + 1]
    elif not last:
        for h in range(HEADS):
            numerator_ref[:, head(h)] = sums[h, :, :HD] + carry_ref[:, head(h)]
            counted_ref[:, h : h + 1] = sums[h, :, HD : HD + 1] + count_ref[:, h : h + 1]
    else:
        key_top = jnp.max(top_ref[16:32, :].astype(f32), 0, keepdims=True)
        bound = jnp.max(top_ref[0:16, :].astype(f32)) * jnp.sum(key_top * key_top) * SCORE_SCALE**2
        large = bound * 1.05 > SAFE_EXPONENT * SAFE_EXPONENT

        @pl.when(large)
        def _():
            before = fill(kept_refs + block_refs, kept_numbers_of(mine) + numbers_of(mine))
            at = pl.ds(pl.multiple_of(before * ROWS, ROWS), ROWS)
            keys[at, :] = own_ref[:, :HD]
            values[at, :HD] = own_ref[:, HD:]
            sums[...] = jnp.zeros_like(sums)
            tops[...] = jnp.full_like(tops, MASKED)

            def step(n, _):
                at = pl.ds(pl.multiple_of((n // (2 * HEADS)) * ROWS, ROWS), ROWS)
                h = (n % (2 * HEADS)) // 2
                a = (n % 2) * TILE
                rows = pl.ds(pl.multiple_of(a, TILE), TILE)
                query = query_ref[rows, pl.ds(pl.multiple_of(h * HD, HD), HD)]
                scores = dot(query, keys[at, :], ((1,), (1,))) * SCORE_SCALE
                row = lax.broadcasted_iota(jnp.int32, (TILE, ROWS), 0) + a
                column = lax.broadcasted_iota(jnp.int32, (TILE, ROWS), 1)
                column = column - jnp.where(n // (2 * HEADS) < before, ROWS, 0)
                visible = column <= row
                scores = jnp.where(visible, scores, MASKED)
                old = tops[h, rows, :]
                new = jnp.maximum(old[:, :1], jnp.max(scores, 1, keepdims=True))
                weights = jnp.where(visible, jnp.exp2(scores - new), 0.0).astype(bf16)
                sums[h, rows, :] = sums[h, rows, :] * jnp.exp2(old[:, :1] - new) + dot(weights, values[at, :])
                tops[h, rows, :] = jnp.broadcast_to(new, (TILE, HD))
                return 0

            lax.fori_loop(0, (before + 1) * 2 * HEADS, step, 0)

        squares = jnp.zeros((ROWS, HD), f32)
        for h in range(HEADS):
            count = sums[h, :, HD:] + jnp.where(large, 0.0, count_ref[:, h : h + 1])
            result = (sums[h, :, :HD] + jnp.where(large, 0.0, carry_ref[:, head(h)])) / count
            result = result.astype(bf16)
            out_ref[:, head(h)] = result
            result = result.astype(f32)
            squares = squares + result * result
        square_ref[...] = dot(jnp.ones((8, HD), f32), squares, ((1,), (1,)), highest)


def attend(mine, query, own, carry, blocks, numbers_of, kept=None, kept_numbers_of=None):
    first, last = carry is None, kept is not None
    kept = kept or []
    size = 16 * ROWS if last else sum(rows for _, _, rows in blocks)
    operands = [query, own] + list(carry or []) + [block for block, _, _ in blocks + kept]
    top = (32, HD)
    scratch = [
        pltpu.VMEM((HEADS, ROWS, 2 * HD), f32),
        pltpu.VMEM((size, HD), bf16),
        pltpu.VMEM((size, 2 * HD), bf16),
    ]
    if last:
        out_shape = (
            jax.ShapeDtypeStruct((ROWS, HEADS * HD), bf16),
            jax.ShapeDtypeStruct((8, ROWS), f32),
        )
        scratch += [pltpu.VMEM(top, bf16), pltpu.VMEM((HEADS, ROWS, HD), f32)]
    else:
        out_shape = (
            jax.ShapeDtypeStruct((ROWS, HEADS * HD), f32),
            jax.ShapeDtypeStruct((ROWS, HD), f32),
            jax.ShapeDtypeStruct(top, bf16),
        )
        if first:
            out_shape = (jax.ShapeDtypeStruct((ROWS, HEADS * HD), bf16),) + out_shape
    return pl.pallas_call(
        functools.partial(
            attend_kernel,
            first,
            last,
            numbers_of,
            [block[1:] for block in blocks],
            kept_numbers_of,
            [block[1:] for block in kept],
        ),
        out_shape=out_shape,
        in_specs=[SMEM] + [VMEM] * len(operands),
        out_specs=(VMEM,) * len(out_shape),
        scratch_shapes=scratch,
        compiler_params=params(20),
        cost_estimate=cost(0.2),
        name="attend_first" if first else "attend_last" if last else "attend_middle",
    )(mine, *operands)


def carry_kernel(
    mine_ref,
    query_hbm,
    local_ref,
    grow_ref,
    kept_ref,
    handed_ref,
    chip_ref,
    core_ref,
    gain_ref,
    out_ref,
):
    mine = mine_ref[0]
    query_ref = query_hbm
    plane, side, core = mine // 4, (mine // 2) % 2, mine % 2
    kept, handed = state_of(kept_ref), state_of(handed_ref)

    def pick(one, two, wanted):
        states = [jnp.where(wanted, jnp.where(core == 0, a, b), 0.0) for a, b in zip(one[0], two[0])]
        return states, jnp.where(wanted, jnp.where(core == 0, one[1], two[1]), 0.0)

    entering = pick(handed, kept, plane >= 2)
    entering = follow(entering, pick(kept, handed, plane >= 1))
    entering = follow(entering, state_of(chip_ref, side == 1))
    entering = follow(entering, state_of(core_ref, core == 1))
    grow = grow_ref[...]
    for h in range(HEADS):
        state = entering[0][h]
        upper = state.astype(bf16)
        lower = (state - upper.astype(f32)).astype(bf16)
        both = dot(query_ref[:, head(h)], jnp.concatenate([upper, lower], 1))
        entered = both[:, :HD] + both[:, HD:]
        result = local_ref[:, head(h)] + entered * grow[:, h : h + 1]
        square = jnp.mean(result * result, -1, keepdims=True)
        out_ref[:, head(h)] = result * lax.rsqrt(square + EPS) * gain_ref[head(h)][None, :]


def finish_kernel(features, attention_ref, square_ref, other_ref, linear_ref, gain_ref, out_ref):
    factor = lax.rsqrt((square_ref[...] + other_ref[...]) / features + EPS)
    factor = dot(factor, jnp.full((8, HD), 0.125, f32), ((0,), (0,)), highest)
    for h in range(HEADS):
        part = attention_ref[:, head(h)].astype(f32) * factor * gain_ref[head(h)][None, :]
        out_ref[:, head(h)] = (part + linear_ref[:, head(h)]).astype(bf16)


def carry_in(place, lh_query, *operands):
    return pl.pallas_call(
        carry_kernel,
        out_shape=jax.ShapeDtypeStruct((ROWS, HEADS * HD), f32),
        in_specs=[SMEM, VMEM] + [VMEM] * len(operands),
        out_specs=VMEM,
        compiler_params=params(14),
        cost_estimate=cost(0.2),
        name="carry",
    )(place, lh_query, *operands)


def finish(features, *operands):
    return pl.pallas_call(
        functools.partial(finish_kernel, features),
        out_shape=jax.ShapeDtypeStruct((ROWS, HEADS * HD), bf16),
        in_specs=[VMEM] * len(operands),
        out_specs=VMEM,
        compiler_params=params(14),
        cost_estimate=cost(0.2),
        name="finish",
    )(*operands)


def body(att_query, att_key, att_value, lh_query, lh_key, lh_value, lh_step, att_gain, lh_gain):
    mine = lax.axis_index("ctx")
    place = mine.reshape(1).astype(jnp.int32)

    def move(value, pairs):
        return lax.ppermute(value, "ctx", pairs)

    every = range(16)
    sibling = [(i, i ^ 1) for i in every]
    sideways = [(i, i ^ 2) for i in every]
    onward = [(i, i + 4) for i in every if i % 2 == 0 and i < 12] + [(i, i + 8) for i in every if i % 2 == 1 and i < 8]
    wrapping = [(i, i + 12) for i in range(4)]
    last_plane = [(i, i + 4) for i in every if i % 2 == 0 and i < 12] + [(i, i + 12) for i in (1, 3)]
    plane_before = [(i, i + 8) for i in every if i % 2 == 1 and i < 8]

    def tied(*values):
        return lax.optimization_barrier(values)

    lh_query, lh_key, lh_value, far_query, att_key, att_value = [
        array
        for array in (lh_query, lh_key, lh_value, att_query, att_key, att_value)
    ]
    lh_step = lh_step.T
    att_query, lh_query, lh_key, lh_value, att_key, att_value = [
        pltpu.with_memory_space_constraint(array, pltpu.HBM)
        for array in (att_query, lh_query, lh_key, lh_value, att_key, att_value)
    ]
    own = beside(att_key, att_value)
    across = move(own, [(i, j) for i, j in sideways if i < 12 or i % 4 < 2])
    wrapped = move(own, wrapping)
    near = move(own, sibling)
    chip = stack(own, near)
    chip, lh_step = tied(chip, lh_step)
    lh_step = pltpu.with_memory_space_constraint(lh_step, pltpu.HBM)
    ring = move(chip, onward)

    local, grow, message = recur(lh_query, lh_key, lh_value, lh_step)

    def where(number, wanted):
        return jnp.where(wanted, number, NEVER)

    def parts(mine):
        return mine // 4, (mine // 2) % 2, mine % 2, mine - mine % 2

    def near_numbers(mine):
        return [where(mine - 1, mine % 2 == 1)]

    def ring_numbers(mine):
        plane, _, core, even = parts(mine)
        one, two = where(even - 4, plane >= 1), where(even - 8, plane >= 2)
        return [jnp.where(core == 0, one, two), jnp.where(core == 0, two, one)]

    def wrapped_numbers(mine):
        plane, _, _, even = parts(mine)
        return [where(even - 12, plane == 3)] * 2

    def across_numbers(mine):
        _, side, _, even = parts(mine)
        return [where(even - 2, side == 1)] * 2

    def middle_numbers(mine):
        return ring_numbers(mine) + wrapped_numbers(mine)

    def last_numbers(mine):
        plane, _, core, even = parts(mine)
        beyond, behind = where(even - 8, plane >= 2), where(even - 4, plane >= 1)
        level_numbers = [where(beyond, core == 1), where(beyond, core == 0)]
        return level_numbers + across_numbers(mine) + wrapped_numbers(mine) + [behind] * 2

    first_pieces = [(near, 0, ROWS)]
    near_query, *carry = attend(place, att_query, own, None, first_pieces, near_numbers)
    carry, message, wrapped, across = tied(carry, message, wrapped, across)
    first = move(message, sibling)
    of_chip, leveled = join_cores(place, message, first, ring)
    level = move(leveled, sideways)
    wrapped_side = move(across, wrapping)
    behind_side = move(across, [(i, i + 4) for i in range(12)])
    bundle = stack(ring, wrapped)
    bundle_near = move(bundle, sibling)
    middle_pieces = [
        (ring, 0, 2 * ROWS),
        (bundle_near, 0, 2 * ROWS),
        (wrapped, 0, ROWS),
        (bundle_near, 2 * ROWS, ROWS),
    ]
    carry = attend(place, near_query, own, carry, middle_pieces, middle_numbers)

    carry, across, wrapped_side, behind_side, level = tied(carry, across, wrapped_side, behind_side, level)
    level_near = move(level, sibling)
    rest = stack(across, wrapped_side, behind_side)
    rest_near = move(rest, sibling)
    of_plane, other_chip = join_sides(place, of_chip, level, level_near)
    state_behind = move(of_plane, last_plane)
    state_beyond = move(of_plane, plane_before)
    last_pieces = [
        (level, 0, 2 * ROWS),
        (level_near, 0, 2 * ROWS),
        (across, 0, ROWS),
        (rest_near, 0, ROWS),
        (wrapped_side, 0, ROWS),
        (rest_near, ROWS, ROWS),
        (behind_side, 0, ROWS),
        (rest_near, 2 * ROWS, ROWS),
    ]
    carry, of_plane = tied(carry, of_plane)
    attention, squares = attend(
        place,
        near_query,
        own,
        carry,
        last_pieces,
        last_numbers,
        first_pieces + middle_pieces,
        lambda mine: near_numbers(mine) + middle_numbers(mine),
    )

    def over(value, bit):
        return lax.ppermute(value, "tp", [(i, i ^ bit) for i in range(8)])

    squares, state_behind, state_beyond = tied(squares, state_behind, state_beyond)
    others = [over(squares, bit) for bit in (2, 4, 6)]
    kept = hand(place, state_behind, state_beyond)
    handed = move(kept, sibling)
    linear = carry_in(place, lh_query, local, grow, kept, handed, other_chip, first, lh_gain)
    others, linear = tied(others, linear)
    squares = squares + others[0] + others[1] + others[2]
    features = HEADS * HD * lax.axis_size("tp")
    return finish(float(features), attention, squares, over(squares, 1), linear, att_gain)


def solution(mesh):
    placed = (P("ctx", "tp"),) * 7 + (P("tp"), P("tp"))
    return jax.shard_map(body, mesh=mesh, in_specs=placed, out_specs=P("ctx", "tp"), check_vma=False)
```

```python
import functools
import math

import jax
import jax.numpy as jnp
from jax import lax
from jax.experimental import pallas as pl
from jax.experimental.pallas import tpu as pltpu
from jax.sharding import PartitionSpec as P

HD = 128
ROWS = 512
HEADS = 6
TILE = 256
EPS = 1e-06
MASKED = -1e30
LOG2E = math.log2(math.e)
SCORE_SCALE = LOG2E / math.sqrt(HD)
SAFE_EXPONENT = 100.0
STATE_ROWS = HEADS * HD + 8
NEVER = 1 << 20

VMEM = pl.BlockSpec(memory_space=pltpu.VMEM)
SMEM = pl.BlockSpec(memory_space=pltpu.SMEM)
f32 = jnp.float32
bf16 = jnp.bfloat16
highest = lax.Precision.HIGHEST


def dot(a, b, contract=((1,), (0,)), precision=None):
    return lax.dot_general(a, b, (contract, ((), ())), precision=precision, preferred_element_type=f32)


def params(megabytes):
    return pltpu.CompilerParams(vmem_limit_bytes=megabytes << 20)


def cost(us):
    return pl.CostEstimate(flops=int(us * 1e9), bytes_accessed=int(us * 1e6), transcendentals=int(us * 1e6))


def head(h):
    return slice(h * HD, (h + 1) * HD)


def recur_kernel(
    q_hbm, k_hbm, v_hbm, step_ref, local_ref, grow_ref, message_ref, padded
):
    k_ref, q_ref, v_ref = k_hbm, q_hbm, v_hbm
    padded[...] = jnp.full((8, ROWS), 0.5, f32)
    padded[:HEADS, :] = step_ref[...]
    step = padded[...]
    rate = step / (1.0 + step)
    total = -jnp.log(1.0 + step) * LOG2E
    place = lax.broadcasted_iota(jnp.int32, (8, ROWS), 1)
    reach = 1
    while reach < ROWS:
        total = total + jnp.where(place >= reach, pltpu.roll(total, reach, 1), 0.0)
        reach *= 2
    source = jnp.log(rate) * LOG2E - total
    end = total[:, ROWS - 1 : ROWS]
    tail = jnp.exp2(end + source)
    rows = jnp.concatenate([total, tail, jnp.zeros((HD - 16, ROWS), f32)], 0)
    columns = jnp.transpose(rows)
    grow_ref[...] = jnp.exp2(columns)
    message_ref[HEADS * HD :, :] = jnp.broadcast_to(end, (8, HD))
    at_row = lax.broadcasted_iota(jnp.int32, (TILE, TILE), 0)
    at_column = lax.broadcasted_iota(jnp.int32, (TILE, TILE), 1)
    seen = at_column <= at_row
    for h in range(HEADS):
        keys = k_ref[:, head(h)].astype(f32)
        keys = keys * lax.rsqrt(jnp.sum(keys * keys, -1, keepdims=True) + EPS)
        unit = keys.astype(bf16)
        values = v_ref[:, head(h)]
        for a in range(0, ROWS, TILE):
            result = None
            for b in range(0, a + TILE, TILE):
                scores = dot(q_ref[a : a + TILE, head(h)], unit[b : b + TILE], ((1,), (1,)))
                decay = jnp.exp2(columns[a : a + TILE, h : h + 1] + source[h : h + 1, b : b + TILE])
                weights = scores * decay
                if a == b:
                    weights = jnp.where(seen, weights, 0.0)
                part = dot(weights.astype(bf16), values[b : b + TILE])
                result = part if result is None else result + part
            local_ref[a : a + TILE, head(h)] = result
        tailed = (values.astype(f32) * columns[:, 8 + h : 9 + h]).astype(bf16)
        message_ref[head(h), :] = dot(unit, tailed, ((0,), (0,)))


def recur(lh_query, lh_key, lh_value, lh_step):
    return pl.pallas_call(
        recur_kernel,
        out_shape=(
            jax.ShapeDtypeStruct((ROWS, HEADS * HD), f32),
            jax.ShapeDtypeStruct((ROWS, HD), f32),
            jax.ShapeDtypeStruct((STATE_ROWS, HD), f32),
        ),
        in_specs=[VMEM] * 4,
        out_specs=(VMEM,) * 3,
        scratch_shapes=[pltpu.VMEM((8, ROWS), f32)]
,
        compiler_params=params(16),
        cost_estimate=cost(0.2),
        name="recur",
    )(lh_query, lh_key, lh_value, lh_step)


def beside_kernel(key_ref, value_ref, out_ref):
    out_ref[:, :HD] = key_ref[...]
    out_ref[:, HD:] = value_ref[...]


def beside(key, value):
    return pl.pallas_call(
        beside_kernel,
        out_shape=jax.ShapeDtypeStruct((ROWS, 2 * HD), bf16),
        in_specs=[VMEM, VMEM],
        out_specs=VMEM,
        compiler_params=params(14),
        name="beside",
    )(key, value)


def stack_kernel(*refs):
    *parts, out_ref = refs
    at = 0
    for part in parts:
        out_ref[at : at + part.shape[0], :] = part[...]
        at += part.shape[0]


def stack(*parts):
    return pl.pallas_call(
        stack_kernel,
        out_shape=jax.ShapeDtypeStruct((sum(part.shape[0] for part in parts), 2 * HD), bf16),
        in_specs=[VMEM] * len(parts),
        out_specs=VMEM,
        compiler_params=params(14),
        name="stack",
    )(*parts)


def follow(early, late):
    logs = early[1] + late[1]
    states = [jnp.exp2(late[1][h : h + 1, :]) * early[0][h] + late[0][h] for h in range(HEADS)]
    return states, logs


def state_of(ref, wanted=None):
    states = [ref[head(h), :] for h in range(HEADS)]
    logs = ref[HEADS * HD :, :]
    if wanted is None:
        return states, logs
    return [jnp.where(wanted, state, 0.0) for state in states], jnp.where(wanted, logs, 0.0)


def put_state(ref, value):
    for h in range(HEADS):
        ref[head(h), :] = value[0][h]
    ref[HEADS * HD :, :] = value[1]


def select(wanted, one, two):
    return [jnp.where(wanted, a, b) for a, b in zip(one[0], two[0])], jnp.where(wanted, one[1], two[1])


def follow_in_order(own_first, own, other):
    return follow(select(own_first, own, other), select(own_first, other, own))


def split(value):
    upper = value.astype(bf16)
    return jnp.concatenate([upper, (value - upper.astype(f32)).astype(bf16)], 1)


def merge(both):
    return both[:, :HD].astype(f32) + both[:, HD:].astype(f32)


def join_cores_kernel(mine_ref, own_ref, other_ref, blocks_ref, out_ref, message_ref):
    even = mine_ref[0] % 2 == 0
    joined = follow_in_order(even, state_of(own_ref), state_of(other_ref))
    put_state(out_ref, joined)
    message_ref[...] = blocks_ref[...]

    @pl.when(even)
    def _():
        for h in range(HEADS):
            message_ref[head(h), :] = split(joined[0][h])
        logs = jnp.concatenate([joined[1], jnp.zeros((8, HD), f32)], 0)
        message_ref[HEADS * HD : HEADS * HD + 16, :] = split(logs)


def join_cores(mine, own, other, blocks):
    return pl.pallas_call(
        join_cores_kernel,
        out_shape=(
            jax.ShapeDtypeStruct((STATE_ROWS, HD), f32),
            jax.ShapeDtypeStruct((2 * ROWS, 2 * HD), bf16),
        ),
        in_specs=[SMEM] + [VMEM] * 3,
        out_specs=(VMEM,) * 2,
        compiler_params=params(14),
        cost_estimate=cost(0.2),
        name="join_cores",
    )(mine, own, other, blocks)


def join_sides_kernel(mine_ref, own_ref, level_ref, level_near_ref, out_ref, other_ref):
    mine = mine_ref[0]
    even = mine % 2 == 0

    def brought(ref):
        logs = merge(ref[HEADS * HD : HEADS * HD + 16, :])[:8, :]
        return [merge(ref[head(h), :]) for h in range(HEADS)], logs

    other = select(even, brought(level_ref), brought(level_near_ref))
    put_state(other_ref, other)
    put_state(out_ref, follow_in_order((mine // 2) % 2 == 0, state_of(own_ref), other))


def join_sides(mine, own, level, level_near):
    return pl.pallas_call(
        join_sides_kernel,
        out_shape=(jax.ShapeDtypeStruct((STATE_ROWS, HD), f32),) * 2,
        in_specs=[SMEM] + [VMEM] * 3,
        out_specs=(VMEM,) * 2,
        compiler_params=params(14),
        cost_estimate=cost(0.2),
        name="join_sides",
    )(mine, own, level, level_near)


def hand_kernel(mine_ref, behind_ref, beyond_ref, out_ref):
    plane, core = mine_ref[0] // 4, mine_ref[0] % 2
    behind = state_of(behind_ref, (plane == 3) | (core == 0))
    beyond = state_of(beyond_ref, (plane >= 2) & (core == 1))
    put_state(out_ref, follow(behind, beyond))


def hand(mine, behind, beyond):
    return pl.pallas_call(
        hand_kernel,
        out_shape=jax.ShapeDtypeStruct((STATE_ROWS, HD), f32),
        in_specs=[SMEM, VMEM, VMEM],
        out_specs=VMEM,
        compiler_params=params(14),
        cost_estimate=cost(0.2),
        name="hand",
    )(mine, behind, beyond)


def attend_kernel(first, last, numbers_of, pieces, kept_numbers_of, kept, mine_ref, query_ref, own_ref, *refs):
    mine = mine_ref[0]
    refs = list(refs)

    def take(count):
        return [refs.pop(0) for _ in range(count)]

    if not first:
        carry_ref, count_ref, top_in_ref = take(3)
    block_refs = [(ref, *piece) for ref, piece in zip(take(len(pieces)), pieces)]
    kept_refs = [(ref, *piece) for ref, piece in zip(take(len(kept)), kept)]
    if last:
        out_ref, square_ref, sums, keys, values, top_ref, tops = refs
    else:
        if first:
            (passed_ref,) = take(1)
            passed_ref[...] = query_ref[...]
        numerator_ref, counted_ref, top_ref, sums, keys, values = refs

    def highest_of(part):
        return jnp.max(jnp.abs(part).reshape(-1, 16, HD), 0)

    def fill(blocks, numbers):
        filled = jnp.int32(0)
        for (block, start, rows), number in zip(blocks, numbers):
            takes = number < mine
            place = filled

            @pl.when(takes)
            def _():
                at = pl.ds(pl.multiple_of(place * ROWS, ROWS), rows)
                block_keys = block[start : start + rows, :HD]
                keys[at, :] = block_keys
                values[at, :HD] = block[start : start + rows, HD:]
                top_ref[16:32, :] = jnp.maximum(top_ref[16:32, :], highest_of(block_keys))

            filled = filled + jnp.where(takes, rows // ROWS, 0)
        return filled

    if first:
        top_ref[16:32, :] = highest_of(own_ref[:, :HD])
        longest = jnp.zeros((ROWS, HD), f32)
        ones = jnp.ones((HD, HD), bf16)
        for h in range(HEADS):
            query = query_ref[:, head(h)].astype(f32)
            longest = jnp.maximum(longest, dot((query * query).astype(bf16), ones))
        top_ref[0:16, :] = jnp.max(longest.reshape(-1, 16, HD), 0).astype(bf16)
    else:
        top_ref[...] = top_in_ref[...]
    values[:, HD:] = jnp.ones((values.shape[0], HD), bf16)
    filled = fill(block_refs, numbers_of(mine))
    sums[...] = jnp.zeros_like(sums)

    def visit(start, count):
        at = pl.ds(pl.multiple_of(start, ROWS), count)
        block_keys = keys[at, :]
        block_values = values[at, :]
        for h in range(HEADS):
            for a in range(0, ROWS, TILE):
                scores = dot(query_ref[a : a + TILE, head(h)], block_keys, ((1,), (1,)))
                weights = jnp.exp2(scores * SCORE_SCALE).astype(bf16)
                sums[h, a : a + TILE, :] += dot(weights, block_values)

    def pair(n, _):
        visit(n * 2 * ROWS, 2 * ROWS)
        return 0

    if not first:
        lax.fori_loop(0, filled // 2, pair, 0)

    if first:

        @pl.when(filled > 0)
        def _():
            visit(0, ROWS)

        at_row = lax.broadcasted_iota(jnp.int32, (TILE, TILE), 0)
        at_column = lax.broadcasted_iota(jnp.int32, (TILE, TILE), 1)
        seen = at_column <= at_row
        values[:ROWS, :HD] = own_ref[:, HD:]
        for h in range(HEADS):
            for a in range(0, ROWS, TILE):
                for b in range(0, a + TILE, TILE):
                    scores = dot(query_ref[a : a + TILE, head(h)], own_ref[b : b + TILE, :HD], ((1,), (1,)))
                    weights = jnp.exp2(scores * SCORE_SCALE)
                    if a == b:
                        weights = jnp.where(seen, weights, 0.0)
                    sums[h, a : a + TILE, :] += dot(weights.astype(bf16), values[b : b + TILE, :])
            numerator_ref[:, head(h)] = sums[h, :, :HD]
            counted_ref[:, h : h + 1] = sums[h, :, HD : HD + 1]
    elif not last:
        for h in range(HEADS):
            numerator_ref[:, head(h)] = sums[h, :, :HD] + carry_ref[:, head(h)]
            counted_ref[:, h : h + 1] = sums[h, :, HD : HD + 1] + count_ref[:, h : h + 1]
    else:
        key_top = jnp.max(top_ref[16:32, :].astype(f32), 0, keepdims=True)
        bound = jnp.max(top_ref[0:16, :].astype(f32)) * jnp.sum(key_top * key_top) * SCORE_SCALE**2
        large = bound * 1.05 > SAFE_EXPONENT * SAFE_EXPONENT

        @pl.when(large)
        def _():
            before = fill(kept_refs + block_refs, kept_numbers_of(mine) + numbers_of(mine))
            at = pl.ds(pl.multiple_of(before * ROWS, ROWS), ROWS)
            keys[at, :] = own_ref[:, :HD]
            values[at, :HD] = own_ref[:, HD:]
            sums[...] = jnp.zeros_like(sums)
            tops[...] = jnp.full_like(tops, MASKED)

            def step(n, _):
                at = pl.ds(pl.multiple_of((n // (2 * HEADS)) * ROWS, ROWS), ROWS)
                h = (n % (2 * HEADS)) // 2
                a = (n % 2) * TILE
                rows = pl.ds(pl.multiple_of(a, TILE), TILE)
                query = query_ref[rows, pl.ds(pl.multiple_of(h * HD, HD), HD)]
                scores = dot(query, keys[at, :], ((1,), (1,))) * SCORE_SCALE
                row = lax.broadcasted_iota(jnp.int32, (TILE, ROWS), 0) + a
                column = lax.broadcasted_iota(jnp.int32, (TILE, ROWS), 1)
                column = column - jnp.where(n // (2 * HEADS) < before, ROWS, 0)
                visible = column <= row
                scores = jnp.where(visible, scores, MASKED)
                old = tops[h, rows, :]
                new = jnp.maximum(old[:, :1], jnp.max(scores, 1, keepdims=True))
                weights = jnp.where(visible, jnp.exp2(scores - new), 0.0).astype(bf16)
                sums[h, rows, :] = sums[h, rows, :] * jnp.exp2(old[:, :1] - new) + dot(weights, values[at, :])
                tops[h, rows, :] = jnp.broadcast_to(new, (TILE, HD))
                return 0

            lax.fori_loop(0, (before + 1) * 2 * HEADS, step, 0)

        squares = jnp.zeros((ROWS, HD), f32)
        for h in range(HEADS):
            count = sums[h, :, HD:] + jnp.where(large, 0.0, count_ref[:, h : h + 1])
            result = (sums[h, :, :HD] + jnp.where(large, 0.0, carry_ref[:, head(h)])) / count
            result = result.astype(bf16)
            out_ref[:, head(h)] = result
            result = result.astype(f32)
            squares = squares + result * result
        square_ref[...] = dot(jnp.ones((8, HD), f32), squares, ((1,), (1,)), highest)


def attend(mine, query, own, carry, blocks, numbers_of, kept=None, kept_numbers_of=None):
    first, last = carry is None, kept is not None
    kept = kept or []
    size = 16 * ROWS if last else sum(rows for _, _, rows in blocks)
    operands = [query, own] + list(carry or []) + [block for block, _, _ in blocks + kept]
    top = (32, HD)
    scratch = [
        pltpu.VMEM((HEADS, ROWS, 2 * HD), f32),
        pltpu.VMEM((size, HD), bf16),
        pltpu.VMEM((size, 2 * HD), bf16),
    ]
    if last:
        out_shape = (
            jax.ShapeDtypeStruct((ROWS, HEADS * HD), bf16),
            jax.ShapeDtypeStruct((8, ROWS), f32),
        )
        scratch += [pltpu.VMEM(top, bf16), pltpu.VMEM((HEADS, ROWS, HD), f32)]
    else:
        out_shape = (
            jax.ShapeDtypeStruct((ROWS, HEADS * HD), f32),
            jax.ShapeDtypeStruct((ROWS, HD), f32),
            jax.ShapeDtypeStruct(top, bf16),
        )
        if first:
            out_shape = (jax.ShapeDtypeStruct((ROWS, HEADS * HD), bf16),) + out_shape
    return pl.pallas_call(
        functools.partial(
            attend_kernel,
            first,
            last,
            numbers_of,
            [block[1:] for block in blocks],
            kept_numbers_of,
            [block[1:] for block in kept],
        ),
        out_shape=out_shape,
        in_specs=[SMEM] + [VMEM] * len(operands),
        out_specs=(VMEM,) * len(out_shape),
        scratch_shapes=scratch,
        compiler_params=params(20),
        cost_estimate=cost(0.2),
        name="attend_first" if first else "attend_last" if last else "attend_middle",
    )(mine, *operands)


def carry_kernel(
    mine_ref,
    query_hbm,
    local_ref,
    grow_ref,
    kept_ref,
    handed_ref,
    chip_ref,
    core_ref,
    gain_ref,
    out_ref,
):
    mine = mine_ref[0]
    query_ref = query_hbm
    plane, side, core = mine // 4, (mine // 2) % 2, mine % 2
    kept, handed = state_of(kept_ref), state_of(handed_ref)

    def pick(one, two, wanted):
        states = [jnp.where(wanted, jnp.where(core == 0, a, b), 0.0) for a, b in zip(one[0], two[0])]
        return states, jnp.where(wanted, jnp.where(core == 0, one[1], two[1]), 0.0)

    entering = pick(handed, kept, plane >= 2)
    entering = follow(entering, pick(kept, handed, plane >= 1))
    entering = follow(entering, state_of(chip_ref, side == 1))
    entering = follow(entering, state_of(core_ref, core == 1))
    grow = grow_ref[...]
    for h in range(HEADS):
        state = entering[0][h]
        upper = state.astype(bf16)
        lower = (state - upper.astype(f32)).astype(bf16)
        both = dot(query_ref[:, head(h)], jnp.concatenate([upper, lower], 1))
        entered = both[:, :HD] + both[:, HD:]
        result = local_ref[:, head(h)] + entered * grow[:, h : h + 1]
        square = jnp.mean(result * result, -1, keepdims=True)
        out_ref[:, head(h)] = result * lax.rsqrt(square + EPS) * gain_ref[head(h)][None, :]


def finish_kernel(features, attention_ref, linear_ref, gain_ref, *refs):
    *square_refs, out_ref = refs
    total = square_refs[0][...]
    for square_ref in square_refs[1:]:
        total = total + square_ref[...]
    factor = lax.rsqrt(total / features + EPS)
    factor = dot(factor, jnp.full((8, HD), 0.125, f32), ((0,), (0,)), highest)
    for h in range(HEADS):
        part = attention_ref[:, head(h)].astype(f32) * factor * gain_ref[head(h)][None, :]
        out_ref[:, head(h)] = (part + linear_ref[:, head(h)]).astype(bf16)


def carry_in(place, lh_query, *operands):
    return pl.pallas_call(
        carry_kernel,
        out_shape=jax.ShapeDtypeStruct((ROWS, HEADS * HD), f32),
        in_specs=[SMEM, VMEM] + [VMEM] * len(operands),
        out_specs=VMEM,
        compiler_params=params(14),
        cost_estimate=cost(0.2),
        name="carry",
    )(place, lh_query, *operands)


def finish(features, *operands):
    return pl.pallas_call(
        functools.partial(finish_kernel, features),
        out_shape=jax.ShapeDtypeStruct((ROWS, HEADS * HD), bf16),
        in_specs=[VMEM] * len(operands),
        out_specs=VMEM,
        compiler_params=params(14),
        cost_estimate=cost(0.2),
        name="finish",
    )(*operands)


def body(att_query, att_key, att_value, lh_query, lh_key, lh_value, lh_step, att_gain, lh_gain):
    mine = lax.axis_index("ctx")
    place = mine.reshape(1).astype(jnp.int32)

    def move(value, pairs):
        return lax.ppermute(value, "ctx", pairs)

    every = range(16)
    sibling = [(i, i ^ 1) for i in every]
    sideways = [(i, i ^ 2) for i in every]
    onward = [(i, i + 4) for i in every if i % 2 == 0 and i < 12] + [(i, i + 8) for i in every if i % 2 == 1 and i < 8]
    wrapping = [(i, i + 12) for i in range(4)]
    last_plane = [(i, i + 4) for i in every if i % 2 == 0 and i < 12] + [(i, i + 12) for i in (1, 3)]
    plane_before = [(i, i + 8) for i in every if i % 2 == 1 and i < 8]

    def tied(*values):
        return lax.optimization_barrier(values)

    lh_query, lh_key, lh_value, far_query, att_key, att_value = [
        array
        for array in (lh_query, lh_key, lh_value, att_query, att_key, att_value)
    ]
    lh_step = lh_step.T
    att_query, lh_query, lh_key, lh_value, att_key, att_value = [
        pltpu.with_memory_space_constraint(array, pltpu.HBM)
        for array in (att_query, lh_query, lh_key, lh_value, att_key, att_value)
    ]
    own = beside(att_key, att_value)
    across = move(own, [(i, j) for i, j in sideways if i < 12 or i % 4 < 2])
    wrapped = move(own, wrapping)
    near = move(own, sibling)
    chip = stack(own, near)
    chip, lh_step = tied(chip, lh_step)
    lh_step = pltpu.with_memory_space_constraint(lh_step, pltpu.HBM)
    ring = move(chip, onward)

    local, grow, message = recur(lh_query, lh_key, lh_value, lh_step)

    def where(number, wanted):
        return jnp.where(wanted, number, NEVER)

    def parts(mine):
        return mine // 4, (mine // 2) % 2, mine % 2, mine - mine % 2

    def near_numbers(mine):
        return [where(mine - 1, mine % 2 == 1)]

    def ring_numbers(mine):
        plane, _, core, even = parts(mine)
        one, two = where(even - 4, plane >= 1), where(even - 8, plane >= 2)
        return [jnp.where(core == 0, one, two), jnp.where(core == 0, two, one)]

    def wrapped_numbers(mine):
        plane, _, _, even = parts(mine)
        return [where(even - 12, plane == 3)] * 2

    def across_numbers(mine):
        _, side, _, even = parts(mine)
        return [where(even - 2, side == 1)] * 2

    def middle_numbers(mine):
        return ring_numbers(mine) + wrapped_numbers(mine)

    def last_numbers(mine):
        plane, _, core, even = parts(mine)
        beyond, behind = where(even - 8, plane >= 2), where(even - 4, plane >= 1)
        level_numbers = [where(beyond, core == 1), where(beyond, core == 0)]
        return level_numbers + across_numbers(mine) + wrapped_numbers(mine) + [behind] * 2

    first_pieces = [(near, 0, ROWS)]
    near_query, *carry = attend(place, att_query, own, None, first_pieces, near_numbers)
    carry, message, wrapped, across = tied(carry, message, wrapped, across)
    first = move(message, sibling)
    of_chip, leveled = join_cores(place, message, first, ring)
    level = move(leveled, sideways)
    wrapped_side = move(across, wrapping)
    behind_side = move(across, [(i, i + 4) for i in range(12)])
    bundle = stack(ring, wrapped)
    bundle_near = move(bundle, sibling)
    middle_pieces = [
        (ring, 0, 2 * ROWS),
        (bundle_near, 0, 2 * ROWS),
        (wrapped, 0, ROWS),
        (bundle_near, 2 * ROWS, ROWS),
    ]
    carry = attend(place, near_query, own, carry, middle_pieces, middle_numbers)

    carry, across, wrapped_side, behind_side, level = tied(carry, across, wrapped_side, behind_side, level)
    level_near = move(level, sibling)
    rest = stack(across, wrapped_side, behind_side)
    rest_near = move(rest, sibling)
    of_plane, other_chip = join_sides(place, of_chip, level, level_near)
    state_behind = move(of_plane, last_plane)
    state_beyond = move(of_plane, plane_before)
    last_pieces = [
        (level, 0, 2 * ROWS),
        (level_near, 0, 2 * ROWS),
        (across, 0, ROWS),
        (rest_near, 0, ROWS),
        (wrapped_side, 0, ROWS),
        (rest_near, ROWS, ROWS),
        (behind_side, 0, ROWS),
        (rest_near, 2 * ROWS, ROWS),
    ]
    carry, of_plane = tied(carry, of_plane)
    attention, squares = attend(
        place,
        near_query,
        own,
        carry,
        last_pieces,
        last_numbers,
        first_pieces + middle_pieces,
        lambda mine: near_numbers(mine) + middle_numbers(mine),
    )

    def over(value, bit):
        return lax.ppermute(value, "tp", [(i, i ^ bit) for i in range(8)])

    squares, state_behind, state_beyond = tied(squares, state_behind, state_beyond)
    others = [over(squares, bit) for bit in range(1, 8)]
    kept = hand(place, state_behind, state_beyond)
    handed = move(kept, sibling)
    linear = carry_in(place, lh_query, local, grow, kept, handed, other_chip, first, lh_gain)
    others, linear = tied(others, linear)
    features = HEADS * HD * lax.axis_size("tp")
    return finish(float(features), attention, linear, att_gain, squares, *others)


def solution(mesh):
    placed = (P("ctx", "tp"),) * 7 + (P("tp"), P("tp"))
    return jax.shard_map(body, mesh=mesh, in_specs=placed, out_specs=P("ctx", "tp"), check_vma=False)
```

```python
import functools
import math

import jax
import jax.numpy as jnp
from jax import lax
from jax.experimental import pallas as pl
from jax.experimental.pallas import tpu as pltpu
from jax.sharding import PartitionSpec as P

HD = 128
ROWS = 512
HEADS = 6
TILE = 256
EPS = 1e-06
MASKED = -1e30
LOG2E = math.log2(math.e)
SCORE_SCALE = LOG2E / math.sqrt(HD)
SAFE_EXPONENT = 100.0
STATE_ROWS = HEADS * HD + 8
NEVER = 1 << 20

VMEM = pl.BlockSpec(memory_space=pltpu.VMEM)
SMEM = pl.BlockSpec(memory_space=pltpu.SMEM)
f32 = jnp.float32
bf16 = jnp.bfloat16
highest = lax.Precision.HIGHEST


def dot(a, b, contract=((1,), (0,)), precision=None):
    return lax.dot_general(a, b, (contract, ((), ())), precision=precision, preferred_element_type=f32)


def params(megabytes):
    return pltpu.CompilerParams(vmem_limit_bytes=megabytes << 20)


def cost(us):
    return pl.CostEstimate(flops=int(us * 1e9), bytes_accessed=int(us * 1e6), transcendentals=int(us * 1e6))


def head(h):
    return slice(h * HD, (h + 1) * HD)


def recur_kernel(
    q_hbm, k_hbm, v_hbm, step_ref, local_ref, grow_ref, message_ref, padded
):
    k_ref, q_ref, v_ref = k_hbm, q_hbm, v_hbm
    padded[...] = jnp.full((8, ROWS), 0.5, f32)
    padded[:HEADS, :] = step_ref[...]
    step = padded[...]
    rate = step / (1.0 + step)
    total = -jnp.log(1.0 + step) * LOG2E
    place = lax.broadcasted_iota(jnp.int32, (8, ROWS), 1)
    reach = 1
    while reach < ROWS:
        total = total + jnp.where(place >= reach, pltpu.roll(total, reach, 1), 0.0)
        reach *= 2
    source = jnp.log(rate) * LOG2E - total
    end = total[:, ROWS - 1 : ROWS]
    tail = jnp.exp2(end + source)
    rows = jnp.concatenate([total, tail, jnp.zeros((HD - 16, ROWS), f32)], 0)
    columns = jnp.transpose(rows)
    grow_ref[...] = jnp.exp2(columns)
    message_ref[HEADS * HD :, :] = jnp.broadcast_to(end, (8, HD))
    at_row = lax.broadcasted_iota(jnp.int32, (TILE, TILE), 0)
    at_column = lax.broadcasted_iota(jnp.int32, (TILE, TILE), 1)
    seen = at_column <= at_row
    for h in range(HEADS):
        keys = k_ref[:, head(h)].astype(f32)
        keys = keys * lax.rsqrt(jnp.sum(keys * keys, -1, keepdims=True) + EPS)
        unit = keys.astype(bf16)
        values = v_ref[:, head(h)]
        for a in range(0, ROWS, TILE):
            result = None
            for b in range(0, a + TILE, TILE):
                scores = dot(q_ref[a : a + TILE, head(h)], unit[b : b + TILE], ((1,), (1,)))
                decay = jnp.exp2(columns[a : a + TILE, h : h + 1] + source[h : h + 1, b : b + TILE])
                weights = scores * decay
                if a == b:
                    weights = jnp.where(seen, weights, 0.0)
                part = dot(weights.astype(bf16), values[b : b + TILE])
                result = part if result is None else result + part
            local_ref[a : a + TILE, head(h)] = result
        tailed = (values.astype(f32) * columns[:, 8 + h : 9 + h]).astype(bf16)
        message_ref[head(h), :] = dot(unit, tailed, ((0,), (0,)))


def recur(lh_query, lh_key, lh_value, lh_step):
    return pl.pallas_call(
        recur_kernel,
        out_shape=(
            jax.ShapeDtypeStruct((ROWS, HEADS * HD), f32),
            jax.ShapeDtypeStruct((ROWS, HD), f32),
            jax.ShapeDtypeStruct((STATE_ROWS, HD), f32),
        ),
        in_specs=[VMEM] * 4,
        out_specs=(VMEM,) * 3,
        scratch_shapes=[pltpu.VMEM((8, ROWS), f32)]
,
        compiler_params=params(16),
        cost_estimate=cost(0.2),
        name="recur",
    )(lh_query, lh_key, lh_value, lh_step)


def beside_kernel(key_ref, value_ref, out_ref):
    out_ref[:, :HD] = key_ref[...]
    out_ref[:, HD:] = value_ref[...]


def beside(key, value):
    return pl.pallas_call(
        beside_kernel,
        out_shape=jax.ShapeDtypeStruct((ROWS, 2 * HD), bf16),
        in_specs=[VMEM, VMEM],
        out_specs=VMEM,
        compiler_params=params(14),
        name="beside",
    )(key, value)


def stack_kernel(*refs):
    *parts, out_ref = refs
    at = 0
    for part in parts:
        out_ref[at : at + part.shape[0], :] = part[...]
        at += part.shape[0]


def stack(*parts):
    return pl.pallas_call(
        stack_kernel,
        out_shape=jax.ShapeDtypeStruct((sum(part.shape[0] for part in parts), 2 * HD), bf16),
        in_specs=[VMEM] * len(parts),
        out_specs=VMEM,
        compiler_params=params(14),
        name="stack",
    )(*parts)


def follow(early, late):
    logs = early[1] + late[1]
    states = [jnp.exp2(late[1][h : h + 1, :]) * early[0][h] + late[0][h] for h in range(HEADS)]
    return states, logs


def state_of(ref, wanted=None):
    states = [ref[head(h), :] for h in range(HEADS)]
    logs = ref[HEADS * HD :, :]
    if wanted is None:
        return states, logs
    return [jnp.where(wanted, state, 0.0) for state in states], jnp.where(wanted, logs, 0.0)


def put_state(ref, value):
    for h in range(HEADS):
        ref[head(h), :] = value[0][h]
    ref[HEADS * HD :, :] = value[1]


def select(wanted, one, two):
    return [jnp.where(wanted, a, b) for a, b in zip(one[0], two[0])], jnp.where(wanted, one[1], two[1])


def follow_in_order(own_first, own, other):
    return follow(select(own_first, own, other), select(own_first, other, own))


def split(value):
    upper = value.astype(bf16)
    return jnp.concatenate([upper, (value - upper.astype(f32)).astype(bf16)], 1)


def merge(both):
    return both[:, :HD].astype(f32) + both[:, HD:].astype(f32)


def join_cores_kernel(mine_ref, own_ref, other_ref, blocks_ref, out_ref, message_ref):
    even = mine_ref[0] % 2 == 0
    joined = follow_in_order(even, state_of(own_ref), state_of(other_ref))
    put_state(out_ref, joined)
    message_ref[...] = blocks_ref[...]

    @pl.when(even)
    def _():
        for h in range(HEADS):
            message_ref[head(h), :] = split(joined[0][h])
        logs = jnp.concatenate([joined[1], jnp.zeros((8, HD), f32)], 0)
        message_ref[HEADS * HD : HEADS * HD + 16, :] = split(logs)


def join_cores(mine, own, other, blocks):
    return pl.pallas_call(
        join_cores_kernel,
        out_shape=(
            jax.ShapeDtypeStruct((STATE_ROWS, HD), f32),
            jax.ShapeDtypeStruct((2 * ROWS, 2 * HD), bf16),
        ),
        in_specs=[SMEM] + [VMEM] * 3,
        out_specs=(VMEM,) * 2,
        compiler_params=params(14),
        cost_estimate=cost(0.2),
        name="join_cores",
    )(mine, own, other, blocks)


def join_sides_kernel(mine_ref, own_ref, level_ref, level_near_ref, out_ref, other_ref):
    mine = mine_ref[0]
    even = mine % 2 == 0

    def brought(ref):
        logs = merge(ref[HEADS * HD : HEADS * HD + 16, :])[:8, :]
        return [merge(ref[head(h), :]) for h in range(HEADS)], logs

    other = select(even, brought(level_ref), brought(level_near_ref))
    put_state(other_ref, other)
    put_state(out_ref, follow_in_order((mine // 2) % 2 == 0, state_of(own_ref), other))


def join_sides(mine, own, level, level_near):
    return pl.pallas_call(
        join_sides_kernel,
        out_shape=(jax.ShapeDtypeStruct((STATE_ROWS, HD), f32),) * 2,
        in_specs=[SMEM] + [VMEM] * 3,
        out_specs=(VMEM,) * 2,
        compiler_params=params(14),
        cost_estimate=cost(0.2),
        name="join_sides",
    )(mine, own, level, level_near)


def hand_kernel(mine_ref, behind_ref, beyond_ref, out_ref):
    plane, core = mine_ref[0] // 4, mine_ref[0] % 2
    behind = state_of(behind_ref, (plane == 3) | (core == 0))
    beyond = state_of(beyond_ref, (plane >= 2) & (core == 1))
    put_state(out_ref, follow(behind, beyond))


def hand(mine, behind, beyond):
    return pl.pallas_call(
        hand_kernel,
        out_shape=jax.ShapeDtypeStruct((STATE_ROWS, HD), f32),
        in_specs=[SMEM, VMEM, VMEM],
        out_specs=VMEM,
        compiler_params=params(14),
        cost_estimate=cost(0.2),
        name="hand",
    )(mine, behind, beyond)


def attend_kernel(first, last, numbers_of, pieces, kept_numbers_of, kept, mine_ref, query_ref, own_ref, *refs):
    mine = mine_ref[0]
    refs = list(refs)

    def take(count):
        return [refs.pop(0) for _ in range(count)]

    if not first:
        carry_ref, count_ref, top_in_ref = take(3)
    block_refs = [(ref, *piece) for ref, piece in zip(take(len(pieces)), pieces)]
    kept_refs = [(ref, *piece) for ref, piece in zip(take(len(kept)), kept)]
    if last:
        out_ref, square_ref, sums, keys, values, top_ref, tops = refs
    else:
        if first:
            (passed_ref,) = take(1)
            passed_ref[...] = query_ref[...]
        numerator_ref, counted_ref, top_ref, sums, keys, values = refs

    def highest_of(part):
        return jnp.max(jnp.abs(part).reshape(-1, 16, HD), 0)

    def fill(blocks, numbers):
        filled = jnp.int32(0)
        for (block, start, rows), number in zip(blocks, numbers):
            takes = number < mine
            place = filled

            @pl.when(takes)
            def _():
                at = pl.ds(pl.multiple_of(place * ROWS, ROWS), rows)
                block_keys = block[start : start + rows, :HD]
                keys[at, :] = block_keys
                values[at, :HD] = block[start : start + rows, HD:]
                top_ref[16:32, :] = jnp.maximum(top_ref[16:32, :], highest_of(block_keys))

            filled = filled + jnp.where(takes, rows // ROWS, 0)
        return filled

    if first:
        top_ref[16:32, :] = highest_of(own_ref[:, :HD])
        longest = jnp.zeros((ROWS, HD), f32)
        ones = jnp.ones((HD, HD), bf16)
        for h in range(HEADS):
            query = query_ref[:, head(h)].astype(f32)
            longest = jnp.maximum(longest, dot((query * query).astype(bf16), ones))
        top_ref[0:16, :] = jnp.max(longest.reshape(-1, 16, HD), 0).astype(bf16)
    else:
        top_ref[...] = top_in_ref[...]
    values[:, HD:] = jnp.ones((values.shape[0], HD), bf16)
    filled = fill(block_refs, numbers_of(mine))
    sums[...] = jnp.zeros_like(sums)

    def visit(start, count):
        at = pl.ds(pl.multiple_of(start, ROWS), count)
        block_keys = keys[at, :]
        block_values = values[at, :]
        for h in range(HEADS):
            for a in range(0, ROWS, TILE):
                scores = dot(query_ref[a : a + TILE, head(h)], block_keys, ((1,), (1,)))
                weights = jnp.exp2(scores * SCORE_SCALE).astype(bf16)
                sums[h, a : a + TILE, :] += dot(weights, block_values)

    def pair(n, _):
        visit(n * 2 * ROWS, 2 * ROWS)
        return 0

    if not first:
        lax.fori_loop(0, filled // 2, pair, 0)

    if first:

        @pl.when(filled > 0)
        def _():
            visit(0, ROWS)

        at_row = lax.broadcasted_iota(jnp.int32, (TILE, TILE), 0)
        at_column = lax.broadcasted_iota(jnp.int32, (TILE, TILE), 1)
        seen = at_column <= at_row
        values[:ROWS, :HD] = own_ref[:, HD:]
        for h in range(HEADS):
            for a in range(0, ROWS, TILE):
                for b in range(0, a + TILE, TILE):
                    scores = dot(query_ref[a : a + TILE, head(h)], own_ref[b : b + TILE, :HD], ((1,), (1,)))
                    weights = jnp.exp2(scores * SCORE_SCALE)
                    if a == b:
                        weights = jnp.where(seen, weights, 0.0)
                    sums[h, a : a + TILE, :] += dot(weights.astype(bf16), values[b : b + TILE, :])
            numerator_ref[:, head(h)] = sums[h, :, :HD]
            counted_ref[:, h : h + 1] = sums[h, :, HD : HD + 1]
    elif not last:
        for h in range(HEADS):
            numerator_ref[:, head(h)] = sums[h, :, :HD] + carry_ref[:, head(h)]
            counted_ref[:, h : h + 1] = sums[h, :, HD : HD + 1] + count_ref[:, h : h + 1]
    else:
        key_top = jnp.max(top_ref[16:32, :].astype(f32), 0, keepdims=True)
        bound = jnp.max(top_ref[0:16, :].astype(f32)) * jnp.sum(key_top * key_top) * SCORE_SCALE**2
        large = bound * 1.05 > SAFE_EXPONENT * SAFE_EXPONENT

        @pl.when(large)
        def _():
            before = fill(kept_refs + block_refs, kept_numbers_of(mine) + numbers_of(mine))
            at = pl.ds(pl.multiple_of(before * ROWS, ROWS), ROWS)
            keys[at, :] = own_ref[:, :HD]
            values[at, :HD] = own_ref[:, HD:]
            sums[...] = jnp.zeros_like(sums)
            tops[...] = jnp.full_like(tops, MASKED)

            def step(n, _):
                at = pl.ds(pl.multiple_of((n // (2 * HEADS)) * ROWS, ROWS), ROWS)
                h = (n % (2 * HEADS)) // 2
                a = (n % 2) * TILE
                rows = pl.ds(pl.multiple_of(a, TILE), TILE)
                query = query_ref[rows, pl.ds(pl.multiple_of(h * HD, HD), HD)]
                scores = dot(query, keys[at, :], ((1,), (1,))) * SCORE_SCALE
                row = lax.broadcasted_iota(jnp.int32, (TILE, ROWS), 0) + a
                column = lax.broadcasted_iota(jnp.int32, (TILE, ROWS), 1)
                column = column - jnp.where(n // (2 * HEADS) < before, ROWS, 0)
                visible = column <= row
                scores = jnp.where(visible, scores, MASKED)
                old = tops[h, rows, :]
                new = jnp.maximum(old[:, :1], jnp.max(scores, 1, keepdims=True))
                weights = jnp.where(visible, jnp.exp2(scores - new), 0.0).astype(bf16)
                sums[h, rows, :] = sums[h, rows, :] * jnp.exp2(old[:, :1] - new) + dot(weights, values[at, :])
                tops[h, rows, :] = jnp.broadcast_to(new, (TILE, HD))
                return 0

            lax.fori_loop(0, (before + 1) * 2 * HEADS, step, 0)

        squares = jnp.zeros((ROWS, HD), f32)
        for h in range(HEADS):
            count = sums[h, :, HD:] + jnp.where(large, 0.0, count_ref[:, h : h + 1])
            result = (sums[h, :, :HD] + jnp.where(large, 0.0, carry_ref[:, head(h)])) / count
            result = result.astype(bf16)
            out_ref[:, head(h)] = result
            result = result.astype(f32)
            squares = squares + result * result
        square_ref[...] = dot(jnp.ones((8, HD), f32), squares, ((1,), (1,)), highest)


def attend(mine, query, own, carry, blocks, numbers_of, kept=None, kept_numbers_of=None):
    first, last = carry is None, kept is not None
    kept = kept or []
    size = 16 * ROWS if last else sum(rows for _, _, rows in blocks)
    operands = [query, own] + list(carry or []) + [block for block, _, _ in blocks + kept]
    top = (32, HD)
    scratch = [
        pltpu.VMEM((HEADS, ROWS, 2 * HD), f32),
        pltpu.VMEM((size, HD), bf16),
        pltpu.VMEM((size, 2 * HD), bf16),
    ]
    if last:
        out_shape = (
            jax.ShapeDtypeStruct((ROWS, HEADS * HD), bf16),
            jax.ShapeDtypeStruct((8, ROWS), f32),
        )
        scratch += [pltpu.VMEM(top, bf16), pltpu.VMEM((HEADS, ROWS, HD), f32)]
    else:
        out_shape = (
            jax.ShapeDtypeStruct((ROWS, HEADS * HD), f32),
            jax.ShapeDtypeStruct((ROWS, HD), f32),
            jax.ShapeDtypeStruct(top, bf16),
        )
        if first:
            out_shape = (jax.ShapeDtypeStruct((ROWS, HEADS * HD), bf16),) + out_shape
    return pl.pallas_call(
        functools.partial(
            attend_kernel,
            first,
            last,
            numbers_of,
            [block[1:] for block in blocks],
            kept_numbers_of,
            [block[1:] for block in kept],
        ),
        out_shape=out_shape,
        in_specs=[SMEM] + [VMEM] * len(operands),
        out_specs=(VMEM,) * len(out_shape),
        scratch_shapes=scratch,
        compiler_params=params(20),
        cost_estimate=cost(0.2),
        name="attend_first" if first else "attend_last" if last else "attend_middle",
    )(mine, *operands)


def carry_kernel(
    mine_ref,
    query_hbm,
    local_ref,
    grow_ref,
    kept_ref,
    handed_ref,
    chip_ref,
    core_ref,
    gain_ref,
    out_ref,
):
    mine = mine_ref[0]
    query_ref = query_hbm
    plane, side, core = mine // 4, (mine // 2) % 2, mine % 2
    kept, handed = state_of(kept_ref), state_of(handed_ref)

    def pick(one, two, wanted):
        states = [jnp.where(wanted, jnp.where(core == 0, a, b), 0.0) for a, b in zip(one[0], two[0])]
        return states, jnp.where(wanted, jnp.where(core == 0, one[1], two[1]), 0.0)

    entering = pick(handed, kept, plane >= 2)
    entering = follow(entering, pick(kept, handed, plane >= 1))
    entering = follow(entering, state_of(chip_ref, side == 1))
    entering = follow(entering, state_of(core_ref, core == 1))
    grow = grow_ref[...]
    for h in range(HEADS):
        state = entering[0][h]
        upper = state.astype(bf16)
        lower = (state - upper.astype(f32)).astype(bf16)
        both = dot(query_ref[:, head(h)], jnp.concatenate([upper, lower], 1))
        entered = both[:, :HD] + both[:, HD:]
        result = local_ref[:, head(h)] + entered * grow[:, h : h + 1]
        square = jnp.mean(result * result, -1, keepdims=True)
        out_ref[:, head(h)] = result * lax.rsqrt(square + EPS) * gain_ref[head(h)][None, :]


def finish_kernel(features, attention_ref, square_ref, other_ref, linear_ref, gain_ref, out_ref):
    factor = lax.rsqrt((square_ref[...] + other_ref[...]) / features + EPS)
    factor = dot(factor, jnp.full((8, HD), 0.125, f32), ((0,), (0,)), highest)
    for h in range(HEADS):
        part = attention_ref[:, head(h)].astype(f32) * factor * gain_ref[head(h)][None, :]
        out_ref[:, head(h)] = (part + linear_ref[:, head(h)]).astype(bf16)


def carry_in(place, lh_query, *operands):
    return pl.pallas_call(
        carry_kernel,
        out_shape=jax.ShapeDtypeStruct((ROWS, HEADS * HD), f32),
        in_specs=[SMEM, VMEM] + [VMEM] * len(operands),
        out_specs=VMEM,
        compiler_params=params(14),
        cost_estimate=cost(0.2),
        name="carry",
    )(place, lh_query, *operands)


def finish(features, *operands):
    return pl.pallas_call(
        functools.partial(finish_kernel, features),
        out_shape=jax.ShapeDtypeStruct((ROWS, HEADS * HD), bf16),
        in_specs=[VMEM] * len(operands),
        out_specs=VMEM,
        compiler_params=params(14),
        cost_estimate=cost(0.2),
        name="finish",
    )(*operands)


def body(att_query, att_key, att_value, lh_query, lh_key, lh_value, lh_step, att_gain, lh_gain):
    mine = lax.axis_index("ctx")
    place = mine.reshape(1).astype(jnp.int32)

    def move(value, pairs):
        return lax.ppermute(value, "ctx", pairs)

    every = range(16)
    sibling = [(i, i ^ 1) for i in every]
    sideways = [(i, i ^ 2) for i in every]
    onward = [(i, i + 4) for i in every if i % 2 == 0 and i < 12] + [(i, i + 8) for i in every if i % 2 == 1 and i < 8]
    wrapping = [(i, i + 12) for i in range(4)]
    last_plane = [(i, i + 4) for i in every if i % 2 == 0 and i < 12] + [(i, i + 12) for i in (1, 3)]
    plane_before = [(i, i + 8) for i in every if i % 2 == 1 and i < 8]

    def tied(*values):
        return lax.optimization_barrier(values)

    lh_query, lh_key, lh_value, far_query, att_key, att_value = [
        array
        for array in (lh_query, lh_key, lh_value, att_query, att_key, att_value)
    ]
    lh_step = lh_step.T
    att_query, lh_query, lh_key, lh_value, att_key, att_value = [
        pltpu.with_memory_space_constraint(array, pltpu.HBM)
        for array in (att_query, lh_query, lh_key, lh_value, att_key, att_value)
    ]
    own = beside(att_key, att_value)
    across = move(own, [(i, j) for i, j in sideways if i < 12 or i % 4 < 2])
    wrapped = move(own, wrapping)
    near = move(own, sibling)
    chip = stack(own, near)
    chip, lh_step = tied(chip, lh_step)
    lh_step = pltpu.with_memory_space_constraint(lh_step, pltpu.HBM)
    ring = move(chip, onward)

    local, grow, message = recur(lh_query, lh_key, lh_value, lh_step)

    def where(number, wanted):
        return jnp.where(wanted, number, NEVER)

    def parts(mine):
        return mine // 4, (mine // 2) % 2, mine % 2, mine - mine % 2

    def near_numbers(mine):
        return [where(mine - 1, mine % 2 == 1)]

    def ring_numbers(mine):
        plane, _, core, even = parts(mine)
        one, two = where(even - 4, plane >= 1), where(even - 8, plane >= 2)
        return [jnp.where(core == 0, one, two), jnp.where(core == 0, two, one)]

    def wrapped_numbers(mine):
        plane, _, _, even = parts(mine)
        return [where(even - 12, plane == 3)] * 2

    def across_numbers(mine):
        _, side, _, even = parts(mine)
        return [where(even - 2, side == 1)] * 2

    def middle_numbers(mine):
        return ring_numbers(mine) + wrapped_numbers(mine)

    def last_numbers(mine):
        plane, _, core, even = parts(mine)
        beyond, behind = where(even - 8, plane >= 2), where(even - 4, plane >= 1)
        level_numbers = [where(beyond, core == 1), where(beyond, core == 0)]
        return level_numbers + across_numbers(mine) + wrapped_numbers(mine) + [behind] * 2

    first_pieces = [(near, 0, ROWS)]
    near_query, *carry = attend(place, att_query, own, None, first_pieces, near_numbers)
    carry, message, wrapped, across = tied(carry, message, wrapped, across)
    first = move(message, sibling)
    of_chip, leveled = join_cores(place, message, first, ring)
    level = move(leveled, sideways)
    wrapped_side = move(across, wrapping)
    behind_side = move(across, [(i, i + 4) for i in range(12)])
    bundle = stack(ring, wrapped)
    bundle_near = move(bundle, sibling)
    middle_pieces = [
        (ring, 0, 2 * ROWS),
        (bundle_near, 0, 2 * ROWS),
        (wrapped, 0, ROWS),
        (bundle_near, 2 * ROWS, ROWS),
    ]
    carry = attend(place, near_query, own, carry, middle_pieces, middle_numbers)

    carry, across, wrapped_side, behind_side, level = tied(carry, across, wrapped_side, behind_side, level)
    level_near = move(level, sibling)
    rest = stack(across, wrapped_side, behind_side)
    rest_near = move(rest, sibling)
    of_plane, other_chip = join_sides(place, of_chip, level, level_near)
    state_behind = move(of_plane, last_plane)
    state_beyond = move(of_plane, plane_before)
    last_pieces = [
        (level, 0, 2 * ROWS),
        (level_near, 0, 2 * ROWS),
        (across, 0, ROWS),
        (rest_near, 0, ROWS),
        (wrapped_side, 0, ROWS),
        (rest_near, ROWS, ROWS),
        (behind_side, 0, ROWS),
        (rest_near, 2 * ROWS, ROWS),
    ]
    carry, of_plane = tied(carry, of_plane)
    attention, squares = attend(
        place,
        near_query,
        own,
        carry,
        last_pieces,
        last_numbers,
        first_pieces + middle_pieces,
        lambda mine: near_numbers(mine) + middle_numbers(mine),
    )

    def over(value, bit):
        return lax.ppermute(value, "tp", [(i, i ^ bit) for i in range(8)])

    squares, state_behind, state_beyond = tied(squares, state_behind, state_beyond)
    others = [over(squares, bit) for bit in (4, 2, 6)]
    kept = hand(place, state_behind, state_beyond)
    handed = move(kept, sibling)
    linear = carry_in(place, lh_query, local, grow, kept, handed, other_chip, first, lh_gain)
    others, linear = tied(others, linear)
    squares = squares + others[0] + others[1] + others[2]
    features = HEADS * HD * lax.axis_size("tp")
    return finish(float(features), attention, squares, over(squares, 1), linear, att_gain)


def solution(mesh):
    placed = (P("ctx", "tp"),) * 7 + (P("tp"), P("tp"))
    return jax.shard_map(body, mesh=mesh, in_specs=placed, out_specs=P("ctx", "tp"), check_vma=False)
```

```python
import functools
import math

import jax
import jax.numpy as jnp
from jax import lax
from jax.experimental import pallas as pl
from jax.experimental.pallas import tpu as pltpu
from jax.sharding import PartitionSpec as P

HD = 128
ROWS = 512
HEADS = 6
TILE = 256
EPS = 1e-06
MASKED = -1e30
LOG2E = math.log2(math.e)
SCORE_SCALE = LOG2E / math.sqrt(HD)
SAFE_EXPONENT = 100.0
STATE_ROWS = HEADS * HD + 8
NEVER = 1 << 20

VMEM = pl.BlockSpec(memory_space=pltpu.VMEM)
SMEM = pl.BlockSpec(memory_space=pltpu.SMEM)
f32 = jnp.float32
bf16 = jnp.bfloat16
highest = lax.Precision.HIGHEST


def dot(a, b, contract=((1,), (0,)), precision=None):
    return lax.dot_general(a, b, (contract, ((), ())), precision=precision, preferred_element_type=f32)


def params(megabytes):
    return pltpu.CompilerParams(vmem_limit_bytes=megabytes << 20)


def cost(us):
    return pl.CostEstimate(flops=int(us * 1e9), bytes_accessed=int(us * 1e6), transcendentals=int(us * 1e6))


def head(h):
    return slice(h * HD, (h + 1) * HD)


def recur_kernel(
    q_hbm, k_hbm, v_hbm, step_ref, local_ref, grow_ref, message_ref, padded
):
    k_ref, q_ref, v_ref = k_hbm, q_hbm, v_hbm
    padded[...] = jnp.full((8, ROWS), 0.5, f32)
    padded[:HEADS, :] = step_ref[...]
    step = padded[...]
    rate = step / (1.0 + step)
    total = -jnp.log(1.0 + step) * LOG2E
    place = lax.broadcasted_iota(jnp.int32, (8, ROWS), 1)
    reach = 1
    while reach < ROWS:
        total = total + jnp.where(place >= reach, pltpu.roll(total, reach, 1), 0.0)
        reach *= 2
    source = jnp.log(rate) * LOG2E - total
    end = total[:, ROWS - 1 : ROWS]
    tail = jnp.exp2(end + source)
    rows = jnp.concatenate([total, tail, jnp.zeros((HD - 16, ROWS), f32)], 0)
    columns = jnp.transpose(rows)
    grow_ref[...] = jnp.exp2(columns)
    message_ref[HEADS * HD :, :] = jnp.broadcast_to(end, (8, HD))
    at_row = lax.broadcasted_iota(jnp.int32, (TILE, TILE), 0)
    at_column = lax.broadcasted_iota(jnp.int32, (TILE, TILE), 1)
    seen = at_column <= at_row
    for h in range(HEADS):
        keys = k_ref[:, head(h)].astype(f32)
        keys = keys * lax.rsqrt(jnp.sum(keys * keys, -1, keepdims=True) + EPS)
        unit = keys.astype(bf16)
        values = v_ref[:, head(h)]
        for a in range(0, ROWS, TILE):
            result = None
            for b in range(0, a + TILE, TILE):
                scores = dot(q_ref[a : a + TILE, head(h)], unit[b : b + TILE], ((1,), (1,)))
                decay = jnp.exp2(columns[a : a + TILE, h : h + 1] + source[h : h + 1, b : b + TILE])
                weights = scores * decay
                if a == b:
                    weights = jnp.where(seen, weights, 0.0)
                part = dot(weights.astype(bf16), values[b : b + TILE])
                result = part if result is None else result + part
            local_ref[a : a + TILE, head(h)] = result
        tailed = (values.astype(f32) * columns[:, 8 + h : 9 + h]).astype(bf16)
        message_ref[head(h), :] = dot(unit, tailed, ((0,), (0,)))


def recur(lh_query, lh_key, lh_value, lh_step):
    return pl.pallas_call(
        recur_kernel,
        out_shape=(
            jax.ShapeDtypeStruct((ROWS, HEADS * HD), f32),
            jax.ShapeDtypeStruct((ROWS, HD), f32),
            jax.ShapeDtypeStruct((STATE_ROWS, HD), f32),
        ),
        in_specs=[VMEM] * 4,
        out_specs=(VMEM,) * 3,
        scratch_shapes=[pltpu.VMEM((8, ROWS), f32)]
,
        compiler_params=params(16),
        cost_estimate=cost(0.2),
        name="recur",
    )(lh_query, lh_key, lh_value, lh_step)


def beside_kernel(key_ref, value_ref, out_ref):
    out_ref[:, :HD] = key_ref[...]
    out_ref[:, HD:] = value_ref[...]


def beside(key, value):
    return pl.pallas_call(
        beside_kernel,
        out_shape=jax.ShapeDtypeStruct((ROWS, 2 * HD), bf16),
        in_specs=[VMEM, VMEM],
        out_specs=VMEM,
        compiler_params=params(14),
        name="beside",
    )(key, value)


def stack_kernel(*refs):
    *parts, out_ref = refs
    at = 0
    for part in parts:
        out_ref[at : at + part.shape[0], :] = part[...]
        at += part.shape[0]


def stack(*parts):
    return pl.pallas_call(
        stack_kernel,
        out_shape=jax.ShapeDtypeStruct((sum(part.shape[0] for part in parts), 2 * HD), bf16),
        in_specs=[VMEM] * len(parts),
        out_specs=VMEM,
        compiler_params=params(14),
        name="stack",
    )(*parts)


def follow(early, late):
    logs = early[1] + late[1]
    states = [jnp.exp2(late[1][h : h + 1, :]) * early[0][h] + late[0][h] for h in range(HEADS)]
    return states, logs


def state_of(ref, wanted=None):
    states = [ref[head(h), :] for h in range(HEADS)]
    logs = ref[HEADS * HD :, :]
    if wanted is None:
        return states, logs
    return [jnp.where(wanted, state, 0.0) for state in states], jnp.where(wanted, logs, 0.0)


def put_state(ref, value):
    for h in range(HEADS):
        ref[head(h), :] = value[0][h]
    ref[HEADS * HD :, :] = value[1]


def select(wanted, one, two):
    return [jnp.where(wanted, a, b) for a, b in zip(one[0], two[0])], jnp.where(wanted, one[1], two[1])


def follow_in_order(own_first, own, other):
    return follow(select(own_first, own, other), select(own_first, other, own))


def split(value):
    upper = value.astype(bf16)
    return jnp.concatenate([upper, (value - upper.astype(f32)).astype(bf16)], 1)


def merge(both):
    return both[:, :HD].astype(f32) + both[:, HD:].astype(f32)


def join_cores_kernel(mine_ref, own_ref, other_ref, blocks_ref, out_ref, message_ref):
    even = mine_ref[0] % 2 == 0
    joined = follow_in_order(even, state_of(own_ref), state_of(other_ref))
    put_state(out_ref, joined)
    message_ref[...] = blocks_ref[...]

    @pl.when(even)
    def _():
        for h in range(HEADS):
            message_ref[head(h), :] = split(joined[0][h])
        logs = jnp.concatenate([joined[1], jnp.zeros((8, HD), f32)], 0)
        message_ref[HEADS * HD : HEADS * HD + 16, :] = split(logs)


def join_cores(mine, own, other, blocks):
    return pl.pallas_call(
        join_cores_kernel,
        out_shape=(
            jax.ShapeDtypeStruct((STATE_ROWS, HD), f32),
            jax.ShapeDtypeStruct((2 * ROWS, 2 * HD), bf16),
        ),
        in_specs=[SMEM] + [VMEM] * 3,
        out_specs=(VMEM,) * 2,
        compiler_params=params(14),
        cost_estimate=cost(0.2),
        name="join_cores",
    )(mine, own, other, blocks)


def join_sides_kernel(mine_ref, own_ref, level_ref, level_near_ref, out_ref, other_ref):
    mine = mine_ref[0]
    even = mine % 2 == 0

    def brought(ref):
        logs = merge(ref[HEADS * HD : HEADS * HD + 16, :])[:8, :]
        return [merge(ref[head(h), :]) for h in range(HEADS)], logs

    other = select(even, brought(level_ref), brought(level_near_ref))
    put_state(other_ref, other)
    put_state(out_ref, follow_in_order((mine // 2) % 2 == 0, state_of(own_ref), other))


def join_sides(mine, own, level, level_near):
    return pl.pallas_call(
        join_sides_kernel,
        out_shape=(jax.ShapeDtypeStruct((STATE_ROWS, HD), f32),) * 2,
        in_specs=[SMEM] + [VMEM] * 3,
        out_specs=(VMEM,) * 2,
        compiler_params=params(14),
        cost_estimate=cost(0.2),
        name="join_sides",
    )(mine, own, level, level_near)


def hand_kernel(mine_ref, behind_ref, beyond_ref, out_ref):
    plane, core = mine_ref[0] // 4, mine_ref[0] % 2
    behind = state_of(behind_ref, (plane == 3) | (core == 0))
    beyond = state_of(beyond_ref, (plane >= 2) & (core == 1))
    put_state(out_ref, follow(behind, beyond))


def hand(mine, behind, beyond):
    return pl.pallas_call(
        hand_kernel,
        out_shape=jax.ShapeDtypeStruct((STATE_ROWS, HD), f32),
        in_specs=[SMEM, VMEM, VMEM],
        out_specs=VMEM,
        compiler_params=params(14),
        cost_estimate=cost(0.2),
        name="hand",
    )(mine, behind, beyond)


def attend_kernel(first, last, numbers_of, pieces, kept_numbers_of, kept, mine_ref, query_ref, own_ref, *refs):
    mine = mine_ref[0]
    refs = list(refs)

    def take(count):
        return [refs.pop(0) for _ in range(count)]

    if not first:
        carry_ref, count_ref, top_in_ref = take(3)
    block_refs = [(ref, *piece) for ref, piece in zip(take(len(pieces)), pieces)]
    kept_refs = [(ref, *piece) for ref, piece in zip(take(len(kept)), kept)]
    if last:
        out_ref, square_ref, sums, keys, values, top_ref, tops = refs
    else:
        if first:
            (passed_ref,) = take(1)
            passed_ref[...] = query_ref[...]
        numerator_ref, counted_ref, top_ref, sums, keys, values = refs

    def highest_of(part):
        return jnp.max(jnp.abs(part).reshape(-1, 16, HD), 0)

    def fill(blocks, numbers):
        filled = jnp.int32(0)
        for (block, start, rows), number in zip(blocks, numbers):
            takes = number < mine
            place = filled

            @pl.when(takes)
            def _():
                at = pl.ds(pl.multiple_of(place * ROWS, ROWS), rows)
                block_keys = block[start : start + rows, :HD]
                keys[at, :] = block_keys
                values[at, :HD] = block[start : start + rows, HD:]
                top_ref[16:32, :] = jnp.maximum(top_ref[16:32, :], highest_of(block_keys))

            filled = filled + jnp.where(takes, rows // ROWS, 0)
        return filled

    if first:
        top_ref[16:32, :] = highest_of(own_ref[:, :HD])
        longest = jnp.zeros((ROWS, HD), f32)
        ones = jnp.ones((HD, HD), bf16)
        for h in range(HEADS):
            query = query_ref[:, head(h)].astype(f32)
            longest = jnp.maximum(longest, dot((query * query).astype(bf16), ones))
        top_ref[0:16, :] = jnp.max(longest.reshape(-1, 16, HD), 0).astype(bf16)
    else:
        top_ref[...] = top_in_ref[...]
    values[:, HD:] = jnp.ones((values.shape[0], HD), bf16)
    filled = fill(block_refs, numbers_of(mine))
    sums[...] = jnp.zeros_like(sums)

    def visit(start, count):
        at = pl.ds(pl.multiple_of(start, ROWS), count)
        block_keys = keys[at, :]
        block_values = values[at, :]
        for h in range(HEADS):
            for a in range(0, ROWS, TILE):
                scores = dot(query_ref[a : a + TILE, head(h)], block_keys, ((1,), (1,)))
                weights = jnp.exp2(scores * SCORE_SCALE).astype(bf16)
                sums[h, a : a + TILE, :] += dot(weights, block_values)

    def pair(n, _):
        visit(n * 2 * ROWS, 2 * ROWS)
        return 0

    if not first:
        lax.fori_loop(0, filled // 2, pair, 0)

    if first:

        @pl.when(filled > 0)
        def _():
            visit(0, ROWS)

        at_row = lax.broadcasted_iota(jnp.int32, (TILE, TILE), 0)
        at_column = lax.broadcasted_iota(jnp.int32, (TILE, TILE), 1)
        seen = at_column <= at_row
        values[:ROWS, :HD] = own_ref[:, HD:]
        for h in range(HEADS):
            for a in range(0, ROWS, TILE):
                for b in range(0, a + TILE, TILE):
                    scores = dot(query_ref[a : a + TILE, head(h)], own_ref[b : b + TILE, :HD], ((1,), (1,)))
                    weights = jnp.exp2(scores * SCORE_SCALE)
                    if a == b:
                        weights = jnp.where(seen, weights, 0.0)
                    sums[h, a : a + TILE, :] += dot(weights.astype(bf16), values[b : b + TILE, :])
            numerator_ref[:, head(h)] = sums[h, :, :HD]
            counted_ref[:, h : h + 1] = sums[h, :, HD : HD + 1]
    elif not last:
        for h in range(HEADS):
            numerator_ref[:, head(h)] = sums[h, :, :HD] + carry_ref[:, head(h)]
            counted_ref[:, h : h + 1] = sums[h, :, HD : HD + 1] + count_ref[:, h : h + 1]
    else:
        key_top = jnp.max(top_ref[16:32, :].astype(f32), 0, keepdims=True)
        bound = jnp.max(top_ref[0:16, :].astype(f32)) * jnp.sum(key_top * key_top) * SCORE_SCALE**2
        large = bound * 1.05 > SAFE_EXPONENT * SAFE_EXPONENT

        @pl.when(large)
        def _():
            before = fill(kept_refs + block_refs, kept_numbers_of(mine) + numbers_of(mine))
            at = pl.ds(pl.multiple_of(before * ROWS, ROWS), ROWS)
            keys[at, :] = own_ref[:, :HD]
            values[at, :HD] = own_ref[:, HD:]
            sums[...] = jnp.zeros_like(sums)
            tops[...] = jnp.full_like(tops, MASKED)

            def step(n, _):
                at = pl.ds(pl.multiple_of((n // (2 * HEADS)) * ROWS, ROWS), ROWS)
                h = (n % (2 * HEADS)) // 2
                a = (n % 2) * TILE
                rows = pl.ds(pl.multiple_of(a, TILE), TILE)
                query = query_ref[rows, pl.ds(pl.multiple_of(h * HD, HD), HD)]
                scores = dot(query, keys[at, :], ((1,), (1,))) * SCORE_SCALE
                row = lax.broadcasted_iota(jnp.int32, (TILE, ROWS), 0) + a
                column = lax.broadcasted_iota(jnp.int32, (TILE, ROWS), 1)
                column = column - jnp.where(n // (2 * HEADS) < before, ROWS, 0)
                visible = column <= row
                scores = jnp.where(visible, scores, MASKED)
                old = tops[h, rows, :]
                new = jnp.maximum(old[:, :1], jnp.max(scores, 1, keepdims=True))
                weights = jnp.where(visible, jnp.exp2(scores - new), 0.0).astype(bf16)
                sums[h, rows, :] = sums[h, rows, :] * jnp.exp2(old[:, :1] - new) + dot(weights, values[at, :])
                tops[h, rows, :] = jnp.broadcast_to(new, (TILE, HD))
                return 0

            lax.fori_loop(0, (before + 1) * 2 * HEADS, step, 0)

        squares = jnp.zeros((ROWS, HD), f32)
        for h in range(HEADS):
            count = sums[h, :, HD:] + jnp.where(large, 0.0, count_ref[:, h : h + 1])
            result = (sums[h, :, :HD] + jnp.where(large, 0.0, carry_ref[:, head(h)])) / count
            result = result.astype(bf16)
            out_ref[:, head(h)] = result
            result = result.astype(f32)
            squares = squares + result * result
        square_ref[...] = dot(jnp.ones((8, HD), f32), squares, ((1,), (1,)), highest)[:1, :]


def attend(mine, query, own, carry, blocks, numbers_of, kept=None, kept_numbers_of=None):
    first, last = carry is None, kept is not None
    kept = kept or []
    size = 16 * ROWS if last else sum(rows for _, _, rows in blocks)
    operands = [query, own] + list(carry or []) + [block for block, _, _ in blocks + kept]
    top = (32, HD)
    scratch = [
        pltpu.VMEM((HEADS, ROWS, 2 * HD), f32),
        pltpu.VMEM((size, HD), bf16),
        pltpu.VMEM((size, 2 * HD), bf16),
    ]
    if last:
        out_shape = (
            jax.ShapeDtypeStruct((ROWS, HEADS * HD), bf16),
            jax.ShapeDtypeStruct((1, ROWS), f32),
        )
        scratch += [pltpu.VMEM(top, bf16), pltpu.VMEM((HEADS, ROWS, HD), f32)]
    else:
        out_shape = (
            jax.ShapeDtypeStruct((ROWS, HEADS * HD), f32),
            jax.ShapeDtypeStruct((ROWS, HD), f32),
            jax.ShapeDtypeStruct(top, bf16),
        )
        if first:
            out_shape = (jax.ShapeDtypeStruct((ROWS, HEADS * HD), bf16),) + out_shape
    return pl.pallas_call(
        functools.partial(
            attend_kernel,
            first,
            last,
            numbers_of,
            [block[1:] for block in blocks],
            kept_numbers_of,
            [block[1:] for block in kept],
        ),
        out_shape=out_shape,
        in_specs=[SMEM] + [VMEM] * len(operands),
        out_specs=(VMEM,) * len(out_shape),
        scratch_shapes=scratch,
        compiler_params=params(20),
        cost_estimate=cost(0.2),
        name="attend_first" if first else "attend_last" if last else "attend_middle",
    )(mine, *operands)


def carry_kernel(
    mine_ref,
    query_hbm,
    local_ref,
    grow_ref,
    kept_ref,
    handed_ref,
    chip_ref,
    core_ref,
    gain_ref,
    out_ref,
):
    mine = mine_ref[0]
    query_ref = query_hbm
    plane, side, core = mine // 4, (mine // 2) % 2, mine % 2
    kept, handed = state_of(kept_ref), state_of(handed_ref)

    def pick(one, two, wanted):
        states = [jnp.where(wanted, jnp.where(core == 0, a, b), 0.0) for a, b in zip(one[0], two[0])]
        return states, jnp.where(wanted, jnp.where(core == 0, one[1], two[1]), 0.0)

    entering = pick(handed, kept, plane >= 2)
    entering = follow(entering, pick(kept, handed, plane >= 1))
    entering = follow(entering, state_of(chip_ref, side == 1))
    entering = follow(entering, state_of(core_ref, core == 1))
    grow = grow_ref[...]
    for h in range(HEADS):
        state = entering[0][h]
        upper = state.astype(bf16)
        lower = (state - upper.astype(f32)).astype(bf16)
        both = dot(query_ref[:, head(h)], jnp.concatenate([upper, lower], 1))
        entered = both[:, :HD] + both[:, HD:]
        result = local_ref[:, head(h)] + entered * grow[:, h : h + 1]
        square = jnp.mean(result * result, -1, keepdims=True)
        out_ref[:, head(h)] = result * lax.rsqrt(square + EPS) * gain_ref[head(h)][None, :]


def finish_kernel(features, attention_ref, square_ref, other_ref, linear_ref, gain_ref, out_ref):
    factor = lax.rsqrt((square_ref[...] + other_ref[...]) / features + EPS)
    factor = jnp.broadcast_to(factor, (8, ROWS))
    factor = dot(factor, jnp.full((8, HD), 0.125, f32), ((0,), (0,)), highest)
    for h in range(HEADS):
        part = attention_ref[:, head(h)].astype(f32) * factor * gain_ref[head(h)][None, :]
        out_ref[:, head(h)] = (part + linear_ref[:, head(h)]).astype(bf16)


def carry_in(place, lh_query, *operands):
    return pl.pallas_call(
        carry_kernel,
        out_shape=jax.ShapeDtypeStruct((ROWS, HEADS * HD), f32),
        in_specs=[SMEM, VMEM] + [VMEM] * len(operands),
        out_specs=VMEM,
        compiler_params=params(14),
        cost_estimate=cost(0.2),
        name="carry",
    )(place, lh_query, *operands)


def finish(features, *operands):
    return pl.pallas_call(
        functools.partial(finish_kernel, features),
        out_shape=jax.ShapeDtypeStruct((ROWS, HEADS * HD), bf16),
        in_specs=[VMEM] * len(operands),
        out_specs=VMEM,
        compiler_params=params(14),
        cost_estimate=cost(0.2),
        name="finish",
    )(*operands)


def body(att_query, att_key, att_value, lh_query, lh_key, lh_value, lh_step, att_gain, lh_gain):
    mine = lax.axis_index("ctx")
    place = mine.reshape(1).astype(jnp.int32)

    def move(value, pairs):
        return lax.ppermute(value, "ctx", pairs)

    every = range(16)
    sibling = [(i, i ^ 1) for i in every]
    sideways = [(i, i ^ 2) for i in every]
    onward = [(i, i + 4) for i in every if i % 2 == 0 and i < 12] + [(i, i + 8) for i in every if i % 2 == 1 and i < 8]
    wrapping = [(i, i + 12) for i in range(4)]
    last_plane = [(i, i + 4) for i in every if i % 2 == 0 and i < 12] + [(i, i + 12) for i in (1, 3)]
    plane_before = [(i, i + 8) for i in every if i % 2 == 1 and i < 8]

    def tied(*values):
        return lax.optimization_barrier(values)

    lh_query, lh_key, lh_value, far_query, att_key, att_value = [
        array
        for array in (lh_query, lh_key, lh_value, att_query, att_key, att_value)
    ]
    lh_step = lh_step.T
    att_query, lh_query, lh_key, lh_value, att_key, att_value = [
        pltpu.with_memory_space_constraint(array, pltpu.HBM)
        for array in (att_query, lh_query, lh_key, lh_value, att_key, att_value)
    ]
    own = beside(att_key, att_value)
    across = move(own, [(i, j) for i, j in sideways if i < 12 or i % 4 < 2])
    wrapped = move(own, wrapping)
    near = move(own, sibling)
    chip = stack(own, near)
    chip, lh_step = tied(chip, lh_step)
    lh_step = pltpu.with_memory_space_constraint(lh_step, pltpu.HBM)
    ring = move(chip, onward)

    local, grow, message = recur(lh_query, lh_key, lh_value, lh_step)

    def where(number, wanted):
        return jnp.where(wanted, number, NEVER)

    def parts(mine):
        return mine // 4, (mine // 2) % 2, mine % 2, mine - mine % 2

    def near_numbers(mine):
        return [where(mine - 1, mine % 2 == 1)]

    def ring_numbers(mine):
        plane, _, core, even = parts(mine)
        one, two = where(even - 4, plane >= 1), where(even - 8, plane >= 2)
        return [jnp.where(core == 0, one, two), jnp.where(core == 0, two, one)]

    def wrapped_numbers(mine):
        plane, _, _, even = parts(mine)
        return [where(even - 12, plane == 3)] * 2

    def across_numbers(mine):
        _, side, _, even = parts(mine)
        return [where(even - 2, side == 1)] * 2

    def middle_numbers(mine):
        return ring_numbers(mine) + wrapped_numbers(mine)

    def last_numbers(mine):
        plane, _, core, even = parts(mine)
        beyond, behind = where(even - 8, plane >= 2), where(even - 4, plane >= 1)
        level_numbers = [where(beyond, core == 1), where(beyond, core == 0)]
        return level_numbers + across_numbers(mine) + wrapped_numbers(mine) + [behind] * 2

    first_pieces = [(near, 0, ROWS)]
    near_query, *carry = attend(place, att_query, own, None, first_pieces, near_numbers)
    carry, message, wrapped, across = tied(carry, message, wrapped, across)
    first = move(message, sibling)
    of_chip, leveled = join_cores(place, message, first, ring)
    level = move(leveled, sideways)
    wrapped_side = move(across, wrapping)
    behind_side = move(across, [(i, i + 4) for i in range(12)])
    bundle = stack(ring, wrapped)
    bundle_near = move(bundle, sibling)
    middle_pieces = [
        (ring, 0, 2 * ROWS),
        (bundle_near, 0, 2 * ROWS),
        (wrapped, 0, ROWS),
        (bundle_near, 2 * ROWS, ROWS),
    ]
    carry = attend(place, near_query, own, carry, middle_pieces, middle_numbers)

    carry, across, wrapped_side, behind_side, level = tied(carry, across, wrapped_side, behind_side, level)
    level_near = move(level, sibling)
    rest = stack(across, wrapped_side, behind_side)
    rest_near = move(rest, sibling)
    of_plane, other_chip = join_sides(place, of_chip, level, level_near)
    state_behind = move(of_plane, last_plane)
    state_beyond = move(of_plane, plane_before)
    last_pieces = [
        (level, 0, 2 * ROWS),
        (level_near, 0, 2 * ROWS),
        (across, 0, ROWS),
        (rest_near, 0, ROWS),
        (wrapped_side, 0, ROWS),
        (rest_near, ROWS, ROWS),
        (behind_side, 0, ROWS),
        (rest_near, 2 * ROWS, ROWS),
    ]
    carry, of_plane = tied(carry, of_plane)
    attention, squares = attend(
        place,
        near_query,
        own,
        carry,
        last_pieces,
        last_numbers,
        first_pieces + middle_pieces,
        lambda mine: near_numbers(mine) + middle_numbers(mine),
    )

    def over(value, bit):
        return lax.ppermute(value, "tp", [(i, i ^ bit) for i in range(8)])

    squares, state_behind, state_beyond = tied(squares, state_behind, state_beyond)
    others = [over(squares, bit) for bit in (4, 2, 6)]
    kept = hand(place, state_behind, state_beyond)
    handed = move(kept, sibling)
    linear = carry_in(place, lh_query, local, grow, kept, handed, other_chip, first, lh_gain)
    others, linear = tied(others, linear)
    squares = squares + others[0] + others[1] + others[2]
    features = HEADS * HD * lax.axis_size("tp")
    return finish(float(features), attention, squares, over(squares, 1), linear, att_gain)


def solution(mesh):
    placed = (P("ctx", "tp"),) * 7 + (P("tp"), P("tp"))
    return jax.shard_map(body, mesh=mesh, in_specs=placed, out_specs=P("ctx", "tp"), check_vma=False)
```
